32 devices in a mesh: section: 2 (over core), dp: 16 (over z, y, x).
Axes of the slice: x: 2, y: 2, z: 4, core: 2. Of those that a mesh axis runs over, the one named last changes fastest.
Arguments:
- input_big: bfloat16 [2, 32, 197, 768], P(None, 'dp'), may hold values from -6 to 6
- input_small: bfloat16 [2, 64, 37, 768], P(None, 'dp'), may hold values from -6 to 6
- small_counts: int32 [2, 16], P(None, 'dp'), may hold values from 1 to 4, as said below
- cotangent_big: bfloat16 [2, 32, 197, 768], P(None, 'dp'), may hold values from -6 to 6
- cotangent_small: bfloat16 [2, 64, 37, 768], P(None, 'dp'), may hold values from -6 to 6
- norm1_gain: float32 [2, 768], P('section'), may hold values from 0.5 to 1.5
- norm1_bias: float32 [2, 768], P('section'), may hold values from -1.75 to 1.75
- qkv_weight: bfloat16 [2, 768, 2304], P('section'), may hold values from -0.21875 to 0.21875
- query_bias: float32 [2, 768], P('section'), may hold values from -1.75 to 1.75
- value_bias: float32 [2, 768], P('section'), may hold values from -1.75 to 1.75
- table_big: float32 [2, 732, 12], P('section'), may hold values from -3 to 3
- table_small: float32 [2, 124, 12], P('section'), may hold values from -3 to 3
- proj_weight: bfloat16 [2, 768, 768], P('section'), may hold values from -1.25 to 1.25
- proj_bias: float32 [2, 768], P('section'), may hold values from -1.75 to 1.75
- attn_scale: float32 [2, 768], P('section'), may hold values from 0.5 to 1.5
- norm2_gain: float32 [2, 768], P('section'), may hold values from 0.5 to 1.5
- norm2_bias: float32 [2, 768], P('section'), may hold values from -1.75 to 1.75
- up_weight: bfloat16 [2, 768, 3072], P('section'), may hold values from -0.21875 to 0.21875
- up_bias: float32 [2, 3072], P('section'), may hold values from -1.75 to 1.75
- down_weight: bfloat16 [2, 3072, 768], P('section'), may hold values from -0.109375 to 0.109375
- down_bias: float32 [2, 768], P('section'), may hold values from -1.75 to 1.75
- mlp_scale: float32 [2, 768], P('section'), may hold values from 0.5 to 1.5
Outputs:
- layer_big: bfloat16 [2, 2, 32, 197, 768], P('section', None, 'dp')
- layer_small: bfloat16 [2, 2, 64, 37, 768], P('section', None, 'dp')
- input_grad_big: bfloat16 [2, 2, 32, 197, 768], P('section', None, 'dp')
- input_grad_small: bfloat16 [2, 2, 64, 37, 768], P('section', None, 'dp')
- grad_norm1_gain: float32 [2, 768], P('section', 'dp')
- grad_norm1_bias: float32 [2, 768], P('section', 'dp')
- grad_qkv_weight: float32 [2, 768, 2304], P('section', 'dp')
- grad_query_bias: float32 [2, 768], P('section', 'dp')
- grad_value_bias: float32 [2, 768], P('section', 'dp')
- grad_table_big: float32 [2, 732, 12], P('section')
- grad_table_small: float32 [2, 124, 12], P('section')
- grad_proj_weight: float32 [2, 768, 768], P('section', 'dp')
- grad_proj_bias: float32 [2, 768], P('section', 'dp')
- grad_attn_scale: float32 [2, 768], P('section', 'dp')
- grad_norm2_gain: float32 [2, 768], P('section', 'dp')
- grad_norm2_bias: float32 [2, 768], P('section', 'dp')
- grad_up_weight: float32 [2, 768, 3072], P('section', 'dp')
- grad_up_bias: float32 [2, 3072], P('section', 'dp')
- grad_down_weight: float32 [2, 3072, 768], P('section', 'dp')
- grad_down_bias: float32 [2, 768], P('section', 'dp')
- grad_mlp_scale: float32 [2, 768], P('section', 'dp')
The draws below stay inside these ranges and needn't reach their ends.
Inputs may be any that keep to these rules, and one draw needn't show every extreme that they name: `small_counts`: each image's number of live small crop slots (the first ones of its 4); some image has 4 and some has 1.
All inputs are finite; a program needn't handle non-finite values.
Results may differ from the reference program's by a relative error of at most 0.018.
Values may be sent and summed in bfloat16 or wider, within the bound.
No kernel may reach another device: no remote copies, remote signals or barrier semaphores. Data moves between devices by JAX's collectives and lax.ppermute only.
A program may use at most 320 MiB of HBM per device.

```python
import jax
import jax.numpy as jnp
from jax import lax

D = 768
HEADS = 12
FF = 3072
GRID_BIG = 14
GRID_SMALL = 6
SC_CAP = 4
MB = 2
LEN_BIG = 197
LEN_SMALL = 37
REL_BIG = 732
REL_SMALL = 124
IMAGES = 16
BIGS = 32
SMALLS = 64
N_SECTION = 2


def draw_small_counts(key, part):
    key = jax.random.fold_in(key, 7)
    first_key, second_key = jax.random.split(key)
    entries = MB * IMAGES
    counts = jax.random.randint(first_key, (entries,), 1, SC_CAP + 1)
    place = jax.random.randint(second_key, (), 0, entries)
    counts = counts.at[place].set(SC_CAP)
    counts = counts.at[(place + 1) % entries].set(1)
    return counts.reshape(MB, IMAGES).astype(jnp.int32)


def block_scale(rng, dims, pieces, low, high):
    def one(position, blocks):
        draws = jax.random.uniform(jax.random.fold_in(jax.random.fold_in(rng, 6), position), (blocks,), jnp.float32, low / len(pieces), high / len(pieces))
        return jnp.repeat(jnp.exp(draws), dims[position] // blocks).reshape((-1,) + (1,) * (len(dims) - position - 1))

    level = one(*pieces[0])
    for cut in pieces[1:]:
        level = level * one(*cut)
    return level


def centred(own_key, dims, scale, most, pieces=(), kind=jnp.bfloat16):
    values = scale * jax.random.normal(own_key, dims, jnp.float32)
    if pieces:
        values = values * block_scale(own_key, dims, pieces, -0.22, 0.18)
    return jnp.clip(values, -most, most).astype(kind)


def setup_inputs(seed: int = 0) -> dict:
    splits = jax.random.split(jax.random.key(seed), 23)
    input_big = centred(splits[0], (MB, BIGS, LEN_BIG, D), 1.0, 6.0, ((1, 16),))
    input_small = centred(splits[1], (MB, SMALLS, LEN_SMALL, D), 1.0, 6.0, ((1, 16),))
    small_counts = draw_small_counts(jax.random.fold_in(splits[22], 71), 0)
    cotangent_big = centred(splits[3], (MB, BIGS, LEN_BIG, D), 1.0, 6.0, ((1, 16),))
    cotangent_small = centred(splits[4], (MB, SMALLS, LEN_SMALL, D), 1.0, 6.0, ((1, 16),))
    norm1_gain = jnp.clip(1.0 + 0.1 * jax.random.normal(splits[5], (N_SECTION, D), jnp.float32), 0.5, 1.5)
    norm1_bias = centred(splits[6], (N_SECTION, D), 0.3, 1.75, ((0, 2),), jnp.float32)
    qkv_weight = centred(splits[7], (N_SECTION, D, 3 * D), D ** -0.5, 0.21875, ((0, 2),))
    query_bias = centred(splits[8], (N_SECTION, D), 0.3, 1.75, ((0, 2),), jnp.float32)
    value_bias = centred(splits[9], (N_SECTION, D), 0.3, 1.75, ((0, 2),), jnp.float32)
    table_big = centred(splits[10], (N_SECTION, REL_BIG, HEADS), 0.5, 3.0, ((0, 2),), jnp.float32)
    table_small = centred(splits[11], (N_SECTION, REL_SMALL, HEADS), 0.5, 3.0, ((0, 2),), jnp.float32)
    proj_weight = centred(splits[12], (N_SECTION, D, D), (D // 32) ** -0.5, 1.25, ((0, 2),))
    proj_bias = centred(splits[13], (N_SECTION, D), 0.3, 1.75, ((0, 2),), jnp.float32)
    attn_scale = jnp.clip(0.5 + 1.0 * jax.random.uniform(splits[14], (N_SECTION, D), jnp.float32) ** block_scale(splits[14], (N_SECTION, D), ((0, 2),), -0.2, 0.2), 0.5, 1.5)
    norm2_gain = jnp.clip(1.0 + 0.1 * jax.random.normal(splits[15], (N_SECTION, D), jnp.float32), 0.5, 1.5)
    norm2_bias = centred(splits[16], (N_SECTION, D), 0.3, 1.75, ((0, 2),), jnp.float32)
    up_weight = centred(splits[17], (N_SECTION, D, FF), D ** -0.5, 0.21875, ((0, 2),))
    up_bias = centred(splits[18], (N_SECTION, FF), 0.3, 1.75, ((0, 2),), jnp.float32)
    down_weight = centred(splits[19], (N_SECTION, FF, D), FF ** -0.5, 0.109375, ((0, 2),))
    down_bias = centred(splits[20], (N_SECTION, D), 0.3, 1.75, ((0, 2),), jnp.float32)
    mlp_scale = jnp.clip(0.5 + 1.0 * jax.random.uniform(splits[21], (N_SECTION, D), jnp.float32) ** block_scale(splits[21], (N_SECTION, D), ((0, 2),), -0.2, 0.2), 0.5, 1.5)
    return {"input_big": input_big, "input_small": input_small, "small_counts": small_counts, "cotangent_big": cotangent_big, "cotangent_small": cotangent_small, "norm1_gain": norm1_gain, "norm1_bias": norm1_bias, "qkv_weight": qkv_weight, "query_bias": query_bias, "value_bias": value_bias, "table_big": table_big, "table_small": table_small, "proj_weight": proj_weight, "proj_bias": proj_bias, "attn_scale": attn_scale, "norm2_gain": norm2_gain, "norm2_bias": norm2_bias, "up_weight": up_weight, "up_bias": up_bias, "down_weight": down_weight, "down_bias": down_bias, "mlp_scale": mlp_scale}


@jax.custom_vjp
def low(v):
    return lax.optimization_barrier(v.astype(jnp.bfloat16)).astype(jnp.float32)

@jax.custom_vjp
def low_back(v):
    return v

def low_keep(v):
    return (low(v), None)

def low_pass(kept, grad):
    return (grad,)

def back_keep(v):
    return (v, None)

def back_low(kept, grad):
    return (low(grad),)
low.defvjp(low_keep, low_pass)
low_back.defvjp(back_keep, back_low)
highest = lax.Precision.HIGHEST

def mult(left, right):
    return jnp.dot(left, right, precision=highest, preferred_element_type=jnp.float32)

def layer_norm(values, gain, shift):
    centre = values - lax.optimization_barrier(jnp.mean(values, axis=-1, keepdims=True))
    spread = lax.optimization_barrier(jnp.mean(centre * centre, axis=-1, keepdims=True))
    return centre * lax.rsqrt(spread + 1e-06) * gain + shift

def rel_index(grid):
    count = grid * grid
    side = 2 * grid - 1
    places = jnp.arange(count, dtype=jnp.int32)
    across = places // grid
    along = places % grid
    inner = (across[:, None] - across[None, :] + grid - 1) * side + (along[:, None] - along[None, :] + grid - 1)
    entries = side * side + 3
    table = jnp.zeros((count + 1, count + 1), jnp.int32)
    table = table.at[1:, 1:].set(inner.astype(jnp.int32))
    table = table.at[0, :].set(entries - 3)
    table = table.at[:, 0].set(entries - 2)
    table = table.at[0, 0].set(entries - 1)
    return table

def attend(projected, table, index):
    crops, length, triple = projected.shape
    width = triple // 3
    head = width // HEADS
    parts = projected.reshape(crops, length, 3, HEADS, head)
    bias = jnp.transpose(jnp.take(table, index, axis=0), (2, 0, 1))
    scores = jnp.einsum('clhd,cmhd->chlm', parts[:, :, 0], parts[:, :, 1], precision=highest) * head ** (-0.5) + bias[None]
    probs = jax.nn.softmax(low_back(scores), axis=-1)
    result = jnp.einsum('chlm,cmhd->clhd', low(probs), parts[:, :, 2], precision=highest)
    return result.reshape(crops * length, width)

def layer(rows, keep, weights, layout):
    norm1_gain, norm1_bias, qkv_weight, query_bias, value_bias, table_big, table_small, proj_weight, proj_bias, attn_scale, norm2_gain, norm2_bias, up_weight, up_bias, down_weight, down_bias, mlp_scale = weights
    crops_big, len_big, crops_small, len_small, index_big, index_small = layout
    split = crops_big * len_big
    normed = low(layer_norm(rows, norm1_gain, norm1_bias))
    projected = mult(normed, qkv_weight) + jnp.concatenate([query_bias, jnp.zeros_like(query_bias), value_bias])
    projected = low_back(low(projected))
    big = attend(projected[:split].reshape(crops_big, len_big, -1), table_big, index_big)
    small = attend(projected[split:].reshape(crops_small, len_small, -1), table_small, index_small)
    attended = low_back(low(jnp.concatenate([big, small], axis=0)))
    branch = low_back(mult(attended, proj_weight) + proj_bias)
    middle = rows + attn_scale * branch
    normed2 = low(layer_norm(middle, norm2_gain, norm2_bias))
    pre = low_back(mult(normed2, up_weight) + up_bias)
    hidden = low(jax.nn.gelu(pre, approximate=False))
    mlp = low_back(mult(hidden, down_weight) + down_bias)
    return (middle + mlp_scale * mlp) * keep[:, None]

def reference(input_big, input_small, small_counts, cotangent_big, cotangent_small, norm1_gain, norm1_bias, qkv_weight, query_bias, value_bias, table_big, table_small, proj_weight, proj_bias, attn_scale, norm2_gain, norm2_bias, up_weight, up_bias, down_weight, down_bias, mlp_scale):
    params = tuple((item.astype(jnp.float32) for item in (norm1_gain, norm1_bias, qkv_weight, query_bias, value_bias, table_big, table_small, proj_weight, proj_bias, attn_scale, norm2_gain, norm2_bias, up_weight, up_bias, down_weight, down_bias, mlp_scale)))
    images = MB * IMAGES
    rows_big = 2 * LEN_BIG
    layout = (2, LEN_BIG, SC_CAP, LEN_SMALL, rel_index(GRID_BIG), rel_index(GRID_SMALL))

    def join(big, small):
        return jnp.concatenate([big.astype(jnp.float32).reshape(images, rows_big, D), small.astype(jnp.float32).reshape(images, SC_CAP * LEN_SMALL, D)], axis=1)
    rows = join(input_big, input_small)
    cotangent = join(cotangent_big, cotangent_small)
    slot_of = jnp.arange(SC_CAP * LEN_SMALL, dtype=jnp.int32) // LEN_SMALL
    small_keep = (slot_of[None, :] < small_counts.reshape(images, 1)).astype(jnp.float32)
    keep = jnp.concatenate([jnp.ones((images, rows_big), jnp.float32), small_keep], axis=1)

    def forward(params, rows, offset):
        first = tuple((item[0] for item in params))
        second = tuple((item[1] for item in params))

        def one_image(item):
            line, keep_line, offset_line = item
            middle = low_back(low(layer(line, keep_line, first, layout))) + offset_line
            return (middle, layer(middle, keep_line, second, layout))
        return lax.map(jax.checkpoint(one_image), (rows, keep, offset))
    offset = jnp.zeros_like(rows)
    (first_out, second_out), pullback = jax.vjp(forward, params, rows, offset)
    grads, grad_rows, grad_offset = pullback((jnp.zeros_like(first_out), cotangent))

    def part_big(values):
        return values[:, :rows_big].reshape(MB, 2 * IMAGES, LEN_BIG, D)

    def part_small(values):
        return values[:, rows_big:].reshape(MB, SC_CAP * IMAGES, LEN_SMALL, D)
    layer_big = jnp.stack([part_big(first_out), part_big(second_out)]).astype(jnp.bfloat16)
    layer_small = jnp.stack([part_small(first_out), part_small(second_out)]).astype(jnp.bfloat16)
    input_grad_big = jnp.stack([part_big(grad_rows), part_big(grad_offset)]).astype(jnp.bfloat16)
    input_grad_small = jnp.stack([part_small(grad_rows), part_small(grad_offset)]).astype(jnp.bfloat16)
    return (layer_big, layer_small, input_grad_big, input_grad_small, grads[0], grads[1], grads[2], grads[3], grads[4], grads[5], grads[6], grads[7], grads[8], grads[9], grads[10], grads[11], grads[12], grads[13], grads[14], grads[15], grads[16])
```

```python
import math

import jax
import jax.numpy as jnp
from jax import lax
from jax.experimental import pallas as pl
from jax.experimental.pallas import tpu as pltpu
from jax.sharding import PartitionSpec as P

HEADS = 12
EPS = 1e-06
LOW = -1e30
VMEM_BYTES = 56 * 1024 * 1024
F32 = jnp.float32
BF16 = jnp.bfloat16
V = pl.BlockSpec(memory_space=pltpu.VMEM)
S = pl.BlockSpec(memory_space=pltpu.SMEM)
H = pl.BlockSpec(memory_space=pl.ANY)


def up_to(value, multiple):
    return -(-value // multiple) * multiple


def mm(left, right):
    return jnp.dot(left, right, preferred_element_type=F32)


def mm_back(left, right):
    return lax.dot_general(left, right, (((1,), (1,)), ((), ())), preferred_element_type=F32)


def mm_outer(left, right):
    return lax.dot_general(left, right, (((0,), (0,)), ((), ())), preferred_element_type=F32)


def norm_parts(values):
    centre = values - jnp.mean(values, axis=-1, keepdims=True)
    spread = jnp.mean(centre * centre, axis=-1, keepdims=True)
    scale = lax.rsqrt(spread + EPS)
    return centre * scale, scale


def norm_back(upstream, values, gain):
    unit, scale = norm_parts(values)
    scaled = upstream * gain
    first = jnp.mean(scaled, axis=-1, keepdims=True)
    second = jnp.mean(scaled * unit, axis=-1, keepdims=True)
    going = scale * (scaled - first - unit * second)
    return (
        going,
        jnp.sum(upstream * unit, axis=0, keepdims=True),
        jnp.sum(upstream, axis=0, keepdims=True),
    )


def gelu_parts(x):
    raised = jnp.exp(-0.5 * x * x)
    t = 1.0 / (1.0 + (0.3275911 * math.sqrt(0.5)) * jnp.abs(x))
    poly = t * (
        0.127414796
        + t * (-0.142248368 + t * (0.7107068705 + t * (-0.7265760135 + t * 0.5307027145)))
    )
    half = poly * raised
    phi = jnp.where(x >= 0, 1.0 - half, half)
    return x * phi, phi + x * (raised * (1.0 / math.sqrt(2.0 * math.pi)))


def column_cuts(width, parts):
    step = width // parts
    return [(slice(None), pl.ds(i * step, step)) for i in range(parts)]


def row_cuts(height, parts):
    step = height // parts
    return [(pl.ds(i * step, step), slice(None)) for i in range(parts)]


def fetch_start(mine, own, other, buffer, sems, cuts):
    for i, cut in enumerate(cuts):

        @pl.when(mine)
        def _():
            pltpu.make_async_copy(own.at[cut], buffer.at[cut], sems.at[i]).start()

        @pl.when(jnp.logical_not(mine))
        def _():
            pltpu.make_async_copy(other.at[cut], buffer.at[cut], sems.at[i]).start()


def fetch_wait(own, buffer, sems, cuts, i):
    pltpu.make_async_copy(own.at[cuts[i]], buffer.at[cuts[i]], sems.at[i]).wait()


def kernel_call(body, ins, outs, scratch, args, flops, **more):
    moved = sum(math.prod(a.shape) * a.dtype.itemsize for a in args) + sum(
        math.prod(o.shape) * o.dtype.itemsize for o in outs
    )
    return pl.pallas_call(
        body,
        in_specs=ins,
        out_specs=[V] * len(outs),
        out_shape=outs,
        scratch_shapes=scratch,
        compiler_params=pltpu.CompilerParams(vmem_limit_bytes=VMEM_BYTES, **more),
        cost_estimate=pl.CostEstimate(flops=flops, bytes_accessed=moved, transcendentals=0),
    )(*args)


def shape(dims, kind):
    return jax.ShapeDtypeStruct(dims, kind)


def qkv_forward(layer, core, x, gain, shift, joined, own, other):
    rows, width = x.shape
    triple = own.shape[1]
    cuts = column_cuts(triple, 3)

    def body(core_ref, x_ref, gain_ref, shift_ref, joined_ref, own_ref, other_ref, normed_ref, proj_ref, buf, sems):
        mine = core_ref[0] == layer
        fetch_start(mine, own_ref, other_ref, buf, sems, cuts)
        unit, _ = norm_parts(x_ref[...].astype(F32))
        normed_ref[...] = (unit * gain_ref[...] + shift_ref[...]).astype(BF16)
        for i in range(3):
            fetch_wait(own_ref, buf, sems, cuts, i)
            cols = pl.ds(i * width, width)
            proj_ref[:, cols] = (mm(normed_ref[...], buf[:, cols]) + joined_ref[:, cols]).astype(BF16)

    return kernel_call(
        body,
        [S, V, V, V, V, H, H],
        [shape((rows, width), BF16), shape((rows, triple), BF16)],
        [pltpu.VMEM((width, triple), BF16), pltpu.SemaphoreType.DMA((3,))],
        (core, x, gain, shift, joined, own, other),
        2 * rows * width * triple,
    )


def build_bias(base, out_ref, block_ref, grid, corner, crops, length, block_rows):
    lanes = base.shape[1]
    head_patch, patch_head, head_head = corner
    lane = lax.broadcasted_iota(jnp.int32, (block_rows, 256), 1)
    line = lax.broadcasted_iota(jnp.int32, (block_rows, 256), 0)
    first = jnp.where(lane == 0, head_head, head_patch)
    block_ref[...] = jnp.where(lane >= length, LOW, first)
    small = lane[:grid]
    for r in range(grid):
        off = (grid - 1 - r) * grid
        moved = base if off == 0 else pltpu.roll(base, lanes - off, 1)
        moved = moved[:grid, :256]
        value = jnp.where(small == 0, patch_head, jnp.where(small >= length, LOW, moved))
        block_ref[pl.ds(1 + grid * r, grid), :] = value
    if crops == 1:
        return
    out_ref[...] = jnp.full(out_ref.shape, LOW, F32)
    for s in range(crops):
        value = block_ref[pl.ds(0, length), :]
        if s:
            value = pltpu.roll(value, s * length, 1)
        out_ref[pl.ds(s * length, length), :] = value


def attention_forward(projected, base_big, base_small, corners, sizes):
    rows, triple = projected.shape
    width = triple // 3
    pairs = HEADS // 2
    crops, len_big, pad_big, slots, len_small, pad_small = sizes
    grid_big, grid_small = math.isqrt(len_big - 1), math.isqrt(len_small - 1)

    def body(corner_ref, q_ref, k_ref, v_ref, bb_ref, bs_ref, out_ref, big, block, small):
        pair = pl.program_id(0)
        lane = lax.broadcasted_iota(jnp.int32, (1, 128), 1)
        for h in range(2):
            head = pair * 2 + h
            take = (lane // 64) == h
            build_bias(bb_ref[h], big, big, grid_big, [corner_ref[0, i, head] for i in range(3)], 1, len_big, pad_big)
            build_bias(bs_ref[h], small, block, grid_small, [corner_ref[1, i, head] for i in range(3)], slots, len_small, block.shape[0])

            def one(start, count, bias):
                part = pl.ds(start, count)
                q = jnp.where(take, q_ref[part, :], 0)
                scores = mm_back(q, k_ref[part, :]) * 0.125 + bias[:, :count]
                raised = jnp.exp(scores - jnp.max(scores, axis=-1, keepdims=True))
                probs = raised / jnp.sum(raised, axis=-1, keepdims=True)
                result = mm(probs.astype(BF16), v_ref[part, :]).astype(BF16)
                if h == 0:
                    out_ref[part, :] = result
                else:
                    out_ref[part, :] = jnp.where(take, result, out_ref[part, :])

            for crop in range(crops):
                one(crop * pad_big, pad_big, big)
            one(crops * pad_big, pad_small, small)

    return pl.pallas_call(
        body,
        grid=(pairs,),
        in_specs=[
            S,
            pl.BlockSpec((rows, 128), lambda p: (0, p)),
            pl.BlockSpec((rows, 128), lambda p: (0, pairs + p)),
            pl.BlockSpec((rows, 128), lambda p: (0, 2 * pairs + p)),
            pl.BlockSpec((2,) + base_big.shape[1:], lambda p: (p, 0, 0)),
            pl.BlockSpec((2,) + base_small.shape[1:], lambda p: (p, 0, 0)),
        ],
        out_specs=pl.BlockSpec((rows, 128), lambda p: (0, p)),
        out_shape=shape((rows, width), BF16),
        scratch_shapes=[
            pltpu.VMEM((pad_big, 256), F32),
            pltpu.VMEM((up_to(len_small, 8), 256), F32),
            pltpu.VMEM((pad_small, 256), F32),
        ],
        compiler_params=pltpu.CompilerParams(vmem_limit_bytes=VMEM_BYTES),
        cost_estimate=pl.CostEstimate(flops=8 * 10**9, bytes_accessed=4 * rows * width * 2, transcendentals=0),
    )(corners, projected, projected, projected, base_big, base_small)


FF_STEP = 512


def up_forward(layer, core, attended, x, vec, up_bias, own, other, own_up, other_up):
    rows, width = x.shape
    hidden = own_up.shape[1]
    count = hidden // FF_STEP
    cuts = [(slice(None), slice(None))]
    up_cuts = column_cuts(hidden, count)

    def body(core_ref, att_ref, x_ref, vec_ref, bias_ref, own_ref, other_ref, own_up_ref, other_up_ref, branch_ref, middle_ref, normed_ref, hidden_ref, slope_ref, buf, buf_up, sems, sems_up):
        mine = core_ref[0] == layer
        fetch_start(mine, own_ref, other_ref, buf, sems, cuts)
        fetch_start(mine, own_up_ref, other_up_ref, buf_up, sems_up, up_cuts)
        fetch_wait(own_ref, buf, sems, cuts, 0)
        branch = mm(att_ref[...], buf[...]) + vec_ref[4:5, :]
        branch_ref[...] = branch
        middle = x_ref[...].astype(F32) + vec_ref[5:6, :] * branch
        middle_ref[...] = middle
        unit, _ = norm_parts(middle)
        normed_ref[...] = (unit * vec_ref[6:7, :] + vec_ref[7:8, :]).astype(BF16)
        for i in range(count):
            fetch_wait(own_up_ref, buf_up, sems_up, up_cuts, i)
            cols = pl.ds(i * FF_STEP, FF_STEP)
            pre = mm(normed_ref[...], buf_up[:, cols]) + bias_ref[:, cols]
            value, slope = gelu_parts(pre)
            hidden_ref[:, cols] = value.astype(BF16)
            slope_ref[:, cols] = slope.astype(BF16)

    return kernel_call(
        body,
        [S, V, V, V, V, H, H, H, H],
        [
            shape((rows, width), F32),
            shape((rows, width), F32),
            shape((rows, width), BF16),
            shape((rows, hidden), BF16),
            shape((rows, hidden), BF16),
        ],
        [
            pltpu.VMEM((width, width), BF16),
            pltpu.VMEM((width, hidden), BF16),
            pltpu.SemaphoreType.DMA((1,)),
            pltpu.SemaphoreType.DMA((count,)),
        ],
        (core, attended, x, vec, up_bias, own, other, own_up, other_up),
        2 * rows * width * (width + hidden),
    )


def down_forward(layer, core, hidden, middle, keep, vec, own, other):
    rows, width = middle.shape
    depth = hidden.shape[1]
    cuts = row_cuts(depth, 2)
    half = depth // 2

    def body(core_ref, hidden_ref, middle_ref, keep_ref, vec_ref, own_ref, other_ref, y_ref, mlp_ref, buf, sems):
        fetch_start(core_ref[0] == layer, own_ref, other_ref, buf, sems, cuts)
        total = vec_ref[8:9, :]
        for i in range(2):
            fetch_wait(own_ref, buf, sems, cuts, i)
            part = pl.ds(i * half, half)
            total = total + mm(hidden_ref[:, part], buf[part, :])
        mlp_ref[...] = total
        y_ref[...] = ((middle_ref[...] + vec_ref[9:10, :] * total) * keep_ref[...]).astype(BF16)

    return kernel_call(
        body,
        [S, V, V, V, V, H, H],
        [shape((rows, width), BF16), shape((rows, width), F32)],
        [pltpu.VMEM((depth, width), BF16), pltpu.SemaphoreType.DMA((2,))],
        (core, hidden, middle, keep, vec, own, other),
        2 * rows * width * depth,
    )


def mlp_backward(layer, core, upstream, keep, vec, slope, middle, branch, down, up, proj):
    rows, width = middle.shape
    depth = slope.shape[1]
    count = depth // FF_STEP
    half_cols, half_width = depth // 2, width // 2
    down_cuts, up_cuts = row_cuts(depth, count), column_cuts(depth, count)
    cuts = [(slice(None), slice(None))]

    def body(core_ref, g_ref, keep_ref, vec_ref, slope_ref, middle_ref, branch_ref, od, td, ou, tu, op, tp, gm_ref, gp_ref, gb_ref, ga_ref, gmid_ref, vecs_ref, ups_ref, acc, low, bd, bu, bp, sd, su, sp):
        me = core_ref[0]
        mine = me == layer
        fetch_start(mine, od, td, bd, sd, down_cuts)
        fetch_start(mine, ou, tu, bu, su, up_cuts)
        fetch_start(mine, op, tp, bp, sp, cuts)
        gm = (vec_ref[9:10, :] * (g_ref[...].astype(F32) * keep_ref[...])).astype(BF16)
        low[...] = gm
        gm_ref[me] = gm[:, :half_width]
        gm_ref[1 - me] = gm[:, half_width:]
        vecs_ref[...] = jnp.zeros_like(vecs_ref)
        vecs_ref[4:5, :] = jnp.sum(gm.astype(F32), axis=0, keepdims=True)
        for i in range(count):
            cols = pl.ds(i * FF_STEP, FF_STEP)
            fetch_wait(od, bd, sd, down_cuts, i)
            gp = (mm_back(low[...], bd[cols, :]) * slope_ref[:, cols].astype(F32)).astype(BF16)
            slot = me if 2 * i < count else 1 - me
            gp_ref[slot, :, pl.ds((i * FF_STEP) % half_cols, FF_STEP)] = gp
            ups_ref[:, cols] = jnp.sum(gp.astype(F32), axis=0, keepdims=True)
            fetch_wait(ou, bu, su, up_cuts, i)
            more = mm_back(gp, bu[:, cols])
            if i == 0:
                acc[...] = more
            else:
                acc[...] += more
        going, gain, shift = norm_back(acc[...], middle_ref[...], vec_ref[6:7, :])
        gmid = g_ref[...].astype(F32) * keep_ref[...] + going
        gmid_ref[...] = gmid
        gb = (vec_ref[5:6, :] * gmid).astype(BF16)
        low[...] = gb
        gb_ref[me] = gb[:, :half_width]
        gb_ref[1 - me] = gb[:, half_width:]
        vecs_ref[0:1, :] = gain
        vecs_ref[1:2, :] = shift
        vecs_ref[2:3, :] = jnp.sum(gmid * branch_ref[...], axis=0, keepdims=True)
        vecs_ref[3:4, :] = jnp.sum(gb.astype(F32), axis=0, keepdims=True)
        fetch_wait(op, bp, sp, cuts, 0)
        ga_ref[...] = mm_back(low[...], bp[...]).astype(BF16)

    return kernel_call(
        body,
        [S, V, V, V, V, V, V] + [H] * 6,
        [
            shape((2, rows, half_width), BF16),
            shape((2, rows, half_cols), BF16),
            shape((2, rows, half_width), BF16),
            shape((rows, width), BF16),
            shape((rows, width), F32),
            shape((8, width), F32),
            shape((1, depth), F32),
        ],
        [
            pltpu.VMEM((rows, width), F32),
            pltpu.VMEM((rows, width), BF16),
            pltpu.VMEM((depth, width), BF16),
            pltpu.VMEM((width, depth), BF16),
            pltpu.VMEM((width, width), BF16),
            pltpu.SemaphoreType.DMA((count,)),
            pltpu.SemaphoreType.DMA((count,)),
            pltpu.SemaphoreType.DMA((1,)),
        ],
        (core, upstream, keep, vec, slope, middle, branch) + down + up + proj,
        2 * rows * width * (2 * depth + width),
    )


def attention_backward(core, projected, upstream, base_big, base_small, corners, sizes):
    rows, triple = projected.shape
    width = triple // 3
    pairs = HEADS // 2
    crops, len_big, pad_big, slots, len_small, pad_small = sizes
    grid_big, grid_small = math.isqrt(len_big - 1), math.isqrt(len_small - 1)
    half = 3 * pairs // 2

    def body(core_ref, corner_ref, q_ref, k_ref, v_ref, g_ref, bb_ref, bs_ref, gproj_ref, tb_ref, ts_ref, sums_ref, big, block, small, dbig, dsmall, dblock):
        pair = pl.program_id(0)
        me = core_ref[0]
        lane = lax.broadcasted_iota(jnp.int32, (1, 128), 1)

        def put(which, part, value, h):
            place = which * pairs + pair + half * me
            place = jnp.where(place >= 2 * half, place - 2 * half, place)
            value = value.astype(BF16)
            if h == 0:
                gproj_ref[place, part, :] = value
            else:
                gproj_ref[place, part, :] = jnp.where((lane // 64) == h, value, gproj_ref[place, part, :])

        for h in range(2):
            head = pair * 2 + h
            take = (lane // 64) == h
            build_bias(bb_ref[h], big, big, grid_big, [corner_ref[0, i, head] for i in range(3)], 1, len_big, pad_big)
            build_bias(bs_ref[h], small, block, grid_small, [corner_ref[1, i, head] for i in range(3)], slots, len_small, block.shape[0])

            def one(start, count, bias, dref, first):
                part = pl.ds(start, count)
                q, k, v, g = q_ref[part, :], k_ref[part, :], v_ref[part, :], g_ref[part, :]
                scores = mm_back(jnp.where(take, q, 0), k) * 0.125 + bias[:, :count]
                raised = jnp.exp(scores - jnp.max(scores, axis=-1, keepdims=True))
                probs = raised / jnp.sum(raised, axis=-1, keepdims=True)
                gpr = mm_back(jnp.where(take, g, 0), v)
                inner = jnp.sum(probs * gpr, axis=-1, keepdims=True)
                gs = (probs * (gpr - inner)).astype(BF16)
                if first:
                    dref[:, :count] = gs.astype(F32)
                else:
                    dref[:, :count] += gs.astype(F32)
                put(0, part, mm(gs, k) * 0.125, h)
                put(1, part, mm_outer(gs, q) * 0.125, h)
                put(2, part, mm_outer(probs.astype(BF16), g), h)

            for crop in range(crops):
                one(crop * pad_big, pad_big, big, dbig, crop == 0)
            one(crops * pad_big, pad_small, small, dsmall, True)

            def fold(dref, grid, length, out_ref):
                lanes = out_ref.shape[2]
                wide = lax.broadcasted_iota(jnp.int32, (grid, 256), 1)
                inside = (wide > 0) & (wide < length)
                total = jnp.zeros((grid, lanes), F32)
                for r in range(grid):
                    value = jnp.where(inside, dref[pl.ds(1 + grid * r, grid), :], 0)
                    if lanes > 256:
                        value = jnp.concatenate([value, jnp.zeros((grid, lanes - 256), F32)], axis=1)
                    off = (grid - 1 - r) * grid
                    total = total + (value if off == 0 else pltpu.roll(value, off, 1))
                out_ref[h, :grid, :] = total
                line = lax.broadcasted_iota(jnp.int32, (length, 256), 0)
                spot = lax.broadcasted_iota(jnp.int32, (length, 256), 1)
                value = jnp.where(spot < length, dref[pl.ds(0, length), :], 0)
                out_ref[h, grid : grid + 1, :256] = value[0:1, :]
                out_ref[h, grid + 1 : grid + 2, :256] = jnp.sum(jnp.where(line > 0, value, 0), axis=0, keepdims=True)

            if h == 0:
                tb_ref[...] = jnp.zeros_like(tb_ref)
                ts_ref[...] = jnp.zeros_like(ts_ref)
            fold(dbig, grid_big, len_big, tb_ref)
            total = dsmall[pl.ds(0, len_small), :]
            for s in range(1, slots):
                total = total + pltpu.roll(dsmall[pl.ds(s * len_small, len_small), :], 256 - s * len_small, 1)
            dblock[pl.ds(0, len_small), :] = total
            fold(dblock, grid_small, len_small, ts_ref)
        for n, which in ((0, 0), (1, 2)):
            place = which * pairs + pair + half * me
            place = jnp.where(place >= 2 * half, place - 2 * half, place)
            sums_ref[n : n + 1, :] = jnp.sum(gproj_ref[place].astype(F32), axis=0, keepdims=True)

    tb_shape, ts_shape = (16, 512), (8, 256)

    def clear(*refs):
        @pl.when(pl.program_id(0) == 0)
        def _():
            refs[-3][...] = jnp.zeros_like(refs[-3])
            refs[-2][...] = jnp.zeros_like(refs[-2])
            refs[-1][...] = jnp.zeros_like(refs[-1])

        body(*refs)

    return pl.pallas_call(
        clear,
        grid=(pairs,),
        in_specs=[
            S,
            S,
            pl.BlockSpec((rows, 128), lambda p: (0, p)),
            pl.BlockSpec((rows, 128), lambda p: (0, pairs + p)),
            pl.BlockSpec((rows, 128), lambda p: (0, 2 * pairs + p)),
            pl.BlockSpec((rows, 128), lambda p: (0, p)),
            pl.BlockSpec((2,) + base_big.shape[1:], lambda p: (p, 0, 0)),
            pl.BlockSpec((2,) + base_small.shape[1:], lambda p: (p, 0, 0)),
        ],
        out_specs=[
            pl.BlockSpec((2 * half, rows, 128), lambda p: (0, 0, 0)),
            pl.BlockSpec((2,) + tb_shape, lambda p: (p, 0, 0)),
            pl.BlockSpec((2,) + ts_shape, lambda p: (p, 0, 0)),
            pl.BlockSpec((2, 128), lambda p: (0, p)),
        ],
        out_shape=[
            shape((2 * half, rows, 128), BF16),
            shape((HEADS,) + tb_shape, F32),
            shape((HEADS,) + ts_shape, F32),
            shape((2, width), F32),
        ],
        scratch_shapes=[
            pltpu.VMEM((pad_big, 256), F32),
            pltpu.VMEM((up_to(len_small, 8), 256), F32),
            pltpu.VMEM((pad_small, 256), F32),
            pltpu.VMEM((pad_big, 256), F32),
            pltpu.VMEM((pad_small, 256), F32),
            pltpu.VMEM((up_to(len_small, 8), 256), F32),
        ],
        compiler_params=pltpu.CompilerParams(vmem_limit_bytes=VMEM_BYTES),
        cost_estimate=pl.CostEstimate(flops=20 * 10**9, bytes_accessed=8 * rows * width * 2, transcendentals=0),
    )(core, corners, projected, projected, projected, upstream, base_big, base_small)


def qkv_backward(layer, core, gproj, x, gmid, gain, own, other):
    rows, width = x.shape
    blocks = gproj.shape[0]
    triple = blocks * 128
    cuts = column_cuts(triple, 3)
    group = blocks // 3

    def body(core_ref, gproj_ref, x_ref, gmid_ref, gain_ref, own_ref, other_ref, gx_ref, vecs_ref, buf, acc, sems):
        me = core_ref[0]
        fetch_start(me == layer, own_ref, other_ref, buf, sems, cuts)
        for i in range(3):
            fetch_wait(own_ref, buf, sems, cuts, i)
            places = [n + (blocks // 2) * me for n in range(i * group, (i + 1) * group)]
            places = [jnp.where(place >= blocks, place - blocks, place) for place in places]
            joined = jnp.concatenate([gproj_ref[place] for place in places], axis=1)
            more = mm_back(joined, buf[:, pl.ds(i * width, width)])
            if i == 0:
                acc[...] = more
            else:
                acc[...] += more
        going, gain_sum, shift_sum = norm_back(acc[...], x_ref[...].astype(F32), gain_ref[...])
        gx_ref[...] = (gmid_ref[...] + going).astype(BF16)
        vecs_ref[0:1, :] = gain_sum
        vecs_ref[1:2, :] = shift_sum

    return kernel_call(
        body,
        [S, V, V, V, V, H, H],
        [shape((rows, width), BF16), shape((2, width), F32)],
        [
            pltpu.VMEM((width, triple), BF16),
            pltpu.VMEM((rows, width), F32),
            pltpu.SemaphoreType.DMA((3,)),
        ],
        (core, gproj, x, gmid, gain, own, other),
        2 * rows * width * triple,
    )


def place_of(relative, order):
    place = 0
    for bit in order:
        place = place * 2 + ((relative >> bit) & 1)
    return place


def store_block(keep, send, place, sub, value):
    low = keep.shape[0]

    @pl.when(place < low)
    def _():
        keep[place, sub] = value

    @pl.when(place >= low)
    def _():
        send[place - low, sub] = value


def weight_grad_tall(where, orders, x_own, x_other, g_own, g_other):
    devices = 1 << len(orders[0])
    rows, tall = x_own.shape
    cols = g_own.shape[1]
    step = 384
    block = tall // devices
    pieces = cols // 128

    def body(where_ref, xo, xt, go, gt, *outs):
        at = pl.program_id(0)
        left = jnp.concatenate([xo[...], xt[...]], axis=0)
        right = jnp.concatenate([go[...], gt[...]], axis=0)
        value = mm_outer(left, right)
        for n in range(step // block):
            relative = (at * (step // block) + n) ^ where_ref[1]
            part = value[n * block : (n + 1) * block]
            for p in range(pieces):
                store_block(outs[2 * p], outs[2 * p + 1], place_of(relative, orders[p]), 0, part[:, p * 128 : (p + 1) * 128].astype(BF16))

    out = shape((devices // 2, 1, block, 128), BF16)
    return pl.pallas_call(
        body,
        grid=(tall // step,),
        in_specs=[
            S,
            pl.BlockSpec((rows, step), lambda i: (0, i)),
            pl.BlockSpec((rows, step), lambda i: (0, i)),
            pl.BlockSpec((rows, cols), lambda i: (0, 0)),
            pl.BlockSpec((rows, cols), lambda i: (0, 0)),
        ],
        out_specs=[pl.BlockSpec(out.shape, lambda i: (0, 0, 0, 0))] * (2 * pieces),
        out_shape=[out] * (2 * pieces),
        compiler_params=pltpu.CompilerParams(vmem_limit_bytes=VMEM_BYTES, fuse_transposed_lhs_in_matmul=True),
        cost_estimate=pl.CostEstimate(flops=4 * rows * tall * cols, bytes_accessed=4 * rows * (tall + cols) + 2 * tall * cols, transcendentals=0),
    )(where, x_own, x_other, g_own, g_other)


def weight_grad_wide(where, orders, parts):
    devices = 1 << len(orders[0])
    pieces = len(orders)
    rows, width = parts[0][0].shape
    block = width // devices
    blocked = [part[2].ndim == 3 for part in parts]
    tiles = [part[2].shape[0] if part[2].ndim == 3 else part[2].shape[1] // 128 for part in parts]
    subs = sum(tiles) // pieces

    def body(where_ref, *refs):
        outs = refs[4 * len(parts) :]
        sub = 0
        for n, part in enumerate(parts):
            xo, xt, go, gt = refs[4 * n : 4 * n + 4]
            left = jnp.concatenate([xo[...], xt[...]], axis=0)
            count = tiles[n] // pieces
            for p in range(pieces):
                t = 0
                while t < count:
                    two = min(2, count - t)
                    at = p * count + t
                    if blocked[n]:
                        right = jnp.concatenate(
                            [jnp.concatenate([go[at + m], gt[at + m]], axis=0) for m in range(two)], axis=1
                        )
                    else:
                        cut = pl.ds(at * 128, two * 128)
                        right = jnp.concatenate([go[:, cut], gt[:, cut]], axis=0)
                    value = mm_outer(left, right)
                    for j in range(devices):
                        relative = j ^ where_ref[1]
                        place = place_of(relative, orders[p])
                        for m in range(two):
                            part_value = value[j * block : (j + 1) * block, m * 128 : (m + 1) * 128]
                            store_block(outs[2 * p], outs[2 * p + 1], place, sub + t + m, part_value.astype(BF16))
                    t += two
            sub += count

    out = shape((devices // 2, subs, block, 128), BF16)
    args = [item for part in parts for item in part]
    return kernel_call(
        body,
        [S] + [V] * len(args),
        [out] * (2 * pieces),
        [],
        (where, *args),
        4 * rows * width * 128 * sum(tiles),
        fuse_transposed_lhs_in_matmul=True,
    )


def swap(value):
    return lax.ppermute(value, "section", [(0, 1), (1, 0)])


def across(value, bit):
    return lax.ppermute(value, "dp", [(i, i ^ (1 << bit)) for i in range(lax.axis_size("dp"))])


def scatter_sum(keep, send, order):
    for n, bit in enumerate(order):
        total = keep.astype(F32) + across(send, bit).astype(F32)
        if n + 1 < len(order):
            total = total.astype(BF16)
            half = total.shape[0] // 2
            keep, send = total[:half], total[half:]
    return total[0]


def bias_base(table, grid, rows, lanes):
    side = 2 * grid - 1
    flipped = table[: side * side].reshape(side, side, -1)[::-1, ::-1]
    base = jnp.stack([flipped[:, grid - 1 - r : 2 * grid - 1 - r] for r in range(grid)])
    base = jnp.transpose(base, (3, 0, 1, 2)).reshape(table.shape[1], grid, side * grid)
    return jnp.pad(base, ((0, 0), (0, rows - grid), (1, lanes - 1 - side * grid)))


def table_grad(folded, grid, length):
    side = 2 * grid - 1
    heads = folded.shape[0]
    body = folded[:, :grid, 1 : 1 + side * grid].reshape(heads, grid, side, grid)
    flipped = sum(
        jnp.pad(body[:, r], ((0, 0), (0, 0), (grid - 1 - r, r))) for r in range(grid)
    )
    inner = jnp.transpose(flipped[:, ::-1, ::-1], (1, 2, 0)).reshape(side * side, heads)
    first = folded[:, grid, :length]
    ends = jnp.stack([jnp.sum(first[:, 1:], axis=1), folded[:, grid + 1, 0], first[:, 0]])
    return jnp.concatenate([inner, ends], axis=0)


def body(input_big, input_small, small_counts, cotangent_big, cotangent_small, norm1_gain, norm1_bias, qkv_weight, query_bias, value_bias, table_big, table_small, proj_weight, proj_bias, attn_scale, norm2_gain, norm2_bias, up_weight, up_bias, down_weight, down_bias, mlp_scale):
    micro, crops, len_big, width = input_big.shape
    slots_all, len_small = input_small.shape[1], input_small.shape[2]
    slots = slots_all // small_counts.shape[1]
    grid_big, grid_small = math.isqrt(len_big - 1), math.isqrt(len_small - 1)
    pad_big = up_to(len_big, 16)
    real_small = slots_all * len_small
    pad_small = up_to(real_small, 16)
    split = crops * pad_big
    rows = split + pad_small
    sizes = (crops, len_big, pad_big, slots_all, len_small, pad_small)
    devices = lax.axis_size("dp")
    bits = devices.bit_length() - 1
    core = lax.axis_index("section")
    place = lax.axis_index("dp")
    where = jnp.stack([core, place]).astype(jnp.int32)
    first = core == 0

    def join(big, small):
        big = lax.dynamic_index_in_dim(big, core, 0, keepdims=False)
        small = lax.dynamic_index_in_dim(small, core, 0, keepdims=False)
        big = jnp.pad(big, ((0, 0), (0, pad_big - len_big), (0, 0))).reshape(split, width)
        small = jnp.pad(small.reshape(real_small, width), ((0, pad_small - real_small), (0, 0)))
        return jnp.concatenate([big, small])

    x0 = join(input_big, input_small)
    cotangent = join(cotangent_big, cotangent_small)
    counts = lax.dynamic_index_in_dim(small_counts, core, 0, keepdims=False)
    line = jnp.arange(rows, dtype=jnp.int32)
    spot = line - split
    limit = jnp.repeat(counts, slots * len_small, total_repeat_length=real_small)
    small_keep = (jnp.arange(real_small, dtype=jnp.int32) // len_small % slots < limit).astype(F32)
    keep = jnp.where(line < split, (line % pad_big < len_big).astype(F32), jnp.pad(small_keep, (split, pad_small - real_small)))
    keep = keep[:, None]

    vec_own = jnp.concatenate(
        [norm1_gain, norm1_bias, query_bias, value_bias, proj_bias, attn_scale, norm2_gain, norm2_bias, down_bias, mlp_scale, up_bias.reshape(-1, width)]
    )
    tables_own = jnp.concatenate([table_big[0], table_small[0]])
    vec_other, tables_other = swap(vec_own), swap(tables_own)
    qkv = (qkv_weight[0], swap(qkv_weight[0]))
    proj = (proj_weight[0], swap(proj_weight[0]))
    up = (up_weight[0], swap(up_weight[0]))
    down = (down_weight[0], swap(down_weight[0]))

    layers = []
    for layer in range(2):
        vec = jnp.where(core == layer, vec_own, vec_other)
        tables = jnp.where(core == layer, tables_own, tables_other)
        part_big, part_small = tables[: table_big.shape[1]], tables[table_big.shape[1] :]
        ups = vec[10:].reshape(1, -1)
        joined = jnp.concatenate([vec[2:3], jnp.zeros_like(vec[2:3]), vec[3:4]], axis=1)
        corners = jnp.stack([part_big[-3:], part_small[-3:]])
        base_big = bias_base(part_big, grid_big, 16, 512)
        base_small = bias_base(part_small, grid_small, 8, 256)
        layers.append((vec, ups, joined, corners, base_big, base_small))

    saved = []
    x = x0
    outs = []
    for layer in range(2):
        vec, ups, joined, corners, base_big, base_small = layers[layer]
        normed, projected = qkv_forward(layer, where, x, vec[0:1], vec[1:2], joined, *qkv)
        attended = attention_forward(projected, base_big, base_small, corners, sizes)
        branch, middle, normed2, hidden, slope = up_forward(layer, where, attended, x, vec, ups, *proj, *up)
        y, mlp = down_forward(layer, where, hidden, middle, keep, vec, *down)
        saved.append((x, normed, projected, attended, branch, middle, normed2, hidden, slope, mlp))
        outs.append(y)
        x = y

    orders = [list(range(bits)), [1, 0] + list(range(2, bits)), [2, 0, 1] + list(range(3, bits))]
    g = cotangent
    backs = [None, None]
    sums = [None, None]
    flats = [None, None]
    for layer in (1, 0):
        vec, ups, joined, corners, base_big, base_small = layers[layer]
        x, normed, projected, attended, branch, middle, normed2, hidden, slope, mlp = saved[layer]
        hidden_other, normed2_other, attended_other, normed_other = swap(hidden), swap(normed2), swap(attended), swap(normed)
        gm, gp, gb, ga, gmid, vecs2, up_sum = mlp_backward(layer, where, g, keep, vec, slope, middle, branch, down, up, proj)
        scale_sum = jnp.sum(g.astype(F32) * keep * mlp, axis=0, keepdims=True)
        gm_other, gp_other, gb_other = swap(gm[1]), swap(gp[1]), swap(gb[1])
        tall = weight_grad_tall(where, orders, hidden, hidden_other, gm[0], gm_other)
        wide = weight_grad_wide(where, orders, [(normed2, normed2_other, gp[0], gp_other)])
        gproj, fold_big, fold_small, qv_sum = attention_backward(where, projected, ga, base_big, base_small, corners, sizes)
        half = gproj.shape[0] // 2
        gproj_other = swap(gproj[half:])
        g, vecs1 = qkv_backward(layer, where, gproj, x, gmid, vec[0:1], *qkv)
        last = weight_grad_wide(where, orders, [(attended, attended_other, gb[0], gb_other), (normed, normed_other, gproj[:half], gproj_other)])
        backs[layer] = g
        sums[layer] = [
            scatter_sum(group[2 * p], group[2 * p + 1], orders[p]) for group in (tall, wide, last) for p in range(3)
        ]
        small = jnp.concatenate([vecs1, qv_sum, vecs2[3:4], vecs2[2:3], vecs2[0:2], vecs2[4:5], scale_sum, up_sum.reshape(-1, width)])
        flat = jnp.concatenate(
            [small.reshape(-1), table_grad(fold_big, grid_big, len_big).reshape(-1), table_grad(fold_small, grid_small, len_small).reshape(-1)]
        )
        flat = jnp.pad(flat, (0, up_to(flat.shape[0], 1024) - flat.shape[0])).reshape(-1, 128)
        flat = flat + swap(flat)
        for bit in range(bits):
            flat = flat + across(flat, bit)
        flats[layer] = flat.reshape(-1)

    def pick(zero, one):
        return jnp.where(first, zero, one)

    def unpad(value):
        big = value[:split].reshape(crops, pad_big, width)[:, :len_big]
        return big, value[split : split + real_small].reshape(slots_all, len_small, width)

    def assemble(zero, one):
        kept, came = pick(zero, one), swap(pick(one, zero))
        parts = [pick(kept, came), pick(came, kept)]
        pairs = [unpad(part) for part in parts]
        return jnp.stack([p[0] for p in pairs])[None], jnp.stack([p[1] for p in pairs])[None]

    layer_big, layer_small = assemble(*outs)
    grad_big, grad_small = assemble(*backs)

    block = width // devices
    halves = [[], []]
    for zero, one in zip(sums[0], sums[1]):
        kept, came = pick(zero, one), swap(pick(one, zero))
        halves[0].append(pick(kept, came))
        halves[1].append(pick(came, kept))

    def columns(pieces, low, high):
        tiles = [piece[n] for piece in pieces for n in range(low, high)]
        return jnp.concatenate(tiles, axis=1)

    grad_down = jnp.concatenate([columns(side[0:3], 0, 1) for side in halves], axis=1)
    wide_subs = sums[0][3].shape[0]
    grad_up = jnp.concatenate([columns(side[3:6], 0, wide_subs) for side in halves], axis=1)
    grad_proj = jnp.concatenate([columns(side[6:9], 0, 1) for side in halves], axis=1)
    grad_qkv = jnp.concatenate([columns(side[6:9], 1, wide_subs) for side in halves], axis=1)

    flat = pick(flats[0], flats[1])

    def vector(row, count=1):
        whole = flat[row * width : (row + count) * width]
        size = count * block
        return lax.dynamic_slice_in_dim(whole, place * size, size)[None]

    ff = up_bias.shape[1] // width
    start = (10 + ff) * width
    size_big, size_small = table_big.shape[1] * HEADS, table_small.shape[1] * HEADS
    grad_table_big = flat[start : start + size_big].reshape(table_big.shape)
    grad_table_small = flat[start + size_big : start + size_big + size_small].reshape(table_small.shape)
    return (
        layer_big,
        layer_small,
        grad_big,
        grad_small,
        vector(0),
        vector(1),
        grad_qkv[None],
        vector(2),
        vector(3),
        grad_table_big,
        grad_table_small,
        grad_proj[None],
        vector(4),
        vector(5),
        vector(6),
        vector(7),
        grad_up[None],
        vector(10, ff),
        grad_down[None],
        vector(8),
        vector(9),
    )


def solution(mesh):
    row = P("section", None)
    whole = P("section", None, None)
    dp4 = P(None, "dp", None, None)
    in_specs = (dp4, dp4, P(None, "dp"), dp4, dp4, row, row, whole, row, row, whole, whole, whole, row, row, row, row, whole, row, whole, row, row)
    out5 = P("section", None, "dp", None, None)
    vec = P("section", "dp")
    mat = P("section", "dp", None)
    out_specs = (out5, out5, out5, out5, vec, vec, mat, vec, vec, whole, whole, mat, vec, vec, vec, vec, mat, vec, mat, vec, vec)
    return jax.shard_map(body, mesh=mesh, in_specs=in_specs, out_specs=out_specs, check_vma=False)
```

```python
import math

import jax
import jax.numpy as jnp
from jax import lax
from jax.experimental import pallas as pl
from jax.experimental.pallas import tpu as pltpu
from jax.sharding import PartitionSpec as P

HEADS = 12
EPS = 1e-06
LOW = -1e30
MIB = 1024 * 1024
F32 = jnp.float32
BF16 = jnp.bfloat16
V = pl.BlockSpec(memory_space=pltpu.VMEM)
S = pl.BlockSpec(memory_space=pltpu.SMEM)
H = pl.BlockSpec(memory_space=pltpu.HBM)


def up_to(value, multiple):
    return -(-value // multiple) * multiple


def mm(left, right):
    return jnp.dot(left, right, preferred_element_type=F32)


def mm_back(left, right):
    return lax.dot_general(left, right, (((1,), (1,)), ((), ())), preferred_element_type=F32)


def mm_outer(left, right):
    return lax.dot_general(left, right, (((0,), (0,)), ((), ())), preferred_element_type=F32)


def norm_parts(values):
    centre = values - jnp.mean(values, axis=-1, keepdims=True)
    spread = jnp.mean(centre * centre, axis=-1, keepdims=True)
    scale = lax.rsqrt(spread + EPS)
    return centre * scale, scale


def norm_back(upstream, values, gain):
    unit, scale = norm_parts(values)
    scaled = upstream * gain
    first = jnp.mean(scaled, axis=-1, keepdims=True)
    second = jnp.mean(scaled * unit, axis=-1, keepdims=True)
    going = scale * (scaled - first - unit * second)
    return (
        going,
        jnp.sum(upstream * unit, axis=0, keepdims=True),
        jnp.sum(upstream, axis=0, keepdims=True),
    )


def gelu_parts(x):
    raised = jnp.exp(-0.5 * x * x)
    t = 1.0 / (1.0 + (0.3275911 * math.sqrt(0.5)) * jnp.abs(x))
    poly = t * (
        0.127414796
        + t * (-0.142248368 + t * (0.7107068705 + t * (-0.7265760135 + t * 0.5307027145)))
    )
    half = poly * raised
    phi = jnp.where(x >= 0, 1.0 - half, half)
    return x * phi, phi + x * (raised * (1.0 / math.sqrt(2.0 * math.pi)))


def column_cuts(width, parts):
    step = width // parts
    return [(slice(None), pl.ds(i * step, step)) for i in range(parts)]


def row_cuts(height, parts):
    step = height // parts
    return [(pl.ds(i * step, step), slice(None)) for i in range(parts)]


def fetch_start(mine, own, other, buffer, sems, cuts):
    for i, cut in enumerate(cuts):

        @pl.when(mine)
        def _():
            pltpu.make_async_copy(own.at[cut], buffer.at[cut], sems.at[i]).start()

        @pl.when(jnp.logical_not(mine))
        def _():
            pltpu.make_async_copy(other.at[cut], buffer.at[cut], sems.at[i]).start()


def fetch_wait(own, buffer, sems, cuts, i):
    pltpu.make_async_copy(own.at[cuts[i]], buffer.at[cuts[i]], sems.at[i]).wait()


def size_of(item):
    return math.prod(item.shape) * jnp.dtype(item.dtype).itemsize


def after_spec(item):
    return V if size_of(item) < 65536 else H


def kernel_call(body, ins, outs, scratch, args, flops, after=(), **more):
    ins, args = list(ins) + [after_spec(item) for item in after], tuple(args) + tuple(after)
    count = len(args)
    inner = body

    def body(*refs):
        inner(*refs[: count - len(after)], *refs[count:])

    held = [a for a, spec in zip(args, ins) if spec is V] + list(outs) + [s for s in scratch if hasattr(s, "dtype") and s.memory_space == pltpu.VMEM]
    need = sum(size_of(item) for item in held) + 8 * MIB
    moved = sum(size_of(a) for a in args) + sum(size_of(o) for o in outs)
    return pl.pallas_call(
        body,
        in_specs=ins,
        out_specs=[V] * len(outs),
        out_shape=outs,
        scratch_shapes=scratch,
        compiler_params=pltpu.CompilerParams(vmem_limit_bytes=need, **more),
        cost_estimate=pl.CostEstimate(flops=flops, bytes_accessed=moved, transcendentals=0),
    )(*args)


def shape(dims, kind):
    return jax.ShapeDtypeStruct(dims, kind)


def qkv_forward(layer, core, x, gain, shift, joined, own, other, after=()):
    rows, width = x.shape
    triple = own.shape[1]
    cuts = column_cuts(triple, 3)

    def body(core_ref, x_ref, gain_ref, shift_ref, joined_ref, own_ref, other_ref, normed_ref, proj_ref, buf, sems):
        mine = core_ref[0] == layer
        fetch_start(mine, own_ref, other_ref, buf, sems, cuts)
        unit, _ = norm_parts(x_ref[...].astype(F32))
        normed_ref[...] = (unit * gain_ref[...] + shift_ref[...]).astype(BF16)
        for i in range(3):
            fetch_wait(own_ref, buf, sems, cuts, i)
            cols = pl.ds(i * width, width)
            proj_ref[:, cols] = (mm(normed_ref[...], buf[:, cols]) + joined_ref[:, cols]).astype(BF16)

    return kernel_call(
        body,
        [S, V, V, V, V, H, H],
        [shape((rows, width), BF16), shape((rows, triple), BF16)],
        [pltpu.VMEM((width, triple), BF16), pltpu.SemaphoreType.DMA((3,))],
        (core, x, gain, shift, joined, own, other),
        5 * 10**9,
        after=after,
    )


def build_bias(base, out_ref, block_ref, grid, corner, crops, length, block_rows):
    lanes = base.shape[1]
    head_patch, patch_head, head_head = corner
    lane = lax.broadcasted_iota(jnp.int32, (block_rows, 256), 1)
    line = lax.broadcasted_iota(jnp.int32, (block_rows, 256), 0)
    first = jnp.where(lane == 0, head_head, head_patch)
    block_ref[...] = jnp.where(lane >= length, LOW, first)
    small = lane[:grid]
    for r in range(grid):
        off = (grid - 1 - r) * grid
        moved = base if off == 0 else pltpu.roll(base, lanes - off, 1)
        moved = moved[:grid, :256]
        value = jnp.where(small == 0, patch_head, jnp.where(small >= length, LOW, moved))
        block_ref[pl.ds(1 + grid * r, grid), :] = value
    if crops == 1:
        return
    out_ref[...] = jnp.full(out_ref.shape, LOW, F32)
    for s in range(crops):
        value = block_ref[pl.ds(0, length), :]
        if s:
            value = pltpu.roll(value, s * length, 1)
        out_ref[pl.ds(s * length, length), :] = value


def pair_bias(pair, corner_ref, bb_ref, bs_ref, big, block, small, sizes):
    crops, len_big, pad_big, slots, len_small, pad_small = sizes
    grid_big, grid_small = math.isqrt(len_big - 1), math.isqrt(len_small - 1)
    for h in range(2):
        head = pair * 2 + h
        build_bias(bb_ref[head], big.at[pl.ds(h * pad_big, pad_big)], big.at[pl.ds(h * pad_big, pad_big)], grid_big, [corner_ref[0, i, head] for i in range(3)], 1, len_big, pad_big)
        build_bias(bs_ref[head], small.at[pl.ds(h * pad_small, pad_small)], block, grid_small, [corner_ref[1, i, head] for i in range(3)], slots, len_small, block.shape[0])


def two_heads(value):
    lane = lax.broadcasted_iota(jnp.int32, (1, 128), 1)
    return jnp.concatenate([jnp.where(lane < 64, value, 0), jnp.where(lane >= 64, value, 0)], axis=0)


def one_line(value):
    count = value.shape[0] // 2
    lane = lax.broadcasted_iota(jnp.int32, (1, 128), 1)
    return jnp.where(lane < 64, value[:count], value[count:])


def attention_probs(scores):
    raised = jnp.exp(scores - jnp.max(scores, axis=-1, keepdims=True))
    return raised * (1.0 / jnp.sum(raised, axis=-1, keepdims=True))


def attention_parts(sizes):
    crops, _, pad_big, _, _, pad_small = sizes
    return [(c * pad_big, pad_big, True) for c in range(crops)] + [(crops * pad_big, pad_small, False)]


def bias_scratch(sizes):
    _, _, pad_big, _, len_small, pad_small = sizes
    return [
        pltpu.VMEM((2 * pad_big, 256), F32),
        pltpu.VMEM((up_to(len_small, 8), 256), F32),
        pltpu.VMEM((2 * pad_small, 256), F32),
    ]


def attention_forward(projected, base_big, base_small, corners, sizes, after=()):
    rows, triple = projected.shape
    width = triple // 3
    pairs = HEADS // 2
    parts = attention_parts(sizes)

    def body(corner_ref, proj_ref, bb_ref, bs_ref, out_ref, big, block, small):
        def step(pair, carry):
            pair_bias(pair, corner_ref, bb_ref, bs_ref, big, block, small, sizes)
            q, k, v = [pl.ds(pl.multiple_of(n * width + pair * 128, 128), 128) for n in range(3)]
            scores = []
            for start, count, is_big in parts:
                part = pl.ds(start, count)
                bias = big if is_big else small
                scores.append(mm_back(two_heads(proj_ref[part, q] * 0.125), proj_ref[part, k]) + bias[:, :count])
            probs = [attention_probs(item).astype(BF16) for item in scores]
            for (start, count, is_big), item in zip(parts, probs):
                part = pl.ds(start, count)
                out_ref[part, q] = one_line(mm(item, proj_ref[part, v])).astype(BF16)
            return carry

        lax.fori_loop(0, pairs, step, 0)

    return kernel_call(
        body,
        [S, V, V, V],
        [shape((rows, width), BF16)],
        bias_scratch(sizes),
        (corners, projected, base_big, base_small),
        10**10,
        after=after,
    )[0]


FF_STEP = 512


def up_forward(layer, core, attended, x, vec, up_bias, own, other, own_up, other_up, after=()):
    rows, width = x.shape
    hidden = own_up.shape[1]
    count = hidden // FF_STEP
    cuts = [(slice(None), slice(None))]
    up_cuts = column_cuts(hidden, count)

    def body(core_ref, att_ref, x_ref, vec_ref, bias_ref, own_ref, other_ref, own_up_ref, other_up_ref, branch_ref, middle_ref, normed_ref, hidden_ref, slope_ref, buf, buf_up, sems, sems_up):
        mine = core_ref[0] == layer
        fetch_start(mine, own_ref, other_ref, buf, sems, cuts)
        fetch_start(mine, own_up_ref, other_up_ref, buf_up, sems_up, up_cuts)
        fetch_wait(own_ref, buf, sems, cuts, 0)
        branch = mm(att_ref[...], buf[...]) + vec_ref[4:5, :]
        branch_ref[...] = branch.astype(BF16)
        middle = x_ref[...].astype(F32) + vec_ref[5:6, :] * branch
        middle_ref[...] = middle
        unit, _ = norm_parts(middle)
        normed_ref[...] = (unit * vec_ref[6:7, :] + vec_ref[7:8, :]).astype(BF16)
        for i in range(count):
            fetch_wait(own_up_ref, buf_up, sems_up, up_cuts, i)

        def pre_of(i):
            cols = pl.ds(i * FF_STEP, FF_STEP)
            return mm(normed_ref[...], buf_up[:, cols]) + bias_ref[:, cols]

        pre = pre_of(0)
        for i in range(count):
            following = pre_of(i + 1) if i + 1 < count else None
            value, slope = gelu_parts(pre)
            cols = pl.ds(i * FF_STEP, FF_STEP)
            hidden_ref[:, cols] = value.astype(BF16)
            slope_ref[:, cols] = slope.astype(BF16)
            pre = following

    return kernel_call(
        body,
        [S, V, V, V, V, H, H, H, H],
        [
            shape((rows, width), BF16),
            shape((rows, width), F32),
            shape((rows, width), BF16),
            shape((rows, hidden), BF16),
            shape((rows, hidden), BF16),
        ],
        [
            pltpu.VMEM((width, width), BF16),
            pltpu.VMEM((width, hidden), BF16),
            pltpu.SemaphoreType.DMA((1,)),
            pltpu.SemaphoreType.DMA((count,)),
        ],
        (core, attended, x, vec, up_bias, own, other, own_up, other_up),
        13 * 10**9,
        after=after,
    )


def down_forward(layer, core, hidden, middle, keep, vec, own, other, upstream=None, after=()):
    rows, width = middle.shape
    depth = hidden.shape[1]
    cuts = row_cuts(depth, 2)
    half = depth // 2
    extra = () if upstream is None else (upstream,)

    def body(core_ref, hidden_ref, middle_ref, keep_ref, vec_ref, *rest):
        own_ref, other_ref, y_ref, mlp_ref, buf, sems = rest[len(extra) :]
        fetch_start(core_ref[0] == layer, own_ref, other_ref, buf, sems, cuts)
        total = vec_ref[8:9, :]
        for i in range(2):
            fetch_wait(own_ref, buf, sems, cuts, i)
            part = pl.ds(i * half, half)
            total = total + mm(hidden_ref[:, part], buf[part, :])
        if extra:
            mlp_ref[...] = jnp.sum(rest[0][...].astype(F32) * keep_ref[...] * total, axis=0, keepdims=True)
        else:
            mlp_ref[...] = total.astype(BF16)
        y_ref[...] = ((middle_ref[...] + vec_ref[9:10, :] * total) * keep_ref[...]).astype(BF16)

    return kernel_call(
        body,
        [S, V, V, V, V] + [V] * len(extra) + [H, H],
        [shape((rows, width), BF16), shape((1, width), F32) if extra else shape((rows, width), BF16)],
        [pltpu.VMEM((depth, width), BF16), pltpu.SemaphoreType.DMA((2,))],
        (core, hidden, middle, keep, vec) + extra + (own, other),
        6 * 10**9,
        after=after,
    )


def mlp_backward(layer, core, upstream, keep, vec, slope, middle, branch, mlp, down, up, proj, after=()):
    rows, width = middle.shape
    depth = slope.shape[1]
    count = depth // FF_STEP
    half_cols, half_width = depth // 2, width // 2
    extra = () if mlp is None else (mlp,)
    down_cuts, up_cuts = row_cuts(depth, count), column_cuts(depth, count)
    cuts = [(slice(None), slice(None))]

    def body(core_ref, g_ref, keep_ref, vec_ref, slope_ref, middle_ref, branch_ref, *rest):
        if mlp is not None:
            mlp_ref, rest = rest[0], rest[1:]
        inner(core_ref, g_ref, keep_ref, vec_ref, slope_ref, middle_ref, branch_ref, *rest)
        if mlp is not None:
            vecs_ref = rest[11]
            vecs_ref[5:6, :] = jnp.sum(g_ref[...].astype(F32) * keep_ref[...] * mlp_ref[...].astype(F32), axis=0, keepdims=True)

    def inner(core_ref, g_ref, keep_ref, vec_ref, slope_ref, middle_ref, branch_ref, od, td, ou, tu, op, tp, gm_ref, gp_ref, gb_ref, ga_ref, gmid_ref, vecs_ref, ups_ref, low, bd, bu, bp, sd, su, sp):
        me = core_ref[0]
        mine = me == layer
        fetch_start(mine, od, td, bd, sd, down_cuts)
        fetch_start(mine, ou, tu, bu, su, up_cuts)
        fetch_start(mine, op, tp, bp, sp, cuts)
        gm = (vec_ref[9:10, :] * (g_ref[...].astype(F32) * keep_ref[...])).astype(BF16)
        low[...] = gm
        gm_ref[me] = gm[:, :half_width]
        gm_ref[1 - me] = gm[:, half_width:]
        vecs_ref[...] = jnp.zeros_like(vecs_ref)
        vecs_ref[4:5, :] = jnp.sum(gm.astype(F32), axis=0, keepdims=True)
        for i in range(count):
            fetch_wait(od, bd, sd, down_cuts, i)
        for i in range(count):
            cols = pl.ds(i * FF_STEP, FF_STEP)
            gp = (mm_back(low[...], bd[cols, :]) * slope_ref[:, cols].astype(F32)).astype(BF16)
            slot = me if 2 * i < count else 1 - me
            gp_ref[slot, :, pl.ds((i * FF_STEP) % half_cols, FF_STEP)] = gp
            ups_ref[:, cols] = jnp.sum(gp.astype(F32), axis=0, keepdims=True)
        for i in range(count):
            fetch_wait(ou, bu, su, up_cuts, i)
        back = mm_back(gp_ref[me], bu[:, :half_cols]) + mm_back(gp_ref[1 - me], bu[:, half_cols:])
        going, gain, shift = norm_back(back, middle_ref[...], vec_ref[6:7, :])
        gmid = g_ref[...].astype(F32) * keep_ref[...] + going
        gmid_ref[...] = gmid
        gb = (vec_ref[5:6, :] * gmid).astype(BF16)
        low[...] = gb
        gb_ref[me] = gb[:, :half_width]
        gb_ref[1 - me] = gb[:, half_width:]
        vecs_ref[0:1, :] = gain
        vecs_ref[1:2, :] = shift
        vecs_ref[2:3, :] = jnp.sum(gmid * branch_ref[...].astype(F32), axis=0, keepdims=True)
        vecs_ref[3:4, :] = jnp.sum(gb.astype(F32), axis=0, keepdims=True)
        fetch_wait(op, bp, sp, cuts, 0)
        ga_ref[...] = mm_back(low[...], bp[...]).astype(BF16)

    return kernel_call(
        body,
        [S, V, V, V, V, V, V] + [V] * len(extra) + [H] * 6,
        [
            shape((2, rows, half_width), BF16),
            shape((2, rows, half_cols), BF16),
            shape((2, rows, half_width), BF16),
            shape((rows, width), BF16),
            shape((rows, width), F32),
            shape((8, width), F32),
            shape((1, depth), F32),
        ],
        [
            pltpu.VMEM((rows, width), BF16),
            pltpu.VMEM((depth, width), BF16),
            pltpu.VMEM((width, depth), BF16),
            pltpu.VMEM((width, width), BF16),
            pltpu.SemaphoreType.DMA((count,)),
            pltpu.SemaphoreType.DMA((count,)),
            pltpu.SemaphoreType.DMA((1,)),
        ],
        (core, upstream, keep, vec, slope, middle, branch) + extra + down + up + proj,
        14 * 10**9,
        after=after,
    )


def attention_backward(core, projected, upstream, base_big, base_small, corners, sizes, after=()):
    rows, triple = projected.shape
    width = triple // 3
    pairs = HEADS // 2
    crops, len_big, pad_big, slots, len_small, pad_small = sizes
    grid_big, grid_small = math.isqrt(len_big - 1), math.isqrt(len_small - 1)
    half = 3 * pairs // 2

    parts = attention_parts(sizes)

    def body(core_ref, corner_ref, proj_ref, g_ref, bb_ref, bs_ref, gproj_ref, tb_ref, ts_ref, sums_ref, big, block, small, dbig, dsmall, dblock):
        dbig[...] = jnp.zeros_like(dbig)
        dsmall[...] = jnp.zeros_like(dsmall)
        dblock[...] = jnp.zeros_like(dblock)
        tb_ref[...] = jnp.zeros_like(tb_ref)
        ts_ref[...] = jnp.zeros_like(ts_ref)

        def step(pair, carry):
            pair_bias(pair, corner_ref, bb_ref, bs_ref, big, block, small, sizes)

            def place_for(which):
                place = which * pairs + pair + half * core_ref[0]
                return jnp.where(place >= 2 * half, place - 2 * half, place)

            q, k, v = [pl.ds(pl.multiple_of(n * width + pair * 128, 128), 128) for n in range(3)]
            places = [place_for(which) for which in range(3)]
            scores, gprs = [], []
            for start, count, is_big in parts:
                part = pl.ds(start, count)
                bias = big if is_big else small
                scores.append(mm_back(two_heads(proj_ref[part, q] * 0.125), proj_ref[part, k]) + bias[:, :count])
                gprs.append(mm_back(two_heads(g_ref[part, q]), proj_ref[part, v]))
            probs = [attention_probs(item) for item in scores]
            gss = [(p * (gpr - jnp.sum(p * gpr, axis=-1, keepdims=True))).astype(BF16) for p, gpr in zip(probs, gprs)]
            for n, ((start, count, is_big), p, gs) in enumerate(zip(parts, probs, gss)):
                part = pl.ds(start, count)
                dref = dbig if is_big else dsmall
                if n == 0 or not is_big:
                    dref[:, :count] = gs.astype(F32)
                else:
                    dref[:, :count] += gs.astype(F32)
                gproj_ref[places[0], part, :] = (one_line(mm(gs, proj_ref[part, k])) * 0.125).astype(BF16)
                gproj_ref[places[1], part, :] = mm_outer(gs, two_heads(proj_ref[part, q] * 0.125)).astype(BF16)
                gproj_ref[places[2], part, :] = mm_outer(p.astype(BF16), two_heads(g_ref[part, q])).astype(BF16)


            for h in range(2):
                hbig, hsmall = dbig.at[pl.ds(h * pad_big, pad_big)], dsmall.at[pl.ds(h * pad_small, pad_small)]

                def fold(dref, grid, length, out_ref):
                    lanes = out_ref.shape[2]
                    wide = lax.broadcasted_iota(jnp.int32, (grid, 256), 1)
                    inside = (wide > 0) & (wide < length)
                    total = jnp.zeros((grid, lanes), F32)
                    for r in range(grid):
                        value = jnp.where(inside, dref[pl.ds(1 + grid * r, grid), :], 0)
                        if lanes > 256:
                            value = jnp.concatenate([value, jnp.zeros((grid, lanes - 256), F32)], axis=1)
                        off = (grid - 1 - r) * grid
                        total = total + (value if off == 0 else pltpu.roll(value, off, 1))
                    out_ref[pair * 2 + h, :grid, :] = total
                    line = lax.broadcasted_iota(jnp.int32, (length, 256), 0)
                    spot = lax.broadcasted_iota(jnp.int32, (length, 256), 1)
                    value = jnp.where(spot < length, dref[pl.ds(0, length), :], 0)
                    out_ref[pair * 2 + h, grid : grid + 1, :256] = value[0:1, :]
                    out_ref[pair * 2 + h, grid + 1 : grid + 2, :256] = jnp.sum(jnp.where(line > 0, value, 0), axis=0, keepdims=True)

                fold(hbig, grid_big, len_big, tb_ref)
                total = hsmall[pl.ds(0, len_small), :]
                for s in range(1, slots):
                    total = total + pltpu.roll(hsmall[pl.ds(s * len_small, len_small), :], 256 - s * len_small, 1)
                dblock[pl.ds(0, len_small), :] = total
                fold(dblock, grid_small, len_small, ts_ref)
            for n, which in ((0, 0), (1, 2)):
                sums_ref[n : n + 1, q] = jnp.sum(gproj_ref[places[which]].astype(F32), axis=0, keepdims=True)
            return carry

        lax.fori_loop(0, pairs, step, 0)

    return kernel_call(
        body,
        [S, S, V, V, V, V],
        [
            shape((2 * half, rows, 128), BF16),
            shape((HEADS, 16, 512), F32),
            shape((HEADS, 8, 256), F32),
            shape((2, width), F32),
        ],
        bias_scratch(sizes)
        + [
            pltpu.VMEM((2 * pad_big, 256), F32),
            pltpu.VMEM((2 * pad_small, 256), F32),
            pltpu.VMEM((up_to(len_small, 8), 256), F32),
        ],
        (core, corners, projected, upstream, base_big, base_small),
        15 * 10**9,
        after=after,
    )


def qkv_backward(layer, core, gproj, x, gmid, gain, own, other, after=()):
    rows, width = x.shape
    blocks = gproj.shape[0]
    triple = blocks * 128
    cuts = column_cuts(triple, 3)
    group = blocks // 3

    def body(core_ref, gproj_ref, x_ref, gmid_ref, gain_ref, own_ref, other_ref, gx_ref, vecs_ref, buf, acc, sems):
        me = core_ref[0]
        fetch_start(me == layer, own_ref, other_ref, buf, sems, cuts)
        for i in range(3):
            fetch_wait(own_ref, buf, sems, cuts, i)
            places = [n + (blocks // 2) * me for n in range(i * group, (i + 1) * group)]
            places = [jnp.where(place >= blocks, place - blocks, place) for place in places]
            joined = jnp.concatenate([gproj_ref[place] for place in places], axis=1)
            more = mm_back(joined, buf[:, pl.ds(i * width, width)])
            if i == 0:
                acc[...] = more
            else:
                acc[...] += more
        going, gain_sum, shift_sum = norm_back(acc[...], x_ref[...].astype(F32), gain_ref[...])
        gx_ref[...] = (gmid_ref[...] + going).astype(BF16)
        vecs_ref[0:1, :] = gain_sum
        vecs_ref[1:2, :] = shift_sum

    return kernel_call(
        body,
        [S, V, V, V, V, H, H],
        [shape((rows, width), BF16), shape((2, width), F32)],
        [
            pltpu.VMEM((width, triple), BF16),
            pltpu.VMEM((rows, width), F32),
            pltpu.SemaphoreType.DMA((3,)),
        ],
        (core, gproj, x, gmid, gain, own, other),
        5 * 10**9,
        after=after,
    )


def place_of(relative, order):
    place = 0
    for bit in order:
        place = place * 2 + ((relative >> bit) & 1)
    return place


def weight_grad(where, orders, parts, flops, after=()):
    devices = 1 << len(orders[0])
    pieces = len(orders)
    rows = parts[0][0].shape[0]
    tiles = [part[2].shape[0] if part[2].ndim == 3 else part[2].shape[1] // 128 for part in parts]
    counts = [count // pieces for count in tiles]
    subs = sum(counts)
    block = parts[0][0].shape[1] // devices
    half = devices // 2

    def body(where_ref, *refs):
        ins, refs = refs[: 4 * len(parts)], refs[4 * len(parts) + len(after) :]
        outs, refs = refs[: 2 * pieces], refs[2 * pieces :]
        held, refs = refs[:pieces], refs[pieces:]
        sems = refs[0]
        me = where_ref[1]
        places = [[place_of(j ^ me, order) for j in range(devices)] for order in orders]

        def columns(ref, low, high):
            if len(ref.shape) == 3:
                return jnp.concatenate([ref[t] for t in range(low, high)], axis=1)
            return ref[:, low * 128 : high * 128]

        def copies(p):
            return [
                pltpu.make_async_copy(held[p].at[pl.ds(0, half)], outs[2 * p], sems.at[2 * p]),
                pltpu.make_async_copy(held[p].at[pl.ds(half, half)], outs[2 * p + 1], sems.at[2 * p + 1]),
            ]

        sub = 0
        for n, part in enumerate(parts):
            xo, xt, go, gt = ins[4 * n : 4 * n + 4]
            width = xo.shape[1]

            def put(value, line, tile, n=n, sub=sub):
                p, at = tile // counts[n], tile % counts[n]
                held[p][places[p][line], sub + at] = value

            if part[4]:
                right = jnp.concatenate([columns(go, 0, tiles[n]), columns(gt, 0, tiles[n])], axis=0)
                step = 768
                for start in range(0, width, step):
                    cut = pl.ds(start, step)
                    left = jnp.concatenate([xo[:, cut], xt[:, cut]], axis=0)
                    value = mm_outer(right, left).astype(BF16).T
                    for j in range(step // block):
                        for t in range(tiles[n]):
                            put(value[j * block : (j + 1) * block, t * 128 : (t + 1) * 128], start // block + j, t)
                for p in range(pieces):
                    if n + 1 == len(parts):
                        for copy in copies(p):
                            copy.start()
            else:
                left = jnp.concatenate([xo[...], xt[...]], axis=0).T
                done = 0
                for low in range(0, tiles[n], 4):
                    high = min(low + 4, tiles[n])
                    value = mm(left, jnp.concatenate([columns(go, low, high), columns(gt, low, high)], axis=0))
                    for j in range(devices):
                        for t in range(low, high):
                            put(value[j * block : (j + 1) * block, (t - low) * 128 : (t - low + 1) * 128].astype(BF16), j, t)
                    while n + 1 == len(parts) and done < pieces and (done + 1) * counts[n] <= high:
                        for copy in copies(done):
                            copy.start()
                        done += 1
            sub += counts[n]
        for p in range(pieces):
            for copy in copies(p):
                copy.wait()

    out = shape((half, subs, block, 128), BF16)
    args = [item for part in parts for item in part[:4]]
    return pl.pallas_call(
        body,
        in_specs=[S] + [V] * len(args) + [after_spec(item) for item in after],
        out_specs=[H] * (2 * pieces),
        out_shape=[out] * (2 * pieces),
        scratch_shapes=[pltpu.VMEM((devices, subs, block, 128), BF16)] * pieces
        + [pltpu.SemaphoreType.DMA((2 * pieces,))],
        compiler_params=pltpu.CompilerParams(vmem_limit_bytes=sum(size_of(a) for a in args) + 16 * MIB),
        cost_estimate=pl.CostEstimate(flops=flops, bytes_accessed=sum(size_of(a) for a in args), transcendentals=0),
    )(where, *args, *after)


TALL, WIDE, LAST = 11 * 10**9, 9 * 10**9, 10 * 10**9


def add_stage(items, after):
    args, outs, plan = [], [], []
    for item in items:
        kept, came, how = item
        if how == "last":
            plan.append((how, len(args), len(kept), len(outs)))
            outs.append(shape((len(kept),) + kept[0].shape[1:], F32))
            args += list(kept) + list(came)
        else:
            plan.append((how, len(args), 1, len(outs)))
            if how == "halves":
                half = shape((kept.shape[0] // 2,) + kept.shape[1:], BF16)
                outs += [half, half]
            else:
                outs.append(shape(kept.shape, F32))
            args += [kept, came]

    def body(*refs):
        ins, results = refs[: len(args)], refs[len(args) :]
        for how, at, count, to in plan:
            if how == "last":
                for n in range(count):
                    results[to][n] = ins[at + n][0].astype(F32) + ins[at + count + n][0].astype(F32)
            elif how == "whole":
                results[to][...] = ins[at][...] + ins[at + 1][...]
            else:
                half = outs[to].shape[0]
                for n in range(2):
                    cut = pl.ds(n * half, half)
                    results[to + n][...] = (ins[at][cut].astype(F32) + ins[at + 1][cut].astype(F32)).astype(BF16)
        results[-1][...] = jnp.zeros((8, 128), F32)

    made = kernel_call(body, [V] * len(args), outs + [shape((8, 128), F32)], [], tuple(args), 10**9, after=after)
    results = []
    for how, _, _, to in plan:
        results.append((made[to], made[to + 1]) if how == "halves" else made[to])
    return results, made[-1]


class Scatter:
    def __init__(self, made, orders):
        self.keeps, self.sends, self.orders = list(made[0::2]), list(made[1::2]), orders
        self.step, self.result = 0, None
        self.launch()

    def launch(self):
        self.came = [across(send, order[self.step]) for send, order in zip(self.sends, self.orders)]

    def items(self):
        if self.step + 1 == len(self.orders[0]):
            return [(self.keeps, self.came, "last")]
        return [(keep, came, "halves") for keep, came in zip(self.keeps, self.came)]

    def take(self, results):
        self.step += 1
        if self.step == len(self.orders[0]):
            self.result = results[0]
            return
        self.keeps, self.sends = [r[0] for r in results], [r[1] for r in results]
        self.launch()


class Total:
    def __init__(self, value, bits):
        self.value, self.bits, self.step, self.result = value, bits, 0, None
        self.came = swap(value)

    def items(self):
        return [(self.value, self.came, "whole")]

    def take(self, results):
        self.value = results[0]
        if self.step == self.bits:
            self.result = self.value
            return
        self.came = across(self.value, self.step)
        self.step += 1


def advance(groups, after):
    groups = [group for group in groups if group.result is None]
    if not groups:
        return after[0]
    items = [group.items() for group in groups]
    results, token = add_stage([item for part in items for item in part], after)
    for group, part in zip(groups, items):
        group.take(results[: len(part)])
        results = results[len(part) :]
    return token


def gather_vectors(parts, after):
    width = parts[0][0].shape[1]
    args = tuple(item for part in parts for item in part)
    count = len(parts[0])

    def body(*refs):
        out = refs[-1]
        out[...] = jnp.zeros_like(out)
        for layer in range(2):
            vecs1, qv, vecs2, scale, ups = refs[layer * count : layer * count + count]
            out[layer, 0:2] = vecs1[...]
            out[layer, 2:4] = qv[...]
            out[layer, 4:5] = vecs2[3:4]
            out[layer, 5:6] = vecs2[2:3]
            out[layer, 6:8] = vecs2[0:2]
            out[layer, 8:9] = vecs2[4:5]
            out[layer, 9:10] = scale[...]
            for n in range(ups.shape[1] // width):
                out[layer, 10 + n : 11 + n] = ups[:, n * width : (n + 1) * width]

    return kernel_call(body, [V] * len(args), [shape((2, 16, width), F32)], [], args, 10**9, after=after)[0]


def arrange_rows(core, own, came, sizes, after):
    crops, len_big, pad_big, slots, len_small, pad_small = sizes
    width = own[0].shape[1]
    split = crops * pad_big

    def body(core_ref, own0, own1, came0, came1, out_big, out_small):
        me = core_ref[0]

        def put(place, ref):
            for c in range(crops):
                out_big[0, place, c] = ref[pl.ds(c * pad_big, len_big), :]
            rest = ref[pl.ds(split, pad_small), :].astype(F32)
            for s in range(slots):
                out_small[0, place, s] = rest[s * len_small : (s + 1) * len_small].astype(BF16)

        @pl.when(me == 0)
        def _():
            put(0, own0)
            put(1, came0)

        @pl.when(me == 1)
        def _():
            put(1, own1)
            put(0, came1)

    return kernel_call(
        body,
        [S, V, V, V, V],
        [shape((1, 2, crops, len_big, width), BF16), shape((1, 2, slots, len_small, width), BF16)],
        [],
        (core, *own, *came),
        4 * 10**9,
        after=after,
    )


def arrange_grads(core, sums, came, block, width):
    pieces = sums[0][0].shape[0]
    tall_rows = sums[0][0].shape[2]
    subs = sums[0][1].shape[1]
    args = tuple(item for part in (*sums, *came) for item in part)

    def body(core_ref, *refs):
        down, up, proj, qkv = refs[12:]

        def put(half, tall, wide, last):
            for p in range(pieces):
                down[0, :, pl.ds((half * pieces + p) * 128, 128)] = tall[p, 0]
                proj[0, :, pl.ds((half * pieces + p) * 128, 128)] = last[p, 0]
                for t in range(subs):
                    up[0, :, pl.ds(((half * pieces + p) * subs + t) * 128, 128)] = wide[p, t]
                for t in range(subs - 1):
                    qkv[0, :, pl.ds(((half * pieces + p) * (subs - 1) + t) * 128, 128)] = last[p, 1 + t]

        @pl.when(core_ref[0] == 0)
        def _():
            put(0, *refs[0:3])
            put(1, *refs[6:9])

        @pl.when(core_ref[0] == 1)
        def _():
            put(1, *refs[3:6])
            put(0, *refs[9:12])

    return kernel_call(
        body,
        [S] + [V] * len(args),
        [
            shape((1, tall_rows, width), F32),
            shape((1, block, 2 * pieces * subs * 128), F32),
            shape((1, block, width), F32),
            shape((1, block, 2 * pieces * (subs - 1) * 128), F32),
        ],
        [],
        (core, *args),
        2 * 10**9,
    )


def swap(value):
    return lax.ppermute(value, "section", [(0, 1), (1, 0)])


def across(value, bit):
    return lax.ppermute(value, "dp", [(i, i ^ (1 << bit)) for i in range(lax.axis_size("dp"))])


def hand_over(value, layer):
    return lax.ppermute(value, "section", [(1 - layer, layer)])


HEAD_ROWS = 16


def table_lines(table, grid):
    layers, _, heads = table.shape
    side = 2 * grid - 1
    square = table[:, : side * side].reshape(layers, side, side, heads)[:, ::-1, ::-1]
    lines = jnp.transpose(square, (1, 0, 3, 2))
    lines = jnp.pad(lines, ((0, 0), (0, 0), (0, HEAD_ROWS - heads), (0, 128 - side)))
    return lines.reshape(side, layers * HEAD_ROWS, 128)


def table_bases(big, small, grids):
    heads = big.shape[1]

    def body(big_ref, small_ref, out_big, out_small):
        lane = lax.broadcasted_iota(jnp.int32, (heads, 128), 1)
        for ref, out, grid in ((big_ref, out_big, grids[0]), (small_ref, out_small, grids[1])):
            for r in range(grid):
                tiles = [jnp.zeros((heads, 128), F32) for _ in range(out.shape[2] // 128)]
                for d in range(2 * grid - 1):
                    low = 1 + d * grid
                    moved = pltpu.roll(ref[d], (low - (grid - 1 - r)) % 128, 1)
                    tile, at = low // 128, low % 128
                    tiles[tile] = jnp.where((lane >= at) & (lane < at + grid), moved, tiles[tile])
                    if at + grid > 128:
                        tiles[tile + 1] = jnp.where(lane < at + grid - 128, moved, tiles[tile + 1])
                out[r] = jnp.concatenate(tiles, axis=1)

    return kernel_call(
        body,
        [V, V],
        [shape((grids[0], heads, 512), F32), shape((grids[1], heads, 256), F32)],
        [],
        (big, small),
        3 * 10**9,
    )


def table_folds(big, small, grids, lengths, after):
    heads = big.shape[1]
    counts = [-(-(2 * grid - 1) // 4) for grid in grids]

    def body(big_ref, small_ref, out):
        lane = lax.broadcasted_iota(jnp.int32, (heads, 128), 1)
        base = 0
        ends = []
        for ref, grid, count, length in zip((big_ref, small_ref), grids, counts, lengths):
            for line in range(count):
                total = jnp.zeros((heads, 128), F32)
                for d in range(4 * line, min(4 * line + 4, 2 * grid - 1)):
                    low = 1 + d * grid
                    tile, at = low // 128, low % 128
                    for r in range(grid):
                        to = 32 * (d % 4) + grid - 1 - r
                        moved = ref[r, :, tile * 128 : tile * 128 + 128]
                        if at + grid > 128:
                            moved = jnp.where(lane >= at, moved, ref[r, :, tile * 128 + 128 : tile * 128 + 256])
                        shift = (to - at) % 128
                        moved = pltpu.roll(moved, shift, 1) if shift else moved
                        total = total + jnp.where((lane >= to) & (lane < to + grid), moved, 0)
                out[base + line] = total
            base += count
            first, second = ref[grid], ref[grid + 1]
            wide = lax.broadcasted_iota(jnp.int32, first.shape, 1)
            ends.append(jnp.sum(jnp.where((wide > 0) & (wide < length), first, 0), axis=1, keepdims=True))
            ends.append(second[:, 0:1])
            ends.append(first[:, 0:1])
        last = out[base - 1]
        for n, end in enumerate(ends):
            last = jnp.where(lane == 96 + n, end, last)
        out[base - 1] = last

    return kernel_call(body, [V, V], [shape((sum(counts), heads, 128), F32)], [], (big, small), 3 * 10**9, after=after)[0]


def table_grads(folded, grids, heads):
    grads, base = [], 0
    for n, grid in enumerate(grids):
        side = 2 * grid - 1
        count = -(-side // 4)
        lines = folded[base : base + count, :heads].reshape(count, heads, 4, 32)
        lines = jnp.transpose(lines, (0, 2, 3, 1)).reshape(count * 4, 32, heads)[:side, :side]
        ends = jnp.transpose(folded[-1, :heads, 96 + 3 * n : 99 + 3 * n])
        grads.append(jnp.concatenate([lines[::-1, ::-1].reshape(side * side, heads), ends]))
        base += count
    return grads


def body(input_big, input_small, small_counts, cotangent_big, cotangent_small, norm1_gain, norm1_bias, qkv_weight, query_bias, value_bias, table_big, table_small, proj_weight, proj_bias, attn_scale, norm2_gain, norm2_bias, up_weight, up_bias, down_weight, down_bias, mlp_scale):
    micro, crops, len_big, width = input_big.shape
    slots_all, len_small = input_small.shape[1], input_small.shape[2]
    slots = slots_all // small_counts.shape[1]
    grid_big, grid_small = math.isqrt(len_big - 1), math.isqrt(len_small - 1)
    pad_big = up_to(len_big, 16)
    real_small = slots_all * len_small
    pad_small = up_to(real_small, 16)
    split = crops * pad_big
    rows = split + pad_small
    sizes = (crops, len_big, pad_big, slots_all, len_small, pad_small)
    devices = lax.axis_size("dp")
    bits = devices.bit_length() - 1
    core = lax.axis_index("section")
    place = lax.axis_index("dp")
    where = jnp.stack([core, place]).astype(jnp.int32)
    first = core == 0

    def join(big, small):
        big = lax.dynamic_index_in_dim(big, core, 0, keepdims=False)
        small = lax.dynamic_index_in_dim(small, core, 0, keepdims=False)
        big = jnp.pad(big, ((0, 0), (0, pad_big - len_big), (0, 0))).reshape(split, width)
        small = jnp.pad(small.reshape(real_small, width), ((0, pad_small - real_small), (0, 0)))
        return jnp.concatenate([big, small])

    x0 = join(input_big, input_small)
    cotangent = join(cotangent_big, cotangent_small)
    counts = lax.dynamic_index_in_dim(small_counts, core, 0, keepdims=False)
    line = jnp.arange(rows, dtype=jnp.int32)
    spot = line - split
    limit = jnp.repeat(counts, slots * len_small, total_repeat_length=real_small)
    small_keep = (jnp.arange(real_small, dtype=jnp.int32) // len_small % slots < limit).astype(F32)
    keep = jnp.where(line < split, (line % pad_big < len_big).astype(F32), jnp.pad(small_keep, (split, pad_small - real_small)))
    keep = keep[:, None]

    vec_own = jnp.concatenate(
        [norm1_gain, norm1_bias, query_bias, value_bias, proj_bias, attn_scale, norm2_gain, norm2_bias, down_bias, mlp_scale, up_bias.reshape(-1, width)]
    )
    tables_own = jnp.concatenate([table_big[0], table_small[0]])
    vec_other, tables_other = swap(vec_own), swap(tables_own)
    qkv = (qkv_weight[0], swap(qkv_weight[0]))
    proj = (proj_weight[0], swap(proj_weight[0]))
    up = (up_weight[0], swap(up_weight[0]))
    down = (down_weight[0], swap(down_weight[0]))

    grids, lengths = (grid_big, grid_small), (len_big, len_small)
    entries_big = table_big.shape[1]
    both = jnp.stack([jnp.where(first, tables_own, tables_other), jnp.where(first, tables_other, tables_own)])
    both_big, both_small = both[:, :entries_big], both[:, entries_big:]
    base_big, base_small = table_bases(table_lines(both_big, grid_big), table_lines(both_small, grid_small), grids)

    def by_head(base, rows):
        base = base.reshape(base.shape[0], 2, HEAD_ROWS, -1)[:, :, :HEADS]
        return jnp.pad(jnp.transpose(base, (1, 2, 0, 3)), ((0, 0), (0, 0), (0, rows - base.shape[0]), (0, 0)))

    base_big, base_small = by_head(base_big, 16), by_head(base_small, 8)
    layers = []
    for layer in range(2):
        vec = jnp.where(core == layer, vec_own, vec_other)
        ups = vec[10:].reshape(1, -1)
        joined = jnp.concatenate([vec[2:3], jnp.zeros_like(vec[2:3]), vec[3:4]], axis=1)
        corners = jnp.stack([both_big[layer, -3:], both_small[layer, -3:]])
        layers.append((vec, ups, joined, corners, base_big[layer], base_small[layer]))

    saved = []
    x = x0
    for layer in range(2):
        vec, ups, joined, corners, big, small = layers[layer]
        normed, projected = qkv_forward(layer, where, x, vec[0:1], vec[1:2], joined, *qkv)
        attended = attention_forward(projected, big, small, corners, sizes)
        branch, middle, normed2, hidden, slope = up_forward(layer, where, attended, x, vec, ups, *proj, *up)
        saved.append((x, normed, projected, attended, branch, middle, normed2, hidden, slope))
        if layer == 0:
            x, mlp0 = down_forward(layer, where, hidden, middle, keep, vec, *down)

    orders = [list(range(bits)), [1, 0] + list(range(2, bits)), [2, 0, 1] + list(range(3, bits))]

    def mlp_part(layer, g, mlp, after=()):
        vec = layers[layer][0]
        x, normed, projected, attended, branch, middle, normed2, hidden, slope = saved[layer]
        return mlp_backward(layer, where, g, keep, vec, slope, middle, branch, mlp, down, up, proj, after=after)

    def attention_part(layer, ga, after):
        _, _, _, corners, big, small = layers[layer]
        return attention_backward(where, saved[layer][2], ga, big, small, corners, sizes, after=after)

    def qkv_part(layer, gproj, gmid, after):
        return qkv_backward(layer, where, gproj, saved[layer][0], gmid, layers[layer][0][0:1], *qkv, after=after)

    def tall_grad(layer, others, gm, gm_other, after):
        part = (saved[layer][7], others[0], gm[0], gm_other, True)
        return weight_grad(where, orders, [part], TALL, after)

    def wide_grad(layer, others, gp, gp_other, after):
        part = (saved[layer][6], others[1], gp[0], gp_other, False)
        return weight_grad(where, orders, [part], WIDE, after)

    def last_grad(layer, others, gb, gb_other, gproj, gproj_other, after):
        parts = [
            (saved[layer][3], others[2], gb[0], gb_other, False),
            (saved[layer][1], others[3], gproj[: gproj.shape[0] // 2], gproj_other, False),
        ]
        return weight_grad(where, orders, parts, LAST, after)

    others = [[swap(saved[layer][n]) for n in (7, 6, 3, 1)] for layer in range(2)]
    came_y0 = hand_over(saved[1][0], 0)

    gm, gp, gb, ga, gmid, vecs2_1, ups_1 = mlp_part(1, cotangent, None)
    gm_other, gp_other, gb_other = swap(gm[1]), swap(gp[1]), swap(gb[1])
    made = tall_grad(1, others[1], gm, gm_other, (ups_1,))
    tall1 = Scatter(made, orders)
    made = wide_grad(1, others[1], gp, gp_other, made[:1])
    wide1 = Scatter(made, orders)
    gproj, fold_big1, fold_small1, qv_1 = attention_part(1, ga, made[:1])
    gproj_other = swap(gproj[gproj.shape[0] // 2 :])
    token = advance([tall1, wide1], (qv_1,))
    gx1, vecs1_1 = qkv_part(1, gproj, gmid, (token,))
    came_gx1 = hand_over(gx1, 1)
    made = last_grad(1, others[1], gb, gb_other, gproj, gproj_other, (vecs1_1,))
    last1 = Scatter(made, orders)
    token = advance([tall1, wide1], made[:1])

    gm, gp, gb, ga, gmid, vecs2_0, ups_0 = mlp_part(0, gx1, mlp0, (token,))
    gm_other, gp_other, gb_other = swap(gm[1]), swap(gp[1]), swap(gb[1])
    token = advance([tall1, wide1, last1], (ups_0,))
    made = tall_grad(0, others[0], gm, gm_other, (token,))
    tall0 = Scatter(made, orders)
    token = advance([tall1, wide1, last1], made[:1])
    made = wide_grad(0, others[0], gp, gp_other, (token,))
    wide0 = Scatter(made, orders)
    token = advance([last1], made[:1])
    gproj, fold_big0, fold_small0, qv_0 = attention_part(0, ga, (token,))
    gproj_other = swap(gproj[gproj.shape[0] // 2 :])
    token = advance([last1, tall0, wide0], (qv_0,))
    y1, scale_1 = down_forward(1, where, saved[1][7], saved[1][5], keep, layers[1][0], *down, upstream=cotangent, after=(token,))
    came_y1 = hand_over(y1, 1)
    made = last_grad(0, others[0], gb, gb_other, gproj, gproj_other, (scale_1,))
    last0 = Scatter(made, orders)
    token = advance([tall0, wide0], made[:1])
    gx0, vecs1_0 = qkv_part(0, gproj, gmid, (token,))
    came_gx0 = hand_over(gx0, 0)

    def by_line(zero, one):
        both = jnp.pad(jnp.stack([zero, one]), ((0, 0), (0, HEAD_ROWS - HEADS), (0, 0), (0, 0)))
        return jnp.transpose(both, (2, 0, 1, 3)).reshape(zero.shape[1], 2 * HEAD_ROWS, -1)

    folded = table_folds(by_line(fold_big0, fold_big1), by_line(fold_small0, fold_small1), grids, lengths, (vecs1_0,))
    tables = Total(folded, bits)
    vectors = gather_vectors(
        [(vecs1_0, qv_0, vecs2_0, vecs2_0[5:6], ups_0), (vecs1_1, qv_1, vecs2_1, scale_1, ups_1)], ()
    )
    vectors = Total(vectors, bits)
    layer_big, layer_small = arrange_rows(where, (saved[1][0], y1), (came_y0, came_y1), sizes, (folded,))
    groups = [last0, tall0, wide0, tables, vectors, last1, tall1, wide1]
    token = advance(groups, (layer_small[0, 0, 0, :8, :128],))
    token = advance(groups, (token,))
    grad_big, grad_small = arrange_rows(where, (gx0, gx1), (came_gx0, came_gx1), sizes, (token,))
    token = grad_small[0, 0, 0, :8, :128]
    while any(group.result is None for group in groups):
        token = advance(groups, (token,))

    sums = [[group.result for group in part] for part in ((tall0, wide0, last0), (tall1, wide1, last1))]
    came = [[hand_over(item, layer) for item in sums[layer]] for layer in range(2)]
    block = width // devices
    grad_down, grad_up, grad_proj, grad_qkv = arrange_grads(where, sums, came, block, width)

    ff = up_bias.shape[1] // width
    mine = lax.dynamic_index_in_dim(vectors.result, core, 0, keepdims=False)
    lines = lax.dynamic_slice(mine, (0, place * block), (10, block))
    grad_up_bias = lax.dynamic_slice(mine[10 : 10 + ff].reshape(1, -1), (0, place * ff * block), (1, ff * block))

    def vector(row):
        return lines[row : row + 1]

    folded = tables.result.reshape(-1, 2, HEAD_ROWS, 128)
    folded = lax.dynamic_index_in_dim(folded, core, 1, keepdims=False)
    grad_table_big, grad_table_small = [item[None] for item in table_grads(folded, grids, HEADS)]
    return (
        layer_big,
        layer_small,
        grad_big,
        grad_small,
        vector(0),
        vector(1),
        grad_qkv,
        vector(2),
        vector(3),
        grad_table_big,
        grad_table_small,
        grad_proj,
        vector(4),
        vector(5),
        vector(6),
        vector(7),
        grad_up,
        grad_up_bias,
        grad_down,
        vector(8),
        vector(9),
    )


def solution(mesh):
    row = P("section", None)
    whole = P("section", None, None)
    dp4 = P(None, "dp", None, None)
    in_specs = (dp4, dp4, P(None, "dp"), dp4, dp4, row, row, whole, row, row, whole, whole, whole, row, row, row, row, whole, row, whole, row, row)
    out5 = P("section", None, "dp", None, None)
    vec = P("section", "dp")
    mat = P("section", "dp", None)
    out_specs = (out5, out5, out5, out5, vec, vec, mat, vec, vec, whole, whole, mat, vec, vec, vec, vec, mat, vec, mat, vec, vec)
    return jax.shard_map(body, mesh=mesh, in_specs=in_specs, out_specs=out_specs, check_vma=False)
```

```python
import math

import jax
import jax.numpy as jnp
from jax import lax
from jax.experimental import pallas as pl
from jax.experimental.pallas import tpu as pltpu
from jax.sharding import PartitionSpec as P

HEADS = 12
EPS = 1e-06
LOW = -1e30
MIB = 1024 * 1024
VMEM_BYTES = 44 * MIB
COST = 0.4
F32 = jnp.float32
BF16 = jnp.bfloat16
V = pl.BlockSpec(memory_space=pltpu.VMEM)
S = pl.BlockSpec(memory_space=pltpu.SMEM)
H = pl.BlockSpec(memory_space=pltpu.HBM)


def up_to(value, multiple):
    return -(-value // multiple) * multiple


def mm(left, right):
    return jnp.dot(left, right, preferred_element_type=F32)


def mm_back(left, right):
    return lax.dot_general(left, right, (((1,), (1,)), ((), ())), preferred_element_type=F32)


def mm_outer(left, right):
    return lax.dot_general(left, right, (((0,), (0,)), ((), ())), preferred_element_type=F32)


def norm_parts(values):
    centre = values - jnp.mean(values, axis=-1, keepdims=True)
    spread = jnp.mean(centre * centre, axis=-1, keepdims=True)
    scale = lax.rsqrt(spread + EPS)
    return centre * scale, scale


def norm_back(upstream, values, gain):
    unit, scale = norm_parts(values)
    scaled = upstream * gain
    first = jnp.mean(scaled, axis=-1, keepdims=True)
    second = jnp.mean(scaled * unit, axis=-1, keepdims=True)
    going = scale * (scaled - first - unit * second)
    return (
        going,
        jnp.sum(upstream * unit, axis=0, keepdims=True),
        jnp.sum(upstream, axis=0, keepdims=True),
    )


def gelu_parts(x):
    raised = jnp.exp(-0.5 * x * x)
    t = 1.0 / (1.0 + (0.3275911 * math.sqrt(0.5)) * jnp.abs(x))
    poly = t * (
        0.127414796
        + t * (-0.142248368 + t * (0.7107068705 + t * (-0.7265760135 + t * 0.5307027145)))
    )
    half = poly * raised
    phi = jnp.where(x >= 0, 1.0 - half, half)
    return x * phi, phi + x * (raised * (1.0 / math.sqrt(2.0 * math.pi)))


def column_cuts(width, parts):
    step = width // parts
    return [(slice(None), pl.ds(i * step, step)) for i in range(parts)]


def row_cuts(height, parts):
    step = height // parts
    return [(pl.ds(i * step, step), slice(None)) for i in range(parts)]


def fetch_start(mine, own, other, buffer, sems, cuts):
    for i, cut in enumerate(cuts):

        @pl.when(mine)
        def _():
            pltpu.make_async_copy(own.at[cut], buffer.at[cut], sems.at[i]).start()

        @pl.when(jnp.logical_not(mine))
        def _():
            pltpu.make_async_copy(other.at[cut], buffer.at[cut], sems.at[i]).start()


def fetch_wait(own, buffer, sems, cuts, i):
    pltpu.make_async_copy(own.at[cuts[i]], buffer.at[cuts[i]], sems.at[i]).wait()


def size_of(item):
    return math.prod(item.shape) * jnp.dtype(item.dtype).itemsize


def after_spec(item):
    return V if size_of(item) < 65536 else H


def kernel_call(body, ins, outs, scratch, args, flops, after=(), out_specs=None, **more):
    ins, args = list(ins) + [after_spec(item) for item in after], tuple(args) + tuple(after)
    count = len(args)
    inner = body

    def body(*refs):
        inner(*refs[: count - len(after)], *refs[count:])

    return pl.pallas_call(
        body,
        in_specs=ins,
        out_specs=out_specs or [V] * len(outs),
        out_shape=[pltpu.HBM(o.shape, o.dtype) if out_specs and out_specs[n] is H else o for n, o in enumerate(outs)],
        scratch_shapes=scratch,
        compiler_params=pltpu.CompilerParams(vmem_limit_bytes=VMEM_BYTES, **more),
        cost_estimate=pl.CostEstimate(flops=int(flops / COST), bytes_accessed=1024, transcendentals=0),
    )(*args)


def shape(dims, kind):
    return jax.ShapeDtypeStruct(dims, kind)


def qkv_forward(layer, core, x, gain, shift, joined, own, other, after=()):
    rows, width = x.shape
    triple = own.shape[1]
    cuts = column_cuts(triple, 3)

    def body(core_ref, x_ref, gain_ref, shift_ref, joined_ref, own_ref, other_ref, normed_ref, proj_ref, buf, sems):
        mine = core_ref[0] == layer
        fetch_start(mine, own_ref, other_ref, buf, sems, cuts)
        unit, _ = norm_parts(x_ref[...].astype(F32))
        normed_ref[...] = (unit * gain_ref[...] + shift_ref[...]).astype(BF16)
        for i in range(3):
            fetch_wait(own_ref, buf, sems, cuts, i)
            cols = pl.ds(i * width, width)
            proj_ref[:, cols] = (mm(normed_ref[...], buf[:, cols]) + joined_ref[:, cols]).astype(BF16)

    return kernel_call(
        body,
        [S, V, V, V, V, H, H],
        [shape((rows, width), BF16), shape((rows, triple), BF16)],
        [pltpu.VMEM((width, triple), BF16), pltpu.SemaphoreType.DMA((3,))],
        (core, x, gain, shift, joined, own, other),
        5 * 10**9,
        after=after,
    )


def build_bias(base, out_ref, block_ref, grid, corner, crops, length, block_rows):
    lanes = base.shape[1]
    head_patch, patch_head, head_head = corner
    lane = lax.broadcasted_iota(jnp.int32, (block_rows, 256), 1)
    line = lax.broadcasted_iota(jnp.int32, (block_rows, 256), 0)
    first = jnp.where(lane == 0, head_head, head_patch)
    block_ref[...] = jnp.where(lane >= length, LOW, first)
    small = lane[:grid]
    for r in range(grid):
        off = (grid - 1 - r) * grid
        moved = base if off == 0 else pltpu.roll(base, lanes - off, 1)
        moved = moved[:grid, :256]
        value = jnp.where(small == 0, patch_head, jnp.where(small >= length, LOW, moved))
        block_ref[pl.ds(1 + grid * r, grid), :] = value
    if crops == 1:
        return
    out_ref[...] = jnp.full(out_ref.shape, LOW, F32)
    for s in range(crops):
        value = block_ref[pl.ds(0, length), :]
        if s:
            value = pltpu.roll(value, s * length, 1)
        out_ref[pl.ds(s * length, length), :] = value


def pair_bias(pair, corner_ref, bb_ref, bs_ref, big, block, small, sizes):
    crops, len_big, pad_big, slots, len_small, pad_small = sizes
    grid_big, grid_small = math.isqrt(len_big - 1), math.isqrt(len_small - 1)
    for h in range(2):
        head = pair * 2 + h
        build_bias(bb_ref[head], big.at[pl.ds(h * pad_big, pad_big)], big.at[pl.ds(h * pad_big, pad_big)], grid_big, [corner_ref[0, i, head] for i in range(3)], 1, len_big, pad_big)
        build_bias(bs_ref[head], small.at[pl.ds(h * pad_small, pad_small)], block, grid_small, [corner_ref[1, i, head] for i in range(3)], slots, len_small, block.shape[0])


def two_heads(value):
    lane = lax.broadcasted_iota(jnp.int32, (1, 128), 1)
    return jnp.concatenate([jnp.where(lane < 64, value, 0), jnp.where(lane >= 64, value, 0)], axis=0)


def one_line(value):
    count = value.shape[0] // 2
    lane = lax.broadcasted_iota(jnp.int32, (1, 128), 1)
    return jnp.where(lane < 64, value[:count], value[count:])


def attention_probs(scores):
    raised = jnp.exp(scores - jnp.max(scores, axis=-1, keepdims=True))
    return raised * (1.0 / jnp.sum(raised, axis=-1, keepdims=True))


def attention_parts(sizes):
    crops, _, pad_big, _, _, pad_small = sizes
    return [(c * pad_big, pad_big, True) for c in range(crops)] + [(crops * pad_big, pad_small, False)]


def bias_scratch(sizes):
    _, _, pad_big, _, len_small, pad_small = sizes
    return [
        pltpu.VMEM((2 * pad_big, 256), F32),
        pltpu.VMEM((up_to(len_small, 8), 256), F32),
        pltpu.VMEM((2 * pad_small, 256), F32),
    ]


def attention_forward(projected, base_big, base_small, corners, sizes, after=()):
    rows, triple = projected.shape
    width = triple // 3
    pairs = HEADS // 2
    parts = attention_parts(sizes)

    def body(corner_ref, proj_ref, bb_ref, bs_ref, out_ref, big, block, small):
        def step(pair, carry):
            pair_bias(pair, corner_ref, bb_ref, bs_ref, big, block, small, sizes)
            q, k, v = [pl.ds(pl.multiple_of(n * width + pair * 128, 128), 128) for n in range(3)]
            scores = []
            for start, count, is_big in parts:
                part = pl.ds(start, count)
                bias = big if is_big else small
                scores.append(mm_back(two_heads(proj_ref[part, q] * 0.125), proj_ref[part, k]) + bias[:, :count])
            probs = [attention_probs(item).astype(BF16) for item in scores]
            for (start, count, is_big), item in zip(parts, probs):
                part = pl.ds(start, count)
                out_ref[part, q] = one_line(mm(item, proj_ref[part, v])).astype(BF16)
            return carry

        lax.fori_loop(0, pairs, step, 0)

    return kernel_call(
        body,
        [S, V, V, V],
        [shape((rows, width), BF16)],
        bias_scratch(sizes),
        (corners, projected, base_big, base_small),
        10**10,
        after=after,
    )[0]


FF_STEP = 512


def saved_cuts(width, hidden):
    return [(0, hidden), (hidden, width), (hidden + width, width), (hidden + 2 * width, width)]


def mlp_forward(layer, core, attended, normed, x, keep, vec, up_bias, proj, up, down=None):
    rows, width = x.shape
    hidden = up[0].shape[1]
    count = hidden // FF_STEP
    cuts = [(slice(None), slice(None))]
    up_cuts = column_cuts(hidden, count)
    down_cuts = row_cuts(hidden, 2)
    spans = saved_cuts(width, hidden)
    total_cols = hidden + 3 * width
    weights = proj + up + (down or ())

    def body(core_ref, att_ref, n1_ref, x_ref, keep_ref, vec_ref, bias_ref, *refs):
        weight_refs, refs = refs[: len(weights)], refs[len(weights) :]
        left_ref, slope_ref, branch_ref, middle_ref, refs = refs[0], refs[1], refs[2], refs[3], refs[4:]
        if down:
            y_ref, mlp_ref, refs = refs[0], refs[1], refs[2:]
        buf, buf_up, hid, slp, br, mid, n2, sems, sems_up, out_sems = refs[:10]
        mine = core_ref[0] == layer
        fetch_start(mine, weight_refs[0], weight_refs[1], buf, sems, cuts)
        fetch_start(mine, weight_refs[2], weight_refs[3], buf_up, sems_up, up_cuts)
        if down:
            buf_down, mlp_buf, sems_down = refs[10:]
            fetch_start(mine, weight_refs[4], weight_refs[5], buf_down, sems_down, down_cuts)
        going = []

        def send(source, target):
            copy = pltpu.make_async_copy(source, target, out_sems.at[len(going)])
            copy.start()
            going.append(copy)

        def span(n):
            return left_ref.at[:, pl.ds(*spans[n])]

        send(att_ref, span(2))
        send(n1_ref, span(3))
        fetch_wait(weight_refs[0], buf, sems, cuts, 0)
        branch = mm(att_ref[...], buf[...]) + vec_ref[4:5, :]
        br[...] = branch.astype(BF16)
        middle = x_ref[...].astype(F32) + vec_ref[5:6, :] * branch
        mid[...] = middle
        unit, _ = norm_parts(middle)
        n2[...] = (unit * vec_ref[6:7, :] + vec_ref[7:8, :]).astype(BF16)
        send(br, branch_ref)
        send(mid, middle_ref)
        send(n2, span(1))
        for i in range(count):
            fetch_wait(weight_refs[2], buf_up, sems_up, up_cuts, i)

        def pre_of(i):
            cols = pl.ds(i * FF_STEP, FF_STEP)
            return mm(n2[...], buf_up[:, cols]) + bias_ref[:, cols]

        pre = pre_of(0)
        for i in range(count):
            following = pre_of(i + 1) if i + 1 < count else None
            value, slope = gelu_parts(pre)
            cols = pl.ds(i * FF_STEP, FF_STEP)
            hid[:, cols] = value.astype(BF16)
            slp[:, cols] = slope.astype(BF16)
            pre = following
            if i % 2 == 1:
                both = pl.ds((i - 1) * FF_STEP, 2 * FF_STEP)
                send(hid.at[:, both], left_ref.at[:, both])
                send(slp.at[:, both], slope_ref.at[:, both])
        if down:
            for i in range(2):
                fetch_wait(weight_refs[4], buf_down, sems_down, down_cuts, i)
            total = mm(hid[...], buf_down[...]) + vec_ref[8:9, :]
            mlp_buf[...] = total.astype(BF16)
            send(mlp_buf, mlp_ref)
            y_ref[...] = ((mid[...] + vec_ref[9:10, :] * total) * keep_ref[...]).astype(BF16)
        for copy in going:
            copy.wait()

    outs = [shape((rows, total_cols), BF16), shape((rows, hidden), BF16), shape((rows, width), BF16), shape((rows, width), F32)]
    out_specs = [H] * 4
    scratch = [
        pltpu.VMEM((width, width), BF16),
        pltpu.VMEM((width, hidden), BF16),
        pltpu.VMEM((rows, hidden), BF16),
        pltpu.VMEM((rows, hidden), BF16),
        pltpu.VMEM((rows, width), BF16),
        pltpu.VMEM((rows, width), F32),
        pltpu.VMEM((rows, width), BF16),
        pltpu.SemaphoreType.DMA((1,)),
        pltpu.SemaphoreType.DMA((count,)),
        pltpu.SemaphoreType.DMA((6 + count,)),
    ]
    if down:
        outs += [shape((rows, width), BF16), shape((rows, width), BF16)]
        out_specs += [V, H]
        scratch += [
            pltpu.VMEM((hidden, width), BF16),
            pltpu.VMEM((rows, width), BF16),
            pltpu.SemaphoreType.DMA((2,)),
        ]
    return kernel_call(
        body,
        [S, V, V, V, V, V, V] + [H] * len(weights),
        outs,
        scratch,
        (core, attended, normed, x, keep, vec, up_bias) + weights,
        (17 if down else 13) * 10**9,
        out_specs=out_specs,
    )


def down_forward(layer, core, left, middle, keep, vec, own, other, upstream, after=()):
    rows, width = middle.shape
    depth = own.shape[0]
    parts = 4
    cuts = row_cuts(depth, parts)
    step = depth // parts

    def body(core_ref, left_ref, middle_ref, keep_ref, vec_ref, g_ref, own_ref, other_ref, y_ref, sum_ref, buf, hid, mid, sems, in_sems):
        fetch_start(core_ref[0] == layer, own_ref, other_ref, buf, sems, cuts)
        copies = [
            pltpu.make_async_copy(left_ref.at[:, pl.ds(i * step, step)], hid.at[:, pl.ds(i * step, step)], in_sems.at[i])
            for i in range(parts)
        ] + [pltpu.make_async_copy(middle_ref, mid, in_sems.at[parts])]
        for copy in copies:
            copy.start()
        total = vec_ref[8:9, :]
        for i in range(parts):
            fetch_wait(own_ref, buf, sems, cuts, i)
            copies[i].wait()
            part = pl.ds(i * step, step)
            total = total + mm(hid[:, part], buf[part, :])
        copies[parts].wait()
        sum_ref[...] = jnp.sum(g_ref[...].astype(F32) * keep_ref[...] * total, axis=0, keepdims=True)
        y_ref[...] = ((mid[...] + vec_ref[9:10, :] * total) * keep_ref[...]).astype(BF16)

    return kernel_call(
        body,
        [S, H, H, V, V, V, H, H],
        [shape((rows, width), BF16), shape((1, width), F32)],
        [
            pltpu.VMEM((depth, width), BF16),
            pltpu.VMEM((rows, depth), BF16),
            pltpu.VMEM((rows, width), F32),
            pltpu.SemaphoreType.DMA((parts,)),
            pltpu.SemaphoreType.DMA((parts + 1,)),
        ],
        (core, left, middle, keep, vec, upstream, own, other),
        6 * 10**9,
        after=after,
    )


def send_halves(me, copies, pair, source, outs, sems):
    keep, send = outs
    for half in range(2):

        @pl.when(me == half)
        def _():
            pltpu.make_async_copy(source(half), keep, sems.at[pair]).start()
            pltpu.make_async_copy(source(1 - half), send, sems.at[pair + 1]).start()

    copies.append(pltpu.make_async_copy(source(0), keep, sems.at[pair]))
    copies.append(pltpu.make_async_copy(source(1), send, sems.at[pair + 1]))


def mlp_backward(layer, core, upstream, keep, vec, slope, middle, branch, mlp, down, up, proj, after=()):
    rows, width = middle.shape
    depth = slope.shape[1]
    count = depth // FF_STEP
    half_cols, half_width = depth // 2, width // 2
    wide = half_cols + 2 * half_width
    extra = () if mlp is None else (mlp,)
    down_cuts, up_cuts = row_cuts(depth, count), column_cuts(depth, count)
    cuts = [(slice(None), slice(None))]

    def body(core_ref, g_ref, keep_ref, vec_ref, slope_ref, middle_ref, branch_ref, *refs):
        mlp_refs, refs = refs[: len(extra)], refs[len(extra) :]
        od, td, ou, tu, op, tp, keep_out, send_out, ga_ref, gmid_ref, vecs_ref, ups_ref, low, back_buf, slp, mid, br, mlp_buf, bd, bu, bp, sd, su, sp, sin, sout = refs
        me = core_ref[0]
        mine = me == layer
        fetch_start(mine, od, td, bd, sd, down_cuts)
        coming = [
            pltpu.make_async_copy(source, target, sin.at[n])
            for n, (source, target) in enumerate([(slope_ref, slp), (middle_ref, mid), (branch_ref, br)] + [(r, mlp_buf) for r in mlp_refs])
        ]
        coming[0].start()
        fetch_start(mine, ou, tu, bu, su, up_cuts)
        for copy in coming[1:]:
            copy.start()
        fetch_start(mine, op, tp, bp, sp, cuts)
        gm = (vec_ref[9:10, :] * (g_ref[...].astype(F32) * keep_ref[...])).astype(BF16)
        low[...] = gm
        for half in range(2):
            back_buf[half, :, :half_width] = gm[:, half * half_width : (half + 1) * half_width]
        vecs_ref[...] = jnp.zeros_like(vecs_ref)
        vecs_ref[4:5, :] = jnp.sum(gm.astype(F32), axis=0, keepdims=True)
        for i in range(count):
            fetch_wait(od, bd, sd, down_cuts, i)
        coming[0].wait()
        for i in range(count):
            cols = pl.ds(i * FF_STEP, FF_STEP)
            gp = (mm_back(low[...], bd[cols, :]) * slp[:, cols].astype(F32)).astype(BF16)
            back_buf[2 * i // count, :, pl.ds(half_width + (i * FF_STEP) % half_cols, FF_STEP)] = gp
            ups_ref[:, cols] = jnp.sum(gp.astype(F32), axis=0, keepdims=True)
        for i in range(count):
            fetch_wait(ou, bu, su, up_cuts, i)
        middle_cols = slice(half_width, half_width + half_cols)
        back = mm_back(back_buf[0, :, middle_cols], bu[:, :half_cols]) + mm_back(back_buf[1, :, middle_cols], bu[:, half_cols:])
        for copy in coming[1:]:
            copy.wait()
        going, gain, shift = norm_back(back, mid[...], vec_ref[6:7, :])
        g = g_ref[...].astype(F32) * keep_ref[...]
        gmid = g + going
        gmid_ref[...] = gmid
        gb = (vec_ref[5:6, :] * gmid).astype(BF16)
        low[...] = gb
        for half in range(2):
            back_buf[half, :, half_width + half_cols :] = gb[:, half * half_width : (half + 1) * half_width]
        copies = []
        send_halves(me, copies, 0, lambda half: back_buf.at[half], (keep_out, send_out), sout)
        vecs_ref[0:1, :] = gain
        vecs_ref[1:2, :] = shift
        vecs_ref[2:3, :] = jnp.sum(gmid * br[...].astype(F32), axis=0, keepdims=True)
        vecs_ref[3:4, :] = jnp.sum(gb.astype(F32), axis=0, keepdims=True)
        if extra:
            vecs_ref[5:6, :] = jnp.sum(g * mlp_buf[...].astype(F32), axis=0, keepdims=True)
        fetch_wait(op, bp, sp, cuts, 0)
        ga_ref[...] = mm_back(low[...], bp[...]).astype(BF16)
        for copy in copies:
            copy.wait()

    return kernel_call(
        body,
        [S, V, V, V, H, H, H] + [H] * (len(extra) + 6),
        [
            shape((rows, wide), BF16),
            shape((rows, wide), BF16),
            shape((rows, width), BF16),
            shape((rows, width), F32),
            shape((8, width), F32),
            shape((1, depth), F32),
        ],
        [
            pltpu.VMEM((rows, width), BF16),
            pltpu.VMEM((2, rows, wide), BF16),
            pltpu.VMEM((rows, depth), BF16),
            pltpu.VMEM((rows, width), F32),
            pltpu.VMEM((rows, width), BF16),
            pltpu.VMEM((rows, width), BF16),
            pltpu.VMEM((depth, width), BF16),
            pltpu.VMEM((width, depth), BF16),
            pltpu.VMEM((width, width), BF16),
            pltpu.SemaphoreType.DMA((count,)),
            pltpu.SemaphoreType.DMA((count,)),
            pltpu.SemaphoreType.DMA((1,)),
            pltpu.SemaphoreType.DMA((4,)),
            pltpu.SemaphoreType.DMA((2,)),
        ],
        (core, upstream, keep, vec, slope, middle, branch) + extra + down + up + proj,
        14 * 10**9,
        after=after,
        out_specs=[H, H, V, V, V, V],
    )


def attention_backward(core, projected, upstream, base_big, base_small, corners, sizes, after=()):
    rows, triple = projected.shape
    width = triple // 3
    pairs = HEADS // 2
    crops, len_big, pad_big, slots, len_small, pad_small = sizes
    grid_big, grid_small = math.isqrt(len_big - 1), math.isqrt(len_small - 1)
    half = 3 * pairs // 2

    parts = attention_parts(sizes)

    def body(core_ref, corner_ref, proj_ref, g_ref, bb_ref, bs_ref, gproj_ref, keep_out, send_out, tb_ref, ts_ref, sums_ref, big, block, small, dbig, dsmall, dblock, sout):
        dbig[...] = jnp.zeros_like(dbig)
        dsmall[...] = jnp.zeros_like(dsmall)
        dblock[...] = jnp.zeros_like(dblock)
        tb_ref[...] = jnp.zeros_like(tb_ref)
        ts_ref[...] = jnp.zeros_like(ts_ref)

        def step(pair, carry):
            pair_bias(pair, corner_ref, bb_ref, bs_ref, big, block, small, sizes)

            q, k, v = [pl.ds(pl.multiple_of(n * width + pair * 128, 128), 128) for n in range(3)]
            places = [which * pairs + pair for which in range(3)]
            scores, gprs = [], []
            for start, count, is_big in parts:
                part = pl.ds(start, count)
                bias = big if is_big else small
                scores.append(mm_back(two_heads(proj_ref[part, q] * 0.125), proj_ref[part, k]) + bias[:, :count])
                gprs.append(mm_back(two_heads(g_ref[part, q]), proj_ref[part, v]))
            probs = [attention_probs(item) for item in scores]
            gss = [(p * (gpr - jnp.sum(p * gpr, axis=-1, keepdims=True))).astype(BF16) for p, gpr in zip(probs, gprs)]
            for n, ((start, count, is_big), p, gs) in enumerate(zip(parts, probs, gss)):
                part = pl.ds(start, count)
                dref = dbig if is_big else dsmall
                if n == 0 or not is_big:
                    dref[:, :count] = gs.astype(F32)
                else:
                    dref[:, :count] += gs.astype(F32)
                gproj_ref[places[0], part, :] = (one_line(mm(gs, proj_ref[part, k])) * 0.125).astype(BF16)
                gproj_ref[places[1], part, :] = mm_outer(gs, two_heads(proj_ref[part, q] * 0.125)).astype(BF16)
                gproj_ref[places[2], part, :] = mm_outer(p.astype(BF16), two_heads(g_ref[part, q])).astype(BF16)


            for h in range(2):
                hbig, hsmall = dbig.at[pl.ds(h * pad_big, pad_big)], dsmall.at[pl.ds(h * pad_small, pad_small)]

                def fold(dref, grid, length, out_ref):
                    lanes = out_ref.shape[2]
                    wide = lax.broadcasted_iota(jnp.int32, (grid, 256), 1)
                    inside = (wide > 0) & (wide < length)
                    total = jnp.zeros((grid, lanes), F32)
                    for r in range(grid):
                        value = jnp.where(inside, dref[pl.ds(1 + grid * r, grid), :], 0)
                        if lanes > 256:
                            value = jnp.concatenate([value, jnp.zeros((grid, lanes - 256), F32)], axis=1)
                        off = (grid - 1 - r) * grid
                        total = total + (value if off == 0 else pltpu.roll(value, off, 1))
                    out_ref[pair * 2 + h, :grid, :] = total
                    line = lax.broadcasted_iota(jnp.int32, (length, 256), 0)
                    spot = lax.broadcasted_iota(jnp.int32, (length, 256), 1)
                    value = jnp.where(spot < length, dref[pl.ds(0, length), :], 0)
                    out_ref[pair * 2 + h, grid : grid + 1, :256] = value[0:1, :]
                    out_ref[pair * 2 + h, grid + 1 : grid + 2, :256] = jnp.sum(jnp.where(line > 0, value, 0), axis=0, keepdims=True)

                fold(hbig, grid_big, len_big, tb_ref)
                total = hsmall[pl.ds(0, len_small), :]
                for s in range(1, slots):
                    total = total + pltpu.roll(hsmall[pl.ds(s * len_small, len_small), :], 256 - s * len_small, 1)
                dblock[pl.ds(0, len_small), :] = total
                fold(dblock, grid_small, len_small, ts_ref)
            for n, which in ((0, 0), (1, 2)):
                sums_ref[n : n + 1, q] = jnp.sum(gproj_ref[places[which]].astype(F32), axis=0, keepdims=True)
            return carry

        lax.fori_loop(0, pairs, step, 0)
        copies = []
        send_halves(core_ref[0], copies, 0, lambda n: gproj_ref.at[pl.ds(n * half, half)], (keep_out, send_out), sout)
        for copy in copies:
            copy.wait()

    return kernel_call(
        body,
        [S, S, V, V, V, V],
        [
            shape((2 * half, rows, 128), BF16),
            shape((half, rows, 128), BF16),
            shape((half, rows, 128), BF16),
            shape((HEADS, 16, 512), F32),
            shape((HEADS, 8, 256), F32),
            shape((2, width), F32),
        ],
        bias_scratch(sizes)
        + [
            pltpu.VMEM((2 * pad_big, 256), F32),
            pltpu.VMEM((2 * pad_small, 256), F32),
            pltpu.VMEM((up_to(len_small, 8), 256), F32),
            pltpu.SemaphoreType.DMA((2,)),
        ],
        (core, corners, projected, upstream, base_big, base_small),
        15 * 10**9,
        out_specs=[V, H, H, V, V, V],
        after=after,
    )


def qkv_backward(layer, core, gproj, x, gmid, gain, own, other, after=()):
    rows, width = x.shape
    blocks = gproj.shape[0]
    triple = blocks * 128
    cuts = column_cuts(triple, 3)
    group = blocks // 3

    def body(core_ref, gproj_ref, x_ref, gmid_ref, gain_ref, own_ref, other_ref, gx_ref, vecs_ref, buf, acc, sems):
        me = core_ref[0]
        fetch_start(me == layer, own_ref, other_ref, buf, sems, cuts)
        for i in range(3):
            fetch_wait(own_ref, buf, sems, cuts, i)
            joined = jnp.concatenate([gproj_ref[n] for n in range(i * group, (i + 1) * group)], axis=1)
            more = mm_back(joined, buf[:, pl.ds(i * width, width)])
            if i == 0:
                acc[...] = more
            else:
                acc[...] += more
        going, gain_sum, shift_sum = norm_back(acc[...], x_ref[...].astype(F32), gain_ref[...])
        gx_ref[...] = (gmid_ref[...] + going).astype(BF16)
        vecs_ref[0:1, :] = gain_sum
        vecs_ref[1:2, :] = shift_sum

    return kernel_call(
        body,
        [S, V, V, V, V, H, H],
        [shape((rows, width), BF16), shape((2, width), F32)],
        [
            pltpu.VMEM((width, triple), BF16),
            pltpu.VMEM((rows, width), F32),
            pltpu.SemaphoreType.DMA((3,)),
        ],
        (core, gproj, x, gmid, gain, own, other),
        5 * 10**9,
        after=after,
    )


def place_of(relative, order):
    place = 0
    for bit in order:
        place = place * 2 + ((relative >> bit) & 1)
    return place


def piece_plan(names, tiles, quarters):
    counts = [
        {name: tiles[name] // 3 * (2 - p) * (quarters if name == "down" else 1) for name in names} for p in range(2)
    ]
    bases = [{name: sum(counts[p][other] for other in names[:n]) for n, name in enumerate(names)} for p in range(2)]
    return counts, bases, [sum(count.values()) for count in counts]


def weight_grad(where, orders, names, left, right, blocks, flops, after=()):
    devices = 1 << len(orders[0][0])
    pieces = len(orders)
    rows, total_cols = left[0].shape
    width = total_cols - 2 * right[0].shape[1]
    hidden = total_cols - 3 * width
    spans = dict(zip(("down", "up", "proj", "qkv"), saved_cuts(width, hidden)))
    backs = {"down": (0, width // 2), "up": (width // 2, hidden // 2), "proj": (width // 2 + hidden // 2, width // 2), "qkv": (0, 3 * width // 2)}
    block = width // devices
    tiles = {name: backs[name][1] // 128 for name in names}
    counts, bases, subs = piece_plan(names, tiles, hidden // width)
    half = devices // 2
    arrays = tuple(left) + tuple(right) + (tuple(blocks) if "qkv" in names else ())
    copies_needed = sum(2 * (hidden // width) + 2 if name == "down" else 2 + 2 * blocks[0].shape[0] if name == "qkv" else 4 for name in names)

    def body(where_ref, *refs):
        ins, refs = refs[: len(arrays)], refs[len(arrays) + len(after) :]
        outs, refs = refs[: 2 * pieces], refs[2 * pieces :]
        held, refs = refs[:pieces], refs[pieces:]
        lefts, refs = refs[: len(names)], refs[len(names) :]
        rights, refs = refs[: len(names)], refs[len(names) :]
        turned, sems, in_sems = refs
        me, first = where_ref[1], where_ref[0] == 0
        places = [
            [jnp.where(first, place_of(j ^ me, order[0]), place_of(j ^ me, order[1])) for j in range(devices)]
            for order in orders
        ]
        coming = {name: [] for name in names}
        used = 0

        def bring(name, source, target):
            nonlocal used
            copy = pltpu.make_async_copy(source, target, in_sems.at[used])
            copy.start()
            used += 1
            coming[name].append(copy)

        for n, name in enumerate(names):
            for side in range(2):
                lines = pl.ds(side * rows, rows)
                if name == "qkv":
                    for t in range(tiles[name]):
                        bring(name, ins[4 + side].at[t], rights[n].at[lines, pl.ds(t * 128, 128)])
                else:
                    bring(name, ins[2 + side].at[:, pl.ds(*backs[name])], rights[n].at[lines, :])
            low, size = spans[name]
            for start in range(0, size, width):
                for side in range(2):
                    lines = pl.ds(side * rows, rows)
                    bring(name, ins[side].at[:, pl.ds(low + start, width)], lefts[n].at[lines, pl.ds(start, width)])

        def put(name, value, line, tile, extra=0):
            large = tiles[name] // 3 * 2
            p, at = (0, tile) if tile < large else (1, tile - large)
            held[p][places[p][line], bases[p][name] + at * (hidden // width if name == "down" else 1) + extra] = value

        def copies(p):
            return [
                pltpu.make_async_copy(held[p].at[pl.ds(0, half)], outs[2 * p], sems.at[2 * p]),
                pltpu.make_async_copy(held[p].at[pl.ds(half, half)], outs[2 * p + 1], sems.at[2 * p + 1]),
            ]

        for n, name in enumerate(names):
            waits = coming[name]
            final = n + 1 == len(names)
            if name == "down":
                for copy in waits[:2]:
                    copy.wait()
                cols = backs[name][1]
                turned[:cols, :] = rights[n][...].T
                lines = block * (hidden // width)
                for c in range(hidden // width):
                    for copy in waits[2 + 2 * c : 4 + 2 * c]:
                        copy.wait()
                    value = mm(turned[:cols, :], lefts[n][:, pl.ds(c * width, width)]).astype(BF16).T
                    for j in range(width // block):
                        at = c * (width // block) + j
                        for t in range(tiles[name]):
                            put(name, value[j * block : (j + 1) * block, t * 128 : (t + 1) * 128], at // (hidden // width), t, at % (hidden // width))
                done = 0
            else:
                for copy in waits:
                    copy.wait()
                turned[...] = lefts[n][...].T
                done = 0
                for low in range(0, tiles[name], 4):
                    high = min(low + 4, tiles[name])
                    value = mm(turned[...], rights[n][:, low * 128 : high * 128])
                    for j in range(devices):
                        for t in range(low, high):
                            put(name, value[j * block : (j + 1) * block, (t - low) * 128 : (t - low + 1) * 128].astype(BF16), j, t)
                    while final and done < pieces and (tiles[name] // 3 * 2, tiles[name])[done] <= high:
                        for copy in copies(done):
                            copy.start()
                        done += 1
            if final:
                for p in range(done, pieces):
                    for copy in copies(p):
                        copy.start()
        for p in range(pieces):
            for copy in copies(p):
                copy.wait()

    outs = [shape((half, subs[p], block, 128), BF16) for p in range(pieces) for _ in range(2)]
    scratch = [pltpu.VMEM((devices, subs[p], block, 128), BF16) for p in range(pieces)]
    scratch += [pltpu.VMEM((2 * rows, spans[name][1]), BF16) for name in names]
    scratch += [pltpu.VMEM((2 * rows, backs[name][1]), BF16) for name in names]
    scratch += [pltpu.VMEM((width, 2 * rows), BF16)]
    return pl.pallas_call(
        body,
        in_specs=[S] + [H] * len(arrays) + [after_spec(item) for item in after],
        out_specs=[H] * (2 * pieces),
        out_shape=[pltpu.HBM(o.shape, o.dtype) for o in outs],
        scratch_shapes=scratch + [pltpu.SemaphoreType.DMA((2 * pieces,)), pltpu.SemaphoreType.DMA((copies_needed,))],
        compiler_params=pltpu.CompilerParams(vmem_limit_bytes=VMEM_BYTES),
        cost_estimate=pl.CostEstimate(flops=int(flops / COST), bytes_accessed=1024, transcendentals=0),
    )(where, *arrays, *after)


NAMES = ("down", "up", "proj", "qkv")


def add_stage(items, after):
    args, outs, plan = [], [], []
    for item in items:
        kept, came, how = item
        if how == "joined":
            plan.append((how, len(args), len(kept), len(outs)))
            half = shape((kept[0].shape[0] // 2, sum(k.shape[1] for k in kept)) + kept[0].shape[2:], BF16)
            outs += [half, half]
            args += list(kept) + list(came)
        elif how == "last":
            plan.append((how, len(args), len(kept), len(outs)))
            outs.append(shape((sum(k.shape[1] for k in kept),) + kept[0].shape[2:], F32))
            args += list(kept) + list(came)
        else:
            plan.append((how, len(args), 1, len(outs)))
            if how == "halves":
                half = shape((kept.shape[0] // 2,) + kept.shape[1:], BF16)
                outs += [half, half]
            else:
                outs.append(shape(kept.shape, F32))
            args += [kept, came]

    def body(*refs):
        ins, results = refs[: len(args)], refs[len(args) :]
        for how, at, count, to in plan:
            if how == "last":
                low = 0
                for n in range(count):
                    high = low + ins[at + n].shape[1]
                    results[to][low:high] = ins[at + n][0].astype(F32) + ins[at + count + n][0].astype(F32)
                    low = high
            elif how == "joined":
                half, low = outs[to].shape[0], 0
                for n in range(count):
                    high = low + ins[at + n].shape[1]
                    for part in range(2):
                        cut = pl.ds(part * half, half)
                        value = ins[at + n][cut].astype(F32) + ins[at + count + n][cut].astype(F32)
                        results[to + part][:, low:high] = value.astype(BF16)
                    low = high
            elif how == "whole":
                results[to][...] = ins[at][...] + ins[at + 1][...]
            else:
                half = outs[to].shape[0]
                for n in range(2):
                    cut = pl.ds(n * half, half)
                    results[to + n][...] = (ins[at][cut].astype(F32) + ins[at + 1][cut].astype(F32)).astype(BF16)
        results[-1][...] = jnp.zeros((8, 128), F32)

    made = kernel_call(body, [V] * len(args), outs + [shape((8, 128), F32)], [], tuple(args), 10**9, after=after)
    results = []
    for how, _, _, to in plan:
        results.append((made[to], made[to + 1]) if how in ("halves", "joined") else made[to])
    return results, made[-1]


class Scatter:
    def __init__(self, made, orders):
        self.keeps, self.sends, self.orders = list(made[0::2]), list(made[1::2]), orders
        self.step, self.result = 0, None
        self.launch()

    def launch(self):
        self.came = [
            across(send, [order[self.step] for order in both]) for send, both in zip(self.sends, self.orders)
        ]

    def items(self):
        if self.step + 1 == len(self.orders[0][0]):
            return [(self.keeps, self.came, "last")]
        return [(keep, came, "halves") for keep, came in zip(self.keeps, self.came)]

    def take(self, results):
        self.step += 1
        if self.step == len(self.orders[0][0]):
            self.result = results[0]
            return
        self.keeps, self.sends = [r[0] for r in results], [r[1] for r in results]
        self.launch()


class Total:
    def __init__(self, value, bits):
        self.value, self.bits, self.step, self.result = value, bits, 0, None
        self.came = swap(value)

    def items(self):
        return [(self.value, self.came, "whole")]

    def take(self, results):
        self.value = results[0]
        if self.step == self.bits:
            self.result = self.value
            return
        self.came = across(self.value, [self.step, self.step])
        self.step += 1


def join_groups(groups, after):
    pieces = len(groups[0].orders)
    items = [([g.keeps[p] for g in groups], [g.came[p] for g in groups], "joined") for p in range(pieces)]
    results, token = add_stage(items, after)
    joined = groups[0]
    joined.take(results)
    return joined, token


def advance(groups, after):
    groups = [group for group in groups if group.result is None]
    if not groups:
        return after[0]
    items = [group.items() for group in groups]
    results, token = add_stage([item for part in items for item in part], after)
    for group, part in zip(groups, items):
        group.take(results[: len(part)])
        results = results[len(part) :]
    return token


def gather_vectors(folded, parts):
    width = parts[0][0].shape[1]
    args = (folded,) + tuple(item for part in parts for item in part)
    count = len(parts[0])
    tiles = width // 128
    table_rows = folded.shape[0] * folded.shape[1]

    def body(folded_ref, *refs):
        out = refs[-1]
        out[pl.ds(2 * 16 * tiles, table_rows), :] = folded_ref[...].reshape(table_rows, 128)
        for layer in range(2):
            vecs1, qv, vecs2, scale, ups = [ref[...] for ref in refs[layer * count : layer * count + count]]
            rows = [vecs1, qv, vecs2[3:4], vecs2[2:3], vecs2[0:2], vecs2[4:5], scale]
            rows += [ups[:, n * width : (n + 1) * width] for n in range(ups.shape[1] // width)]
            rows.append(jnp.zeros((16 - sum(row.shape[0] for row in rows), width), F32))
            whole = jnp.concatenate(rows, axis=0)
            for t in range(tiles):
                out[pl.ds((layer * tiles + t) * 16, 16), :] = whole[:, t * 128 : (t + 1) * 128]

    return kernel_call(body, [V] * len(args), [shape((2 * 16 * tiles + table_rows, 128), F32)], [], args, 10**9)[0]


def arrange_rows(core, own, came, sizes, after):
    crops, len_big, pad_big, slots, len_small, pad_small = sizes
    width = own[0].shape[1]
    split = crops * pad_big

    def body(core_ref, own0, own1, came0, came1, out_big, out_small):
        me = core_ref[0]

        def put(place, ref):
            for c in range(crops):
                out_big[0, place, c] = ref[pl.ds(c * pad_big, len_big), :]
            rest = ref[pl.ds(split, pad_small), :].astype(F32)
            for s in range(slots):
                out_small[0, place, s] = rest[s * len_small : (s + 1) * len_small].astype(BF16)

        @pl.when(me == 0)
        def _():
            put(0, own0)
            put(1, came0)

        @pl.when(me == 1)
        def _():
            put(1, own1)
            put(0, came1)

    return kernel_call(
        body,
        [S, V, V, V, V],
        [shape((1, 2, crops, len_big, width), BF16), shape((1, 2, slots, len_small, width), BF16)],
        [],
        (core, *own, *came),
        4 * 10**9,
        after=after,
    )


def arrange_grads(core, sums, came, block, width, hidden):
    args = tuple(item for part in (*sums, *came) for _, item in part)
    quarters = hidden // width
    tiles = {"down": width // 256, "up": hidden // 256, "proj": width // 256, "qkv": 3 * width // 256}

    def body(core_ref, *refs):
        outs = dict(zip(NAMES, refs[len(args) :]))

        def put(half, part, refs):
            for (names, _), ref in zip(part, refs):
                counts, bases, subs = piece_plan(names, tiles, quarters)
                for name in names:
                    for tile in range(tiles[name]):
                        large = tiles[name] // 3 * 2
                        p, at = (0, tile) if tile < large else (1, tile - large)
                        times = quarters if name == "down" else 1
                        for q in range(times):
                            value = ref[p * subs[0] + bases[p][name] + at * times + q]
                            outs[name][0, pl.ds(q * block, block), pl.ds((half * tiles[name] + tile) * 128, 128)] = value

        count = len(args) // 2
        starts = [0, len(sums[0]), count, count + len(came[0])]
        for me in range(2):

            @pl.when(core_ref[0] == me)
            def _():
                put(me, sums[me], refs[starts[me] :])
                put(1 - me, came[me], refs[starts[2 + me] :])

    return kernel_call(
        body,
        [S] + [V] * len(args),
        [
            shape((1, quarters * block, width), F32),
            shape((1, block, hidden), F32),
            shape((1, block, width), F32),
            shape((1, block, 3 * width), F32),
        ],
        [],
        (core, *args),
        2 * 10**9,
    )


def swap(value):
    return lax.ppermute(value, "section", [(0, 1), (1, 0)])


def across(value, bits):
    devices = lax.axis_size("dp")
    pairs = [(core * devices + i, core * devices + (i ^ (1 << bits[core]))) for core in range(2) for i in range(devices)]
    return lax.ppermute(value, ("section", "dp"), pairs)


def hand_over(value, layer):
    return lax.ppermute(value, "section", [(1 - layer, layer)])


HEAD_ROWS = 16


def flip_lanes(side):
    row = lax.broadcasted_iota(jnp.int32, (side, 128), 0)
    lane = lax.broadcasted_iota(jnp.int32, (side, 128), 1)
    return jnp.where(row + lane == side - 1, 1.0, 0.0)


def table_bases(core, own, other, grids, entries_big):
    heads = own.shape[1]
    both = 2 * HEAD_ROWS

    def body(core_ref, own_ref, other_ref, out_big, out_small, corners, own_buf, other_buf):
        first = core_ref[0] == 0
        own_buf[...] = own_ref[...]
        other_buf[...] = other_ref[...]
        out_big[...] = jnp.zeros_like(out_big)
        out_small[...] = jnp.zeros_like(out_small)
        corners[...] = jnp.zeros_like(corners)
        lane = lax.broadcasted_iota(jnp.int32, (both, 128), 1)

        def lines(start, count):
            mine, theirs = own_buf[pl.ds(start, count), :], other_buf[pl.ds(start, count), :]
            return jnp.where(first, mine, theirs), jnp.where(first, theirs, mine)

        start = 0
        for n, (out, grid) in enumerate(((out_big, grids[0]), (out_small, grids[1]))):
            side = 2 * grid - 1
            flip = flip_lanes(side)
            flipped = []
            for d in range(side):
                pair = []
                for part in lines(start + (side - 1 - d) * side, side):
                    turned = lax.dot_general(part, flip, (((0,), (0,)), ((), ())), precision=lax.Precision.HIGHEST, preferred_element_type=F32)
                    pair.append(jnp.concatenate([turned, jnp.zeros((HEAD_ROWS - heads, 128), F32)], axis=0))
                flipped.append(jnp.concatenate(pair, axis=0))
            for r in range(grid):
                tiles = [jnp.zeros((both, 128), F32) for _ in range(out.shape[3] // 128)]
                for d in range(side):
                    low = 1 + d * grid
                    shift = (low - (grid - 1 - r)) % 128
                    moved = pltpu.roll(flipped[d], shift, 1) if shift else flipped[d]
                    tile, at = low // 128, low % 128
                    tiles[tile] = jnp.where((lane >= at) & (lane < at + grid), moved, tiles[tile])
                    if at + grid > 128:
                        tiles[tile + 1] = jnp.where(lane < at + grid - 128, moved, tiles[tile + 1])
                value = jnp.concatenate(tiles, axis=1)
                for layer in range(2):
                    out[layer, :, r, :] = value[layer * HEAD_ROWS : layer * HEAD_ROWS + heads]
            for layer, part in enumerate(lines(start + side * side, 3)):
                corners[layer, n, 0:3, 0:heads] = part
            start = entries_big

    return kernel_call(
        body,
        [S, V, V],
        [shape((2, heads, 16, 512), F32), shape((2, heads, 8, 256), F32), shape((2, 2, 8, 128), F32)],
        [pltpu.VMEM(own.shape, F32), pltpu.VMEM(own.shape, F32)],
        (core, own, other),
        3 * 10**9,
    )


def table_folds(big, small, grids, lengths, after):
    heads = big.shape[1]
    counts = [-(-(2 * grid - 1) // 4) for grid in grids]

    def body(big_ref, small_ref, out):
        lane = lax.broadcasted_iota(jnp.int32, (heads, 128), 1)
        base = 0
        ends = []
        for ref, grid, count, length in zip((big_ref, small_ref), grids, counts, lengths):
            for line in range(count):
                total = jnp.zeros((heads, 128), F32)
                for d in range(4 * line, min(4 * line + 4, 2 * grid - 1)):
                    low = 1 + d * grid
                    tile, at = low // 128, low % 128
                    for r in range(grid):
                        to = 32 * (d % 4) + grid - 1 - r
                        moved = ref[r, :, tile * 128 : tile * 128 + 128]
                        if at + grid > 128:
                            moved = jnp.where(lane >= at, moved, ref[r, :, tile * 128 + 128 : tile * 128 + 256])
                        shift = (to - at) % 128
                        moved = pltpu.roll(moved, shift, 1) if shift else moved
                        total = total + jnp.where((lane >= to) & (lane < to + grid), moved, 0)
                out[base + line] = total
            base += count
            first, second = ref[grid], ref[grid + 1]
            wide = lax.broadcasted_iota(jnp.int32, first.shape, 1)
            ends.append(jnp.sum(jnp.where((wide > 0) & (wide < length), first, 0), axis=1, keepdims=True))
            ends.append(second[:, 0:1])
            ends.append(first[:, 0:1])
        last = out[base - 1]
        for n, end in enumerate(ends):
            last = jnp.where(lane == 96 + n, end, last)
        out[base - 1] = last

    return kernel_call(body, [V, V], [shape((sum(counts), heads, 128), F32)], [], (big, small), 3 * 10**9, after=after)[0]


def arrange_small(where, flat, grids, entries, width, block, ups, vectors):
    tiles = width // 128
    counts = [-(-(2 * grid - 1) // 4) for grid in grids]

    def body(where_ref, flat_ref, *outs):
        layer, place = where_ref[0], where_ref[1]
        lines = jnp.concatenate(
            [flat_ref[pl.ds(pl.multiple_of((layer * tiles + t) * 16, 16), 16), :] for t in range(tiles)], axis=1
        )
        moved = pltpu.roll(lines, lax.rem(width - place * block, width), 1)
        for n in range(vectors):
            outs[n][...] = moved[n : n + 1, :block]
        per_row = width // (ups * block)
        moved = pltpu.roll(lines, lax.rem(width - lax.rem(place, per_row) * (ups * block), width), 1)
        row = lax.broadcasted_iota(jnp.int32, (16, ups * block), 0)
        chosen = jnp.where(row == vectors + place // per_row, moved[:, : ups * block], 0)
        outs[vectors][...] = jnp.sum(chosen, axis=0, keepdims=True)
        base = 2 * 16 * tiles

        def at(line):
            return flat_ref[pl.ds(pl.multiple_of(base + (line * 2 + layer) * HEAD_ROWS, HEAD_ROWS), HEAD_ROWS), :]

        line, last = 0, sum(counts) - 1
        for n, grid in enumerate(grids):
            side = 2 * grid - 1
            out = outs[vectors + 1 + n]
            row = lax.broadcasted_iota(jnp.int32, (side, 128), 0)
            lane = lax.broadcasted_iota(jnp.int32, (side, 128), 1)
            for d in range(side):
                pick = jnp.where(lane - 32 * (d % 4) + row == side - 1, 1.0, 0.0)
                value = lax.dot_general(pick, at(line + d // 4), (((1,), (1,)), ((), ())), precision=lax.Precision.HIGHEST, preferred_element_type=F32)
                out[0, pl.ds((side - 1 - d) * side, side), :] = value[:, :HEADS]
            pick = jnp.where(lane[:3] == 96 + 3 * n + row[:3], 1.0, 0.0)
            value = lax.dot_general(pick, at(last), (((1,), (1,)), ((), ())), precision=lax.Precision.HIGHEST, preferred_element_type=F32)
            out[0, pl.ds(side * side, 3), :] = value[:, :HEADS]
            line += counts[n]

    outs = [shape((1, block), F32)] * vectors + [shape((1, ups * block), F32)] + [shape((1, count, HEADS), F32) for count in entries]
    return kernel_call(body, [S, V], outs, [], (where, flat), 3 * 10**9)


def body(input_big, input_small, small_counts, cotangent_big, cotangent_small, norm1_gain, norm1_bias, qkv_weight, query_bias, value_bias, table_big, table_small, proj_weight, proj_bias, attn_scale, norm2_gain, norm2_bias, up_weight, up_bias, down_weight, down_bias, mlp_scale):
    micro, crops, len_big, width = input_big.shape
    slots_all, len_small = input_small.shape[1], input_small.shape[2]
    slots = slots_all // small_counts.shape[1]
    grid_big, grid_small = math.isqrt(len_big - 1), math.isqrt(len_small - 1)
    pad_big = up_to(len_big, 16)
    real_small = slots_all * len_small
    pad_small = up_to(real_small, 16)
    split = crops * pad_big
    rows = split + pad_small
    sizes = (crops, len_big, pad_big, slots_all, len_small, pad_small)
    devices = lax.axis_size("dp")
    bits = devices.bit_length() - 1
    core = lax.axis_index("section")
    place = lax.axis_index("dp")
    where = jnp.stack([core, place]).astype(jnp.int32)
    first = core == 0

    def join(big, small):
        big = lax.dynamic_index_in_dim(big, core, 0, keepdims=False)
        small = lax.dynamic_index_in_dim(small, core, 0, keepdims=False)
        big = jnp.pad(big, ((0, 0), (0, pad_big - len_big), (0, 0))).reshape(split, width)
        small = jnp.pad(small.reshape(real_small, width), ((0, pad_small - real_small), (0, 0)))
        return jnp.concatenate([big, small])

    x0 = join(input_big, input_small)
    cotangent = join(cotangent_big, cotangent_small)
    counts = lax.dynamic_index_in_dim(small_counts, core, 0, keepdims=False)
    line = jnp.arange(rows, dtype=jnp.int32)
    spot = line - split
    slot_of = jnp.arange(slots * len_small, dtype=jnp.int32) // len_small
    small_keep = (slot_of[None, :] < counts[:, None]).astype(F32).reshape(real_small)
    keep = jnp.where(line < split, (line % pad_big < len_big).astype(F32), jnp.pad(small_keep, (split, pad_small - real_small)))
    keep = keep[:, None]

    vec_own = jnp.concatenate(
        [norm1_gain, norm1_bias, query_bias, value_bias, proj_bias, attn_scale, norm2_gain, norm2_bias, down_bias, mlp_scale, up_bias.reshape(-1, width)]
    )
    tables_own = jnp.concatenate([table_big[0], table_small[0]])
    vec_other, tables_other = swap(vec_own), swap(tables_own)
    qkv = (qkv_weight[0], swap(qkv_weight[0]))
    proj = (proj_weight[0], swap(proj_weight[0]))
    up = (up_weight[0], swap(up_weight[0]))
    down = (down_weight[0], swap(down_weight[0]))

    grids, lengths = (grid_big, grid_small), (len_big, len_small)
    entries_big = table_big.shape[1]
    base_big, base_small, corners_all = table_bases(where, tables_own, tables_other, grids, entries_big)
    layers = []
    for layer in range(2):
        vec = jnp.where(core == layer, vec_own, vec_other)
        ups = vec[10:].reshape(1, -1)
        joined = jnp.concatenate([vec[2:3], jnp.zeros_like(vec[2:3]), vec[3:4]], axis=1)
        layers.append((vec, ups, joined, corners_all[layer], base_big[layer], base_small[layer]))

    saved = []
    x = x0
    for layer in range(2):
        vec, ups, joined, corners, big, small = layers[layer]
        normed, projected = qkv_forward(layer, where, x, vec[0:1], vec[1:2], joined, *qkv)
        attended = attention_forward(projected, big, small, corners, sizes)
        made = mlp_forward(layer, where, attended, normed, x, keep, vec, ups, proj, up, down if layer == 0 else None)
        saved.append((x, projected) + tuple(made[:4]))
        if layer == 0:
            x, mlp0 = made[4:]

    rest = list(range(3, bits))
    orders = [([0, 1, 2] + rest, [1, 0, 2] + rest), ([2, 0, 1] + rest, [2, 1, 0] + rest)]

    def mlp_part(layer, g, mlp, after=()):
        slope, branch, middle = saved[layer][3:]
        return mlp_backward(layer, where, g, keep, layers[layer][0], slope, middle, branch, mlp, down, up, proj, after=after)

    def attention_part(layer, ga, after):
        _, _, _, corners, big, small = layers[layer]
        return attention_backward(where, saved[layer][1], ga, big, small, corners, sizes, after=after)

    def qkv_part(layer, gproj, gmid, after):
        return qkv_backward(layer, where, gproj, saved[layer][0], gmid, layers[layer][0][0:1], *qkv, after=after)

    lefts = [(saved[layer][2], swap(saved[layer][2])) for layer in range(2)]
    came_y0 = hand_over(saved[1][0], 0)

    kept, sent, ga, gmid, vecs2_1, ups_1 = mlp_part(1, cotangent, None, (lefts[0][1], came_y0))
    right = (kept, swap(sent))
    gproj, kept, sent, fold_big1, fold_small1, qv_1 = attention_part(1, ga, (ups_1,))
    blocks = (kept, swap(sent))
    made = weight_grad(where, orders, NAMES[:2], lefts[1], right, blocks, 14 * 10**9, (qv_1,))
    most1 = Scatter(made, orders)
    gx1, vecs1_1 = qkv_part(1, gproj, gmid, made[:1])
    came_gx1 = hand_over(gx1, 1)
    made = weight_grad(where, orders, NAMES[2:], lefts[1], right, blocks, 7 * 10**9, (vecs1_1,))
    last1 = Scatter(made, orders)

    kept, sent, ga, gmid, vecs2_0, ups_0 = mlp_part(0, gx1, mlp0, tuple(made[:1]) + (came_gx1,))
    right = (kept, swap(sent))
    all1, token = join_groups([most1, last1], (ups_0,))
    gproj, kept, sent, fold_big0, fold_small0, qv_0 = attention_part(0, ga, (token,))
    blocks = (kept, swap(sent))
    token = advance([all1], (qv_0,))
    made = weight_grad(where, orders, NAMES[:2], lefts[0], right, blocks, 14 * 10**9, (token,))
    most0 = Scatter(made, orders)
    token = advance([all1], made[:1])
    gx0, vecs1_0 = qkv_part(0, gproj, gmid, (token,))
    came_gx0 = hand_over(gx0, 0)
    made = weight_grad(where, orders, NAMES[2:], lefts[0], right, blocks, 7 * 10**9, (vecs1_0,))
    last0 = Scatter(made, orders)
    token = advance([all1], tuple(made[:1]) + (came_gx0,))
    y1, scale_1 = down_forward(1, where, saved[1][2], saved[1][5], keep, layers[1][0], *down, upstream=cotangent, after=(token,))
    came_y1 = hand_over(y1, 1)

    def by_line(zero, one):
        both = jnp.pad(jnp.stack([zero, one]), ((0, 0), (0, HEAD_ROWS - HEADS), (0, 0), (0, 0)))
        return jnp.transpose(both, (2, 0, 1, 3)).reshape(zero.shape[1], 2 * HEAD_ROWS, -1)

    folded = table_folds(by_line(fold_big0, fold_big1), by_line(fold_small0, fold_small1), grids, lengths, (scale_1,))
    flat = gather_vectors(
        folded, [(vecs1_0, qv_0, vecs2_0, vecs2_0[5:6], ups_0), (vecs1_1, qv_1, vecs2_1, scale_1, ups_1)]
    )
    flat = Total(flat, bits)
    token = advance([most0], (folded,))
    layer_big, layer_small = arrange_rows(where, (saved[1][0], y1), (came_y0, came_y1), sizes, (token,))
    token = advance([last0, flat], (layer_small[0, 0, 0, :8, :128],))
    grad_big, grad_small = arrange_rows(where, (gx0, gx1), (came_gx0, came_gx1), sizes, (token,))
    token = advance([most0], (grad_small[0, 0, 0, :8, :128],))
    token = advance([last0, flat], (token,))
    while any(group.result is None for group in (flat, most0, last0, all1)):
        token = advance([most0, all1], (token,))
        token = advance([last0, flat], (token,))
    flat = flat.result

    sums = [[(NAMES[:2], most0.result), (NAMES[2:], last0.result)], [(NAMES, all1.result)]]
    came = [[(names, hand_over(item, layer)) for names, item in sums[layer]] for layer in range(2)]
    block = width // devices
    hidden = up_bias.shape[1]
    grad_down, grad_up, grad_proj, grad_qkv = arrange_grads(where, sums, came, block, width, hidden)

    small = arrange_small(where, flat, grids, (entries_big, table_small.shape[1]), width, block, hidden // width, 10)
    grad_up_bias, grad_table_big, grad_table_small = small[10:]

    def vector(row):
        return small[row]

    return (
        layer_big,
        layer_small,
        grad_big,
        grad_small,
        vector(0),
        vector(1),
        grad_qkv,
        vector(2),
        vector(3),
        grad_table_big,
        grad_table_small,
        grad_proj,
        vector(4),
        vector(5),
        vector(6),
        vector(7),
        grad_up,
        grad_up_bias,
        grad_down,
        vector(8),
        vector(9),
    )


def solution(mesh):
    row = P("section", None)
    whole = P("section", None, None)
    dp4 = P(None, "dp", None, None)
    in_specs = (dp4, dp4, P(None, "dp"), dp4, dp4, row, row, whole, row, row, whole, whole, whole, row, row, row, row, whole, row, whole, row, row)
    out5 = P("section", None, "dp", None, None)
    vec = P("section", "dp")
    mat = P("section", "dp", None)
    out_specs = (out5, out5, out5, out5, vec, vec, mat, vec, vec, whole, whole, mat, vec, vec, vec, vec, mat, vec, mat, vec, vec)
    return jax.shard_map(body, mesh=mesh, in_specs=in_specs, out_specs=out_specs, check_vma=False)
```

```python
import math

import jax
import jax.numpy as jnp
from jax import lax
from jax.experimental import pallas as pl
from jax.experimental.pallas import tpu as pltpu
from jax.sharding import PartitionSpec as P

HEADS = 12
EPS = 1e-06
LOW = -1e30
MIB = 1024 * 1024
VMEM_BYTES = 44 * MIB
COST = 0.4
SMALL = 10**8
LATE = 4 * 10**9
F32 = jnp.float32
BF16 = jnp.bfloat16
V = pl.BlockSpec(memory_space=pltpu.VMEM)
S = pl.BlockSpec(memory_space=pltpu.SMEM)
H = pl.BlockSpec(memory_space=pltpu.HBM)


def up_to(value, multiple):
    return -(-value // multiple) * multiple


def mm(left, right):
    return jnp.dot(left, right, preferred_element_type=F32)


def mm_back(left, right):
    return lax.dot_general(left, right, (((1,), (1,)), ((), ())), preferred_element_type=F32)


def mm_outer(left, right):
    return lax.dot_general(left, right, (((0,), (0,)), ((), ())), preferred_element_type=F32)


def norm_parts(values):
    centre = values - jnp.mean(values, axis=-1, keepdims=True)
    spread = jnp.mean(centre * centre, axis=-1, keepdims=True)
    scale = lax.rsqrt(spread + EPS)
    return centre * scale, scale


def norm_back(upstream, values, gain):
    unit, scale = norm_parts(values)
    scaled = upstream * gain
    first = jnp.mean(scaled, axis=-1, keepdims=True)
    second = jnp.mean(scaled * unit, axis=-1, keepdims=True)
    going = scale * (scaled - first - unit * second)
    return (
        going,
        jnp.sum(upstream * unit, axis=0, keepdims=True),
        jnp.sum(upstream, axis=0, keepdims=True),
    )


def gelu_parts(x):
    raised = jnp.exp(-0.5 * x * x)
    t = 1.0 / (1.0 + (0.3275911 * math.sqrt(0.5)) * jnp.abs(x))
    poly = t * (
        0.127414796
        + t * (-0.142248368 + t * (0.7107068705 + t * (-0.7265760135 + t * 0.5307027145)))
    )
    half = poly * raised
    phi = jnp.where(x >= 0, 1.0 - half, half)
    return x * phi, phi + x * (raised * (1.0 / math.sqrt(2.0 * math.pi)))


def column_cuts(width, parts):
    step = width // parts
    return [(slice(None), pl.ds(i * step, step)) for i in range(parts)]


def row_cuts(height, parts):
    step = height // parts
    return [(pl.ds(i * step, step), slice(None)) for i in range(parts)]


def fetch_start(mine, own, other, buffer, sems, cuts):
    for i, cut in enumerate(cuts):

        @pl.when(mine)
        def _():
            pltpu.make_async_copy(own.at[cut], buffer.at[cut], sems.at[i]).start()

        @pl.when(jnp.logical_not(mine))
        def _():
            pltpu.make_async_copy(other.at[cut], buffer.at[cut], sems.at[i]).start()


def fetch_wait(own, buffer, sems, cuts, i):
    pltpu.make_async_copy(own.at[cuts[i]], buffer.at[cuts[i]], sems.at[i]).wait()


def size_of(item):
    return math.prod(item.shape) * jnp.dtype(item.dtype).itemsize


ANY = pl.BlockSpec(memory_space=pl.ANY)


def after_spec(item):
    return V if size_of(item) < 65536 else ANY if size_of(item) < 2 * MIB else H


def kernel_call(body, ins, outs, scratch, args, flops, after=(), out_specs=None, through=()):
    specs = list(ins) + [after_spec(item) for item in after] + [H] * len(through)
    out_specs = list(out_specs or [V] * len(outs)) + [H] * len(through)
    outs = list(outs) + [shape(item.shape, item.dtype) for item in through]
    count, given, made = len(args), len(specs), len(outs)

    def inner(*refs):
        body(*refs[:count], *refs[given : given + made - len(through)], *refs[given + made :])

    args = tuple(args) + tuple(after) + tuple(through)
    return pl.pallas_call(
        inner,
        in_specs=specs,
        out_specs=out_specs,
        out_shape=[pltpu.HBM(o.shape, o.dtype) if spec is H else o for o, spec in zip(outs, out_specs)],
        scratch_shapes=scratch,
        input_output_aliases={given - len(through) + n: made - len(through) + n for n in range(len(through))},
        compiler_params=pltpu.CompilerParams(vmem_limit_bytes=VMEM_BYTES),
        cost_estimate=pl.CostEstimate(flops=int(flops / COST), bytes_accessed=1024, transcendentals=0),
    )(*in_hbm(args, specs))


def in_hbm(args, specs):
    return [pltpu.with_memory_space_constraint(a, pltpu.HBM) if spec is H else a for a, spec in zip(args, specs)]


def shape(dims, kind):
    return jax.ShapeDtypeStruct(dims, kind)


def qkv_forward(layer, core, x, gain, shift, joined, own, other, after=(), through=()):
    rows, width = x.shape
    triple = own.shape[1]
    cuts = column_cuts(triple, 3)

    def body(core_ref, x_ref, gain_ref, shift_ref, joined_ref, own_ref, other_ref, normed_ref, proj_ref, buf, sems):
        mine = core_ref[0] == layer
        fetch_start(mine, own_ref, other_ref, buf, sems, cuts)
        unit, _ = norm_parts(x_ref[...].astype(F32))
        normed_ref[...] = (unit * gain_ref[...] + shift_ref[...]).astype(BF16)
        for i in range(3):
            fetch_wait(own_ref, buf, sems, cuts, i)

        def step(i, carry):
            cols = pl.ds(pl.multiple_of(i * width, width), width)
            proj_ref[:, cols] = (mm(normed_ref[...], buf[:, cols]) + joined_ref[:, cols]).astype(BF16)
            return carry

        lax.fori_loop(0, 3, step, 0)

    return kernel_call(
        body,
        [S, V, V, V, V, H, H],
        [shape((rows, width), BF16), shape((rows, triple), BF16)],
        [pltpu.VMEM((width, triple), BF16), pltpu.SemaphoreType.DMA((3,))],
        (core, x, gain, shift, joined, own, other),
        5 * 10**9,
        after=after,
        through=through,
    )


def build_bias(base, out_ref, block_ref, grid, corner, crops, length, block_rows):
    lanes = base.shape[1]
    head_patch, patch_head, head_head = corner
    lane = lax.broadcasted_iota(jnp.int32, (block_rows, 256), 1)
    line = lax.broadcasted_iota(jnp.int32, (block_rows, 256), 0)
    first = jnp.where(lane == 0, head_head, head_patch)
    block_ref[...] = jnp.where(lane >= length, LOW, first)
    small = lane[:grid]
    for r in range(grid):
        off = (grid - 1 - r) * grid
        moved = base if off == 0 else pltpu.roll(base, lanes - off, 1)
        moved = moved[:grid, :256]
        value = jnp.where(small == 0, patch_head, jnp.where(small >= length, LOW, moved))
        block_ref[pl.ds(1 + grid * r, grid), :] = value
    if crops == 1:
        return
    out_ref[...] = jnp.full(out_ref.shape, LOW, F32)
    for s in range(crops):
        value = block_ref[pl.ds(0, length), :]
        if s:
            value = pltpu.roll(value, s * length, 1)
        out_ref[pl.ds(s * length, length), :] = value


def pair_bias(pair, corner_ref, bb_ref, bs_ref, big, block, small, sizes):
    crops, len_big, pad_big, slots, len_small, pad_small = sizes
    grid_big, grid_small = math.isqrt(len_big - 1), math.isqrt(len_small - 1)
    for h in range(2):
        head = pair * 2 + h
        build_bias(bb_ref[head], big.at[pl.ds(h * pad_big, pad_big)], big.at[pl.ds(h * pad_big, pad_big)], grid_big, [corner_ref[0, i, head] for i in range(3)], 1, len_big, pad_big)
        build_bias(bs_ref[head], small.at[pl.ds(h * pad_small, pad_small)], block, grid_small, [corner_ref[1, i, head] for i in range(3)], slots, len_small, block.shape[0])


def two_heads(value):
    lane = lax.broadcasted_iota(jnp.int32, (1, 128), 1)
    return jnp.concatenate([jnp.where(lane < 64, value, 0), jnp.where(lane >= 64, value, 0)], axis=0)


def one_line(value):
    count = value.shape[0] // 2
    lane = lax.broadcasted_iota(jnp.int32, (1, 128), 1)
    return jnp.where(lane < 64, value[:count], value[count:])


def attention_probs(scores):
    raised = jnp.exp(scores - jnp.max(scores, axis=-1, keepdims=True))
    return raised * (1.0 / jnp.sum(raised, axis=-1, keepdims=True))


def attention_parts(sizes):
    crops, _, pad_big, _, _, pad_small = sizes
    return [(c * pad_big, pad_big, True) for c in range(crops)] + [(crops * pad_big, pad_small, False)]


def bias_scratch(sizes):
    _, _, pad_big, _, len_small, pad_small = sizes
    return [
        pltpu.VMEM((2 * pad_big, 256), F32),
        pltpu.VMEM((up_to(len_small, 8), 256), F32),
        pltpu.VMEM((2 * pad_small, 256), F32),
    ]


def attention_forward(projected, base_big, base_small, corners, sizes, after=()):
    rows, triple = projected.shape
    width = triple // 3
    pairs = HEADS // 2
    parts = attention_parts(sizes)

    def body(corner_ref, proj_ref, bb_ref, bs_ref, out_ref, big, block, small):
        def step(pair, carry):
            pair_bias(pair, corner_ref, bb_ref, bs_ref, big, block, small, sizes)
            q, k, v = [pl.ds(pl.multiple_of(n * width + pair * 128, 128), 128) for n in range(3)]
            scores = []
            for start, count, is_big in parts:
                part = pl.ds(start, count)
                bias = big if is_big else small
                scores.append(mm_back(two_heads(proj_ref[part, q] * 0.125), proj_ref[part, k]) + bias[:, :count])
            probs = [attention_probs(item).astype(BF16) for item in scores]
            for (start, count, is_big), item in zip(parts, probs):
                part = pl.ds(start, count)
                out_ref[part, q] = one_line(mm(item, proj_ref[part, v])).astype(BF16)
            return carry

        lax.fori_loop(0, pairs, step, 0)

    return kernel_call(
        body,
        [S, V, V, V],
        [shape((rows, width), BF16)],
        bias_scratch(sizes),
        (corners, projected, base_big, base_small),
        10**10,
        after=after,
    )[0]


FF_STEP = 512


def saved_cuts(width, hidden):
    return [(0, hidden), (hidden, width), (hidden + width, width), (hidden + 2 * width, width)]


def mlp_forward(layer, core, attended, normed, x, keep, vec, up_bias, proj, up, down=None):
    rows, width = x.shape
    hidden = up[0].shape[1]
    count = hidden // FF_STEP
    cuts = [(slice(None), slice(None))]
    up_cuts = column_cuts(hidden, count)
    down_cuts = row_cuts(hidden, 2)
    spans = saved_cuts(width, hidden)
    total_cols = hidden + 3 * width
    weights = proj + up + (down or ())

    def body(core_ref, att_ref, n1_ref, x_ref, keep_ref, vec_ref, bias_ref, *refs):
        weight_refs, refs = refs[: len(weights)], refs[len(weights) :]
        left_ref, slope_ref, branch_ref, middle_ref, refs = refs[0], refs[1], refs[2], refs[3], refs[4:]
        if down:
            y_ref, mlp_ref, refs = refs[0], refs[1], refs[2:]
        buf, buf_up, hid, slp, br, mid, n2, sems, sems_up, out_sems = refs[:10]
        mine = core_ref[0] == layer
        fetch_start(mine, weight_refs[0], weight_refs[1], buf, sems, cuts)
        fetch_start(mine, weight_refs[2], weight_refs[3], buf_up, sems_up, up_cuts)
        if down:
            buf_down, mlp_buf, sems_down = refs[10:]
            fetch_start(mine, weight_refs[4], weight_refs[5], buf_down, sems_down, down_cuts)
        going = []

        def send(source, target):
            copy = pltpu.make_async_copy(source, target, out_sems.at[len(going)])
            copy.start()
            going.append(copy)

        def span(n):
            return left_ref.at[:, pl.ds(*spans[n])]

        send(att_ref, span(2))
        send(n1_ref, span(3))
        fetch_wait(weight_refs[0], buf, sems, cuts, 0)
        branch = mm(att_ref[...], buf[...]) + vec_ref[4:5, :]
        br[...] = branch.astype(BF16)
        middle = x_ref[...].astype(F32) + vec_ref[5:6, :] * branch
        mid[...] = middle
        unit, _ = norm_parts(middle)
        n2[...] = (unit * vec_ref[6:7, :] + vec_ref[7:8, :]).astype(BF16)
        send(br, branch_ref)
        send(mid, middle_ref)
        send(n2, span(1))
        for i in range(count):
            fetch_wait(weight_refs[2], buf_up, sems_up, up_cuts, i)

        def pre_of(i):
            cols = pl.ds(i * FF_STEP, FF_STEP)
            return mm(n2[...], buf_up[:, cols]) + bias_ref[:, cols]

        pre = pre_of(0)
        for i in range(count):
            following = pre_of(i + 1) if i + 1 < count else None
            value, slope = gelu_parts(pre)
            cols = pl.ds(i * FF_STEP, FF_STEP)
            hid[:, cols] = value.astype(BF16)
            slp[:, cols] = slope.astype(BF16)
            pre = following
            if i % 2 == 1:
                both = pl.ds((i - 1) * FF_STEP, 2 * FF_STEP)
                send(hid.at[:, both], left_ref.at[:, both])
                send(slp.at[:, both], slope_ref.at[:, both])
        if down:
            for i in range(2):
                fetch_wait(weight_refs[4], buf_down, sems_down, down_cuts, i)
            total = mm(hid[...], buf_down[...]) + vec_ref[8:9, :]
            mlp_buf[...] = total.astype(BF16)
            send(mlp_buf, mlp_ref)
            y_ref[...] = ((mid[...] + vec_ref[9:10, :] * total) * keep_ref[...]).astype(BF16)
        for copy in going:
            copy.wait()

    outs = [shape((rows, total_cols), BF16), shape((rows, hidden), BF16), shape((rows, width), BF16), shape((rows, width), F32)]
    out_specs = [H] * 4
    scratch = [
        pltpu.VMEM((width, width), BF16),
        pltpu.VMEM((width, hidden), BF16),
        pltpu.VMEM((rows, hidden), BF16),
        pltpu.VMEM((rows, hidden), BF16),
        pltpu.VMEM((rows, width), BF16),
        pltpu.VMEM((rows, width), F32),
        pltpu.VMEM((rows, width), BF16),
        pltpu.SemaphoreType.DMA((1,)),
        pltpu.SemaphoreType.DMA((count,)),
        pltpu.SemaphoreType.DMA((6 + count,)),
    ]
    if down:
        outs += [shape((rows, width), BF16), shape((rows, width), BF16)]
        out_specs += [V, H]
        scratch += [
            pltpu.VMEM((hidden, width), BF16),
            pltpu.VMEM((rows, width), BF16),
            pltpu.SemaphoreType.DMA((2,)),
        ]
    return kernel_call(
        body,
        [S, V, V, V, V, V, V] + [H] * len(weights),
        outs,
        scratch,
        (core, attended, normed, x, keep, vec, up_bias) + weights,
        (17 if down else 13) * 10**9,
        out_specs=out_specs,
    )


def down_forward(layer, core, left, middle, keep, vec, own, other, upstream, after=()):
    rows, width = middle.shape
    depth = own.shape[0]
    parts = 4
    cuts = row_cuts(depth, parts)
    step = depth // parts

    def body(core_ref, left_ref, middle_ref, keep_ref, vec_ref, g_ref, own_ref, other_ref, y_ref, sum_ref, buf, hid, mid, sems, in_sems):
        fetch_start(core_ref[0] == layer, own_ref, other_ref, buf, sems, cuts)
        copies = [
            pltpu.make_async_copy(left_ref.at[:, pl.ds(i * step, step)], hid.at[:, pl.ds(i * step, step)], in_sems.at[i])
            for i in range(parts)
        ] + [pltpu.make_async_copy(middle_ref, mid, in_sems.at[parts])]
        for copy in copies:
            copy.start()
        total = vec_ref[8:9, :]
        for i in range(parts):
            fetch_wait(own_ref, buf, sems, cuts, i)
            copies[i].wait()
            part = pl.ds(i * step, step)
            total = total + mm(hid[:, part], buf[part, :])
        copies[parts].wait()
        sum_ref[...] = jnp.sum(g_ref[...].astype(F32) * keep_ref[...] * total, axis=0, keepdims=True)
        y_ref[...] = ((mid[...] + vec_ref[9:10, :] * total) * keep_ref[...]).astype(BF16)

    return kernel_call(
        body,
        [S, H, H, V, V, V, H, H],
        [shape((rows, width), BF16), shape((1, width), F32)],
        [
            pltpu.VMEM((depth, width), BF16),
            pltpu.VMEM((rows, depth), BF16),
            pltpu.VMEM((rows, width), F32),
            pltpu.SemaphoreType.DMA((parts,)),
            pltpu.SemaphoreType.DMA((parts + 1,)),
        ],
        (core, left, middle, keep, vec, upstream, own, other),
        9 * 10**9,
        after=after,
    )


def send_halves(me, copies, pair, source, outs, sems):
    keep, send = outs
    for half in range(2):

        @pl.when(me == half)
        def _():
            pltpu.make_async_copy(source(half), keep, sems.at[pair]).start()
            pltpu.make_async_copy(source(1 - half), send, sems.at[pair + 1]).start()

    copies.append(pltpu.make_async_copy(source(0), keep, sems.at[pair]))
    copies.append(pltpu.make_async_copy(source(1), send, sems.at[pair + 1]))


def mlp_backward(layer, core, upstream, keep, vec, slope, middle, branch, mlp, down, up, proj, after=(), through=()):
    rows, width = middle.shape
    depth = slope.shape[1]
    count = depth // FF_STEP
    half_cols, half_width = depth // 2, width // 2
    wide = half_cols + 2 * half_width
    extra = () if mlp is None else (mlp,)
    down_cuts, up_cuts = row_cuts(depth, count), column_cuts(depth, count)
    cuts = [(slice(None), slice(None))]

    def body(core_ref, g_ref, keep_ref, vec_ref, slope_ref, middle_ref, branch_ref, *refs):
        mlp_refs, refs = refs[: len(extra)], refs[len(extra) :]
        od, td, ou, tu, op, tp, keep_out, send_out, ga_ref, gmid_ref, vecs_ref, ups_ref, low, back_buf, slp, mid, br, mlp_buf, bd, bu, bp, sd, su, sp, sin, sout = refs
        me = core_ref[0]
        mine = me == layer
        fetch_start(mine, od, td, bd, sd, down_cuts)
        coming = [
            pltpu.make_async_copy(source, target, sin.at[n])
            for n, (source, target) in enumerate([(middle_ref, mid), (branch_ref, br)] + [(r, mlp_buf) for r in mlp_refs])
        ]
        slopes = []
        for n in range(count // 2):
            part = pl.ds(n * 2 * FF_STEP, 2 * FF_STEP)
            slopes.append(pltpu.make_async_copy(slope_ref.at[:, part], slp.at[:, part], sin.at[3 + n]))
            slopes[n].start()
        fetch_start(mine, ou, tu, bu, su, up_cuts)
        for copy in coming:
            copy.start()
        fetch_start(mine, op, tp, bp, sp, cuts)
        gm = (vec_ref[9:10, :] * (g_ref[...].astype(F32) * keep_ref[...])).astype(BF16)
        low[...] = gm
        for half in range(2):
            back_buf[half, :, :half_width] = gm[:, half * half_width : (half + 1) * half_width]
        vecs_ref[...] = jnp.zeros_like(vecs_ref)
        vecs_ref[4:5, :] = jnp.sum(gm.astype(F32), axis=0, keepdims=True)
        for i in range(count):
            if i % 2 == 0:
                fetch_wait(od, bd, sd, down_cuts, i)
                fetch_wait(od, bd, sd, down_cuts, i + 1)
                slopes[i // 2].wait()
            cols = pl.ds(i * FF_STEP, FF_STEP)
            gp = (mm_back(low[...], bd[cols, :]) * slp[:, cols].astype(F32)).astype(BF16)
            back_buf[2 * i // count, :, pl.ds(half_width + (i * FF_STEP) % half_cols, FF_STEP)] = gp
            ups_ref[:, cols] = jnp.sum(gp.astype(F32), axis=0, keepdims=True)
        for i in range(count):
            fetch_wait(ou, bu, su, up_cuts, i)
        middle_cols = slice(half_width, half_width + half_cols)
        back = mm_back(back_buf[0, :, middle_cols], bu[:, :half_cols]) + mm_back(back_buf[1, :, middle_cols], bu[:, half_cols:])
        for copy in coming:
            copy.wait()
        going, gain, shift = norm_back(back, mid[...], vec_ref[6:7, :])
        g = g_ref[...].astype(F32) * keep_ref[...]
        gmid = g + going
        gmid_ref[...] = gmid
        gb = (vec_ref[5:6, :] * gmid).astype(BF16)
        low[...] = gb
        for half in range(2):
            back_buf[half, :, half_width + half_cols :] = gb[:, half * half_width : (half + 1) * half_width]
        copies = []
        send_halves(me, copies, 0, lambda half: back_buf.at[half], (keep_out, send_out), sout)
        vecs_ref[0:1, :] = gain
        vecs_ref[1:2, :] = shift
        vecs_ref[2:3, :] = jnp.sum(gmid * br[...].astype(F32), axis=0, keepdims=True)
        vecs_ref[3:4, :] = jnp.sum(gb.astype(F32), axis=0, keepdims=True)
        if extra:
            vecs_ref[5:6, :] = jnp.sum(g * mlp_buf[...].astype(F32), axis=0, keepdims=True)
        fetch_wait(op, bp, sp, cuts, 0)
        ga_ref[...] = mm_back(low[...], bp[...]).astype(BF16)
        for copy in copies:
            copy.wait()

    return kernel_call(
        body,
        [S, V, V, V, H, H, H] + [H] * (len(extra) + 6),
        [
            shape((rows, wide), BF16),
            shape((rows, wide), BF16),
            shape((rows, width), BF16),
            shape((rows, width), F32),
            shape((8, width), F32),
            shape((1, depth), F32),
        ],
        [
            pltpu.VMEM((rows, width), BF16),
            pltpu.VMEM((2, rows, wide), BF16),
            pltpu.VMEM((rows, depth), BF16),
            pltpu.VMEM((rows, width), F32),
            pltpu.VMEM((rows, width), BF16),
            pltpu.VMEM((rows, width), BF16),
            pltpu.VMEM((depth, width), BF16),
            pltpu.VMEM((width, depth), BF16),
            pltpu.VMEM((width, width), BF16),
            pltpu.SemaphoreType.DMA((count,)),
            pltpu.SemaphoreType.DMA((count,)),
            pltpu.SemaphoreType.DMA((1,)),
            pltpu.SemaphoreType.DMA((3 + count // 2,)),
            pltpu.SemaphoreType.DMA((2,)),
        ],
        (core, upstream, keep, vec, slope, middle, branch) + extra + down + up + proj,
        SMALL,
        after=after,
        out_specs=[H, H, V, V, V, V],
        through=through,
    )


def attention_backward(core, projected, upstream, base_big, base_small, corners, sizes, after=()):
    rows, triple = projected.shape
    width = triple // 3
    pairs = HEADS // 2
    crops, len_big, pad_big, slots, len_small, pad_small = sizes
    grid_big, grid_small = math.isqrt(len_big - 1), math.isqrt(len_small - 1)
    half = 3 * pairs // 2

    parts = attention_parts(sizes)

    def body(core_ref, corner_ref, proj_ref, g_ref, bb_ref, bs_ref, gproj_ref, keep_out, send_out, tb_ref, ts_ref, sums_ref, big, block, small, dbig, dsmall, dblock, sout):
        dbig[...] = jnp.zeros_like(dbig)
        dsmall[...] = jnp.zeros_like(dsmall)
        dblock[...] = jnp.zeros_like(dblock)
        tb_ref[...] = jnp.zeros_like(tb_ref)
        ts_ref[...] = jnp.zeros_like(ts_ref)

        def step(pair, carry):
            pair_bias(pair, corner_ref, bb_ref, bs_ref, big, block, small, sizes)

            q, k, v = [pl.ds(pl.multiple_of(n * width + pair * 128, 128), 128) for n in range(3)]
            places = [which * pairs + pair for which in range(3)]
            scores, gprs = [], []
            for start, count, is_big in parts:
                part = pl.ds(start, count)
                bias = big if is_big else small
                scores.append(mm_back(two_heads(proj_ref[part, q] * 0.125), proj_ref[part, k]) + bias[:, :count])
                gprs.append(mm_back(two_heads(g_ref[part, q]), proj_ref[part, v]))
            probs = [attention_probs(item) for item in scores]
            gss = [(p * (gpr - jnp.sum(p * gpr, axis=-1, keepdims=True))).astype(BF16) for p, gpr in zip(probs, gprs)]
            for n, ((start, count, is_big), p, gs) in enumerate(zip(parts, probs, gss)):
                part = pl.ds(start, count)
                dref = dbig if is_big else dsmall
                if n == 0 or not is_big:
                    dref[:, :count] = gs.astype(F32)
                else:
                    dref[:, :count] += gs.astype(F32)
                gproj_ref[places[0], part, :] = (one_line(mm(gs, proj_ref[part, k])) * 0.125).astype(BF16)
                gproj_ref[places[1], part, :] = mm_outer(gs, two_heads(proj_ref[part, q] * 0.125)).astype(BF16)
                gproj_ref[places[2], part, :] = mm_outer(p.astype(BF16), two_heads(g_ref[part, q])).astype(BF16)


            for h in range(2):
                hbig, hsmall = dbig.at[pl.ds(h * pad_big, pad_big)], dsmall.at[pl.ds(h * pad_small, pad_small)]

                def fold(dref, grid, length, out_ref):
                    lanes = out_ref.shape[2]
                    wide = lax.broadcasted_iota(jnp.int32, (grid, 256), 1)
                    inside = (wide > 0) & (wide < length)
                    total = jnp.zeros((grid, lanes), F32)
                    for r in range(grid):
                        value = jnp.where(inside, dref[pl.ds(1 + grid * r, grid), :], 0)
                        if lanes > 256:
                            value = jnp.concatenate([value, jnp.zeros((grid, lanes - 256), F32)], axis=1)
                        off = (grid - 1 - r) * grid
                        total = total + (value if off == 0 else pltpu.roll(value, off, 1))
                    out_ref[pair * 2 + h, :grid, :] = total
                    line = lax.broadcasted_iota(jnp.int32, (length, 256), 0)
                    spot = lax.broadcasted_iota(jnp.int32, (length, 256), 1)
                    value = jnp.where(spot < length, dref[pl.ds(0, length), :], 0)
                    out_ref[pair * 2 + h, grid : grid + 1, :256] = value[0:1, :]
                    out_ref[pair * 2 + h, grid + 1 : grid + 2, :256] = jnp.sum(jnp.where(line > 0, value, 0), axis=0, keepdims=True)

                fold(hbig, grid_big, len_big, tb_ref)
                total = hsmall[pl.ds(0, len_small), :]
                for s in range(1, slots):
                    total = total + pltpu.roll(hsmall[pl.ds(s * len_small, len_small), :], 256 - s * len_small, 1)
                dblock[pl.ds(0, len_small), :] = total
                fold(dblock, grid_small, len_small, ts_ref)
            for n, which in ((0, 0), (1, 2)):
                sums_ref[n : n + 1, q] = jnp.sum(gproj_ref[places[which]].astype(F32), axis=0, keepdims=True)
            return carry

        lax.fori_loop(0, pairs, step, 0)
        copies = []
        send_halves(core_ref[0], copies, 0, lambda n: gproj_ref.at[pl.ds(n * half, half)], (keep_out, send_out), sout)
        for copy in copies:
            copy.wait()

    return kernel_call(
        body,
        [S, S, V, V, V, V],
        [
            shape((2 * half, rows, 128), BF16),
            shape((half, rows, 128), BF16),
            shape((half, rows, 128), BF16),
            shape((HEADS, 16, 512), F32),
            shape((HEADS, 8, 256), F32),
            shape((2, width), F32),
        ],
        bias_scratch(sizes)
        + [
            pltpu.VMEM((2 * pad_big, 256), F32),
            pltpu.VMEM((2 * pad_small, 256), F32),
            pltpu.VMEM((up_to(len_small, 8), 256), F32),
            pltpu.SemaphoreType.DMA((2,)),
        ],
        (core, corners, projected, upstream, base_big, base_small),
        15 * 10**9,
        out_specs=[V, H, H, V, V, V],
        after=after,
    )


def qkv_backward(layer, core, gproj, x, gmid, gain, own, other, after=(), flops=10**8):
    rows, width = x.shape
    blocks = gproj.shape[0]
    triple = blocks * 128
    cuts = column_cuts(triple, 3)
    group = blocks // 3

    def body(core_ref, gproj_ref, x_ref, gmid_ref, gain_ref, own_ref, other_ref, gx_ref, vecs_ref, buf, acc, sems):
        me = core_ref[0]
        fetch_start(me == layer, own_ref, other_ref, buf, sems, cuts)
        for i in range(3):
            fetch_wait(own_ref, buf, sems, cuts, i)
            joined = jnp.concatenate([gproj_ref[n] for n in range(i * group, (i + 1) * group)], axis=1)
            more = mm_back(joined, buf[:, pl.ds(i * width, width)])
            if i == 0:
                acc[...] = more
            else:
                acc[...] += more
        going, gain_sum, shift_sum = norm_back(acc[...], x_ref[...].astype(F32), gain_ref[...])
        gx_ref[...] = (gmid_ref[...] + going).astype(BF16)
        vecs_ref[0:1, :] = gain_sum
        vecs_ref[1:2, :] = shift_sum

    return kernel_call(
        body,
        [S, V, V, V, V, H, H],
        [shape((rows, width), BF16), shape((2, width), F32)],
        [
            pltpu.VMEM((width, triple), BF16),
            pltpu.VMEM((rows, width), F32),
            pltpu.SemaphoreType.DMA((3,)),
        ],
        (core, gproj, x, gmid, gain, own, other),
        flops,
        after=after,
    )


def place_of(relative, order):
    place = 0
    for bit in order:
        place = place * 2 + ((relative >> bit) & 1)
    return place


def piece_plan(names, tiles, quarters):
    counts = [
        {name: tiles[name] // 3 * (2 - p) * (quarters if name == "down" else 1) for name in names} for p in range(2)
    ]
    bases = [{name: sum(counts[p][other] for other in names[:n]) for n, name in enumerate(names)} for p in range(2)]
    return counts, bases, [sum(count.values()) for count in counts]


def weight_grad(where, orders, names, left, right, blocks, flops, after=()):
    devices = 1 << len(orders[0][0])
    pieces = len(orders)
    rows, total_cols = left[0].shape
    width = total_cols - 2 * right[0].shape[1]
    hidden = total_cols - 3 * width
    spans = dict(zip(("down", "up", "proj", "qkv"), saved_cuts(width, hidden)))
    backs = {"down": (0, width // 2), "up": (width // 2, hidden // 2), "proj": (width // 2 + hidden // 2, width // 2), "qkv": (0, 3 * width // 2)}
    block = width // devices
    tiles = {name: backs[name][1] // 128 for name in names}
    counts, bases, subs = piece_plan(names, tiles, hidden // width)
    half = devices // 2
    arrays = tuple(left) + tuple(right) + (tuple(blocks) if "qkv" in names else ())
    copies_needed = sum(2 * (hidden // width) + 2 if name == "down" else 2 + 2 * blocks[0].shape[0] if name == "qkv" else 4 for name in names)

    def body(where_ref, *refs):
        ins, refs = refs[: len(arrays)], refs[len(arrays) + len(after) :]
        outs, refs = refs[: 2 * pieces], refs[2 * pieces :]
        held, refs = refs[:pieces], refs[pieces:]
        lefts, refs = refs[: len(names)], refs[len(names) :]
        rights, refs = refs[: len(names)], refs[len(names) :]
        turned, sems, in_sems = refs
        me, first = where_ref[1], where_ref[0] == 0
        places = [
            [jnp.where(first, place_of(j ^ me, order[0]), place_of(j ^ me, order[1])) for j in range(devices)]
            for order in orders
        ]
        coming = {name: [] for name in names}
        used = 0

        def bring(name, source, target):
            nonlocal used
            copy = pltpu.make_async_copy(source, target, in_sems.at[used])
            copy.start()
            used += 1
            coming[name].append(copy)

        for n, name in enumerate(names):
            for side in range(2):
                lines = pl.ds(side * rows, rows)
                if name == "qkv":
                    for t in range(tiles[name]):
                        bring(name, ins[4 + side].at[t], rights[n].at[lines, pl.ds(t * 128, 128)])
                else:
                    bring(name, ins[2 + side].at[:, pl.ds(*backs[name])], rights[n].at[lines, :])
            low, size = spans[name]
            for start in range(0, size, width):
                for side in range(2):
                    lines = pl.ds(side * rows, rows)
                    bring(name, ins[side].at[:, pl.ds(low + start, width)], lefts[n].at[lines, pl.ds(start, width)])

        def put(name, value, line, tile, extra=0):
            large = tiles[name] // 3 * 2
            p, at = (0, tile) if tile < large else (1, tile - large)
            held[p][places[p][line], bases[p][name] + at * (hidden // width if name == "down" else 1) + extra] = value

        def copies(p):
            return [
                pltpu.make_async_copy(held[p].at[pl.ds(0, half)], outs[2 * p], sems.at[2 * p]),
                pltpu.make_async_copy(held[p].at[pl.ds(half, half)], outs[2 * p + 1], sems.at[2 * p + 1]),
            ]

        for n, name in enumerate(names):
            waits = coming[name]
            final = n + 1 == len(names)
            if name == "down":
                for copy in waits[:2]:
                    copy.wait()
                cols = backs[name][1]
                turned[:cols, :] = rights[n][...].T
                lines = block * (hidden // width)
                for c in range(hidden // width):
                    for copy in waits[2 + 2 * c : 4 + 2 * c]:
                        copy.wait()
                    value = mm(turned[:cols, :], lefts[n][:, pl.ds(c * width, width)]).astype(BF16).T
                    for j in range(width // block):
                        at = c * (width // block) + j
                        for t in range(tiles[name]):
                            put(name, value[j * block : (j + 1) * block, t * 128 : (t + 1) * 128], at // (hidden // width), t, at % (hidden // width))
                done = 0
            else:
                for copy in waits:
                    copy.wait()
                turned[...] = lefts[n][...].T
                done = 0
                for low in range(0, tiles[name], 4):
                    high = min(low + 4, tiles[name])
                    value = mm(turned[...], rights[n][:, low * 128 : high * 128])
                    for j in range(devices):
                        for t in range(low, high):
                            put(name, value[j * block : (j + 1) * block, (t - low) * 128 : (t - low + 1) * 128].astype(BF16), j, t)
                    while final and done < pieces and (tiles[name] // 3 * 2, tiles[name])[done] <= high:
                        for copy in copies(done):
                            copy.start()
                        done += 1
            if final:
                for p in range(done, pieces):
                    for copy in copies(p):
                        copy.start()
        for p in range(pieces):
            for copy in copies(p):
                copy.wait()

    outs = [shape((half, subs[p], block, 128), BF16) for p in range(pieces) for _ in range(2)]
    scratch = [pltpu.VMEM((devices, subs[p], block, 128), BF16) for p in range(pieces)]
    scratch += [pltpu.VMEM((2 * rows, spans[name][1]), BF16) for name in names]
    scratch += [pltpu.VMEM((2 * rows, backs[name][1]), BF16) for name in names]
    scratch += [pltpu.VMEM((width, 2 * rows), BF16)]
    specs = [S] + [H] * len(arrays) + [after_spec(item) for item in after]
    return pl.pallas_call(
        body,
        in_specs=specs,
        out_specs=[H] * (2 * pieces),
        out_shape=outs,
        scratch_shapes=scratch + [pltpu.SemaphoreType.DMA((2 * pieces,)), pltpu.SemaphoreType.DMA((copies_needed,))],
        compiler_params=pltpu.CompilerParams(vmem_limit_bytes=VMEM_BYTES),
        cost_estimate=pl.CostEstimate(flops=int(flops / COST), bytes_accessed=1024, transcendentals=0),
    )(*in_hbm((where, *arrays, *after), specs))


NAMES = ("down", "up", "proj", "qkv")


def add_stage(items, after, flops=10**9):
    args, outs, plan = [], [], []
    for item in items:
        kept, came, how = item
        if how == "joined":
            plan.append((how, len(args), len(kept), len(outs)))
            half = shape((kept[0].shape[0] // 2, sum(k.shape[1] for k in kept)) + kept[0].shape[2:], BF16)
            outs += [half, half]
            args += list(kept) + list(came)
        elif how == "last":
            plan.append((how, len(args), len(kept), len(outs)))
            outs.append(shape((sum(k.shape[1] for k in kept),) + kept[0].shape[2:], F32))
            args += list(kept) + list(came)
        else:
            plan.append((how, len(args), 1, len(outs)))
            if how == "halves":
                half = shape((kept.shape[0] // 2,) + kept.shape[1:], BF16)
                outs += [half, half]
            else:
                outs.append(shape(kept.shape, F32))
            args += [kept, came]

    def body(*refs):
        ins, results = refs[: len(args)], refs[len(args) :]
        for how, at, count, to in plan:
            if how == "last":
                low = 0
                for n in range(count):
                    high = low + ins[at + n].shape[1]
                    results[to][low:high] = ins[at + n][0].astype(F32) + ins[at + count + n][0].astype(F32)
                    low = high
            elif how == "joined":
                half, low = outs[to].shape[0], 0
                for n in range(count):
                    high = low + ins[at + n].shape[1]
                    for part in range(2):
                        cut = pl.ds(part * half, half)
                        value = ins[at + n][cut].astype(F32) + ins[at + count + n][cut].astype(F32)
                        results[to + part][:, low:high] = value.astype(BF16)
                    low = high
            elif how == "whole":
                results[to][...] = ins[at][...] + ins[at + 1][...]
            else:
                half = outs[to].shape[0]
                for n in range(2):
                    cut = pl.ds(n * half, half)
                    results[to + n][...] = (ins[at][cut].astype(F32) + ins[at + 1][cut].astype(F32)).astype(BF16)
        results[-1][...] = jnp.zeros((8, 128), F32)

    args = [pltpu.with_memory_space_constraint(a, pltpu.HBM) if size_of(a) > 500000 else a for a in args]
    made = kernel_call(body, [V] * len(args), outs + [shape((8, 128), F32)], [], tuple(args), flops, after=after)
    results = []
    for how, _, _, to in plan:
        results.append((made[to], made[to + 1]) if how in ("halves", "joined") else made[to])
    return results, made[-1]


class Scatter:
    def __init__(self, made, orders):
        self.keeps, self.sends, self.orders = list(made[0::2]), list(made[1::2]), orders
        self.step, self.result = 0, None
        self.launch()

    def launch(self):
        self.came = [
            across(send, [order[self.step] for order in both]) for send, both in zip(self.sends, self.orders)
        ]

    def items(self):
        if self.step + 1 == len(self.orders[0][0]):
            return [(self.keeps, self.came, "last")]
        return [(keep, came, "halves") for keep, came in zip(self.keeps, self.came)]

    def take(self, results):
        self.step += 1
        if self.step == len(self.orders[0][0]):
            self.result = results[0]
            return
        self.keeps, self.sends = [r[0] for r in results], [r[1] for r in results]
        self.launch()


class Total:
    def __init__(self, value, sent, bits):
        self.value, self.bits, self.step, self.result = value, bits, 0, None
        self.came = swap(sent)

    def items(self):
        return [(self.value, self.came, "whole")]

    def take(self, results):
        self.value = results[0]
        if self.step == self.bits:
            self.result = self.value
            return
        self.came = across(self.value, [self.step, self.step])
        self.step += 1


def join_groups(groups, after):
    pieces = len(groups[0].orders)
    items = [([g.keeps[p] for g in groups], [g.came[p] for g in groups], "joined") for p in range(pieces)]
    results, token = add_stage(items, after, 14 * 10**9)
    joined = groups[0]
    joined.take(results)
    return joined, token


def advance(groups, after, flops=10**9):
    groups = [group for group in groups if group.result is None]
    if not groups:
        return after[0]
    items = [group.items() for group in groups]
    results, token = add_stage([item for part in items for item in part], after, flops)
    for group, part in zip(groups, items):
        group.take(results[: len(part)])
        results = results[len(part) :]
    return token


def gather_vectors(core, folded, parts):
    width = parts[0][0].shape[1]
    args = (core, folded) + tuple(item for part in parts for item in part)
    count = len(parts[0])
    tiles = width // 128
    lines = folded.shape[0]

    def body(core_ref, folded_ref, *refs):
        kept, sent = refs[-2:]
        first = core_ref[0] == 0
        wholes = []
        for layer in range(2):
            vecs1, qv, vecs2, scale, ups = [ref[...] for ref in refs[layer * count : layer * count + count]]
            rows = [vecs1, qv, vecs2[3:4], vecs2[2:3], vecs2[0:2], vecs2[4:5], scale]
            rows += [ups[:, n * width : (n + 1) * width] for n in range(ups.shape[1] // width)]
            rows.append(jnp.zeros((16 - sum(row.shape[0] for row in rows), width), F32))
            wholes.append(jnp.concatenate(rows, axis=0))

        def put(at, zero, one):
            kept[pl.ds(at, 16), :] = jnp.where(first, zero, one)
            sent[pl.ds(at, 16), :] = jnp.where(first, one, zero)

        for t in range(tiles):
            put(t * 16, *[whole[:, t * 128 : (t + 1) * 128] for whole in wholes])
        for n in range(lines):
            put((tiles + n) * 16, folded_ref[n, :HEAD_ROWS], folded_ref[n, HEAD_ROWS:])

    out = shape((16 * (tiles + lines), 128), F32)
    return kernel_call(body, [S] + [V] * (len(args) - 1), [out, out], [], args, SMALL)


def pick_rows(core, zero, one, after):
    rows, width = zero[0].shape

    def body(core_ref, zero_y, zero_g, one_y, one_g, kept, sent, token):
        first = core_ref[0] == 0
        for n, (a, b) in enumerate(((zero_y, one_y), (zero_g, one_g))):
            kept[n] = jnp.where(first, a[...], b[...])
            sent[n] = jnp.where(first, b[...], a[...])
        token[...] = jnp.zeros((8, 128), F32)

    both = shape((2, rows, width), BF16)
    return kernel_call(body, [S, V, V, V, V], [both, both, shape((8, 128), F32)], [], (core, *zero, *one), SMALL, after=after)


def arrange_rows(core, own, came, sizes, after):
    crops, len_big, pad_big, slots, len_small, pad_small = sizes
    width = own.shape[2]
    split = crops * pad_big

    def body(core_ref, own_ref, came_ref, *outs):
        me = core_ref[0]
        for n in range(2):
            out_big, out_small = outs[2 * n : 2 * n + 2]
            for place, ref in ((me, own_ref), (1 - me, came_ref)):
                for c in range(crops):
                    out_big[0, place, c] = ref[n, pl.ds(c * pad_big, len_big), :]
                rest = ref[n, pl.ds(split, pad_small), :].astype(F32)
                for s in range(slots):
                    out_small[0, place, s] = rest[s * len_small : (s + 1) * len_small].astype(BF16)

    big = shape((1, 2, crops, len_big, width), BF16)
    small = shape((1, 2, slots, len_small, width), BF16)
    return kernel_call(body, [S, V, V], [big, small, big, small], [], (core, own, came), SMALL, after=after)


def arrange_grads(core, sums, came, block, width, hidden):
    args = tuple(item for part in (*sums, *came) for _, item in part)
    quarters = hidden // width
    tiles = {"down": width // 256, "up": hidden // 256, "proj": width // 256, "qkv": 3 * width // 256}

    def body(core_ref, *refs):
        outs = dict(zip(NAMES, refs[len(args) :]))

        def put(half, part, refs):
            for (names, _), ref in zip(part, refs):
                counts, bases, subs = piece_plan(names, tiles, quarters)
                for name in names:
                    for tile in range(tiles[name]):
                        large = tiles[name] // 3 * 2
                        p, at = (0, tile) if tile < large else (1, tile - large)
                        times = quarters if name == "down" else 1
                        for q in range(times):
                            value = ref[p * subs[0] + bases[p][name] + at * times + q]
                            outs[name][0, pl.ds(q * block, block), pl.ds((half * tiles[name] + tile) * 128, 128)] = value

        count = len(args) // 2
        starts = [0, len(sums[0]), count, count + len(came[0])]
        for me in range(2):

            @pl.when(core_ref[0] == me)
            def _():
                put(me, sums[me], refs[starts[me] :])
                put(1 - me, came[me], refs[starts[2 + me] :])

    return kernel_call(
        body,
        [S] + [V] * len(args),
        [
            shape((1, quarters * block, width), F32),
            shape((1, block, hidden), F32),
            shape((1, block, width), F32),
            shape((1, block, 3 * width), F32),
        ],
        [],
        (core, *args),
        SMALL,
    )


def swap(value):
    return lax.ppermute(value, "section", [(0, 1), (1, 0)])


def across(value, bits):
    devices = lax.axis_size("dp")
    pairs = [(core * devices + i, core * devices + (i ^ (1 << bits[core]))) for core in range(2) for i in range(devices)]
    return lax.ppermute(value, ("section", "dp"), pairs)


def hand_over(value, layer):
    return lax.ppermute(value, "section", [(1 - layer, layer)])


HEAD_ROWS = 16


def flip_lanes(side):
    row = lax.broadcasted_iota(jnp.int32, (side, 128), 0)
    lane = lax.broadcasted_iota(jnp.int32, (side, 128), 1)
    return jnp.where(row + lane == side - 1, 1.0, 0.0)


def table_bases(core, own, other, grids, entries_big):
    heads = own.shape[1]
    both = 2 * HEAD_ROWS

    def body(core_ref, own_ref, other_ref, out_big, out_small, corners, own_buf, other_buf):
        first = core_ref[0] == 0
        own_buf[...] = own_ref[...]
        other_buf[...] = other_ref[...]
        out_big[...] = jnp.zeros_like(out_big)
        out_small[...] = jnp.zeros_like(out_small)
        corners[...] = jnp.zeros_like(corners)
        lane = lax.broadcasted_iota(jnp.int32, (both, 128), 1)

        def lines(start, count):
            mine, theirs = own_buf[pl.ds(start, count), :], other_buf[pl.ds(start, count), :]
            return jnp.where(first, mine, theirs), jnp.where(first, theirs, mine)

        start = 0
        for n, (out, grid) in enumerate(((out_big, grids[0]), (out_small, grids[1]))):
            side = 2 * grid - 1
            flip = flip_lanes(side)
            flipped = []
            for d in range(side):
                pair = []
                for part in lines(start + (side - 1 - d) * side, side):
                    turned = lax.dot_general(part, flip, (((0,), (0,)), ((), ())), precision=lax.Precision.HIGHEST, preferred_element_type=F32)
                    pair.append(jnp.concatenate([turned, jnp.zeros((HEAD_ROWS - heads, 128), F32)], axis=0))
                flipped.append(jnp.concatenate(pair, axis=0))
            for r in range(grid):
                tiles = [jnp.zeros((both, 128), F32) for _ in range(out.shape[3] // 128)]
                for d in range(side):
                    low = 1 + d * grid
                    shift = (low - (grid - 1 - r)) % 128
                    moved = pltpu.roll(flipped[d], shift, 1) if shift else flipped[d]
                    tile, at = low // 128, low % 128
                    tiles[tile] = jnp.where((lane >= at) & (lane < at + grid), moved, tiles[tile])
                    if at + grid > 128:
                        tiles[tile + 1] = jnp.where(lane < at + grid - 128, moved, tiles[tile + 1])
                value = jnp.concatenate(tiles, axis=1)
                for layer in range(2):
                    out[layer, :, r, :] = value[layer * HEAD_ROWS : layer * HEAD_ROWS + heads]
            for layer, part in enumerate(lines(start + side * side, 3)):
                corners[layer, n, 0:3, 0:heads] = part
            start = entries_big

    return kernel_call(
        body,
        [S, V, V],
        [shape((2, heads, 16, 512), F32), shape((2, heads, 8, 256), F32), shape((2, 2, 8, 128), F32)],
        [pltpu.VMEM(own.shape, F32), pltpu.VMEM(own.shape, F32)],
        (core, own, other),
        SMALL,
    )


def table_folds(big, small, grids, lengths, after):
    heads = big.shape[1]
    counts = [-(-(2 * grid - 1) // 4) for grid in grids]

    def body(big_ref, small_ref, out):
        lane = lax.broadcasted_iota(jnp.int32, (heads, 128), 1)
        base = 0
        ends = []
        for ref, grid, count, length in zip((big_ref, small_ref), grids, counts, lengths):
            for line in range(count):
                total = jnp.zeros((heads, 128), F32)
                for d in range(4 * line, min(4 * line + 4, 2 * grid - 1)):
                    low = 1 + d * grid
                    tile, at = low // 128, low % 128
                    for r in range(grid):
                        to = 32 * (d % 4) + grid - 1 - r
                        moved = ref[r, :, tile * 128 : tile * 128 + 128]
                        if at + grid > 128:
                            moved = jnp.where(lane >= at, moved, ref[r, :, tile * 128 + 128 : tile * 128 + 256])
                        shift = (to - at) % 128
                        moved = pltpu.roll(moved, shift, 1) if shift else moved
                        total = total + jnp.where((lane >= to) & (lane < to + grid), moved, 0)
                out[base + line] = total
            base += count
            first, second = ref[grid], ref[grid + 1]
            wide = lax.broadcasted_iota(jnp.int32, first.shape, 1)
            ends.append(jnp.sum(jnp.where((wide > 0) & (wide < length), first, 0), axis=1, keepdims=True))
            ends.append(second[:, 0:1])
            ends.append(first[:, 0:1])
        last = out[base - 1]
        for n, end in enumerate(ends):
            last = jnp.where(lane == 96 + n, end, last)
        out[base - 1] = last

    return kernel_call(body, [V, V], [shape((sum(counts), heads, 128), F32)], [], (big, small), SMALL, after=after)[0]


def arrange_small(where, flat, grids, entries, width, block, ups, vectors):
    tiles = width // 128
    counts = [-(-(2 * grid - 1) // 4) for grid in grids]

    def body(where_ref, flat_ref, *outs):
        place = where_ref[1]
        lines = jnp.concatenate([flat_ref[pl.ds(t * 16, 16), :] for t in range(tiles)], axis=1)
        moved = pltpu.roll(lines, lax.rem(width - place * block, width), 1)
        for n in range(vectors):
            outs[n][...] = moved[n : n + 1, :block]
        per_row = width // (ups * block)
        moved = pltpu.roll(lines, lax.rem(width - lax.rem(place, per_row) * (ups * block), width), 1)
        row = lax.broadcasted_iota(jnp.int32, (16, ups * block), 0)
        chosen = jnp.where(row == vectors + place // per_row, moved[:, : ups * block], 0)
        outs[vectors][...] = jnp.sum(chosen, axis=0, keepdims=True)
        base = 16 * tiles

        def at(line):
            return flat_ref[pl.ds(base + line * HEAD_ROWS, HEAD_ROWS), :]

        line, last = 0, sum(counts) - 1
        for n, grid in enumerate(grids):
            side = 2 * grid - 1
            out = outs[vectors + 1 + n]
            row = lax.broadcasted_iota(jnp.int32, (side, 128), 0)
            lane = lax.broadcasted_iota(jnp.int32, (side, 128), 1)
            for d in range(side):
                pick = jnp.where(lane - 32 * (d % 4) + row == side - 1, 1.0, 0.0)
                value = lax.dot_general(pick, at(line + d // 4), (((1,), (1,)), ((), ())), precision=lax.Precision.HIGHEST, preferred_element_type=F32)
                out[0, pl.ds((side - 1 - d) * side, side), :] = value[:, :HEADS]
            pick = jnp.where(lane[:3] == 96 + 3 * n + row[:3], 1.0, 0.0)
            value = lax.dot_general(pick, at(last), (((1,), (1,)), ((), ())), precision=lax.Precision.HIGHEST, preferred_element_type=F32)
            out[0, pl.ds(side * side, 3), :] = value[:, :HEADS]
            line += counts[n]

    outs = [shape((1, block), F32)] * vectors + [shape((1, ups * block), F32)] + [shape((1, count, HEADS), F32) for count in entries]
    return kernel_call(body, [S, V], outs, [], (where, flat), SMALL)


def body(input_big, input_small, small_counts, cotangent_big, cotangent_small, norm1_gain, norm1_bias, qkv_weight, query_bias, value_bias, table_big, table_small, proj_weight, proj_bias, attn_scale, norm2_gain, norm2_bias, up_weight, up_bias, down_weight, down_bias, mlp_scale):
    micro, crops, len_big, width = input_big.shape
    slots_all, len_small = input_small.shape[1], input_small.shape[2]
    slots = slots_all // small_counts.shape[1]
    grid_big, grid_small = math.isqrt(len_big - 1), math.isqrt(len_small - 1)
    pad_big = up_to(len_big, 16)
    real_small = slots_all * len_small
    pad_small = up_to(real_small, 16)
    split = crops * pad_big
    rows = split + pad_small
    sizes = (crops, len_big, pad_big, slots_all, len_small, pad_small)
    devices = lax.axis_size("dp")
    bits = devices.bit_length() - 1
    core = lax.axis_index("section")
    place = lax.axis_index("dp")
    where = jnp.stack([core, place]).astype(jnp.int32)
    first = core == 0

    def join(big, small):
        big = lax.dynamic_index_in_dim(big, core, 0, keepdims=False)
        small = lax.dynamic_index_in_dim(small, core, 0, keepdims=False)
        big = jnp.pad(big, ((0, 0), (0, pad_big - len_big), (0, 0))).reshape(split, width)
        small = jnp.pad(small.reshape(real_small, width), ((0, pad_small - real_small), (0, 0)))
        return jnp.concatenate([big, small])

    x0 = join(input_big, input_small)
    cotangent = join(cotangent_big, cotangent_small)
    counts = lax.dynamic_index_in_dim(small_counts, core, 0, keepdims=False)
    line = jnp.arange(rows, dtype=jnp.int32)
    spot = line - split
    slot_of = jnp.arange(slots * len_small, dtype=jnp.int32) // len_small
    small_keep = (slot_of[None, :] < counts[:, None]).astype(F32).reshape(real_small)
    keep = jnp.where(line < split, (line % pad_big < len_big).astype(F32), jnp.pad(small_keep, (split, pad_small - real_small)))
    keep = keep[:, None]

    vec_own = jnp.concatenate(
        [norm1_gain, norm1_bias, query_bias, value_bias, proj_bias, attn_scale, norm2_gain, norm2_bias, down_bias, mlp_scale, up_bias.reshape(-1, width)]
    )
    tables_own = jnp.concatenate([table_big[0], table_small[0]])
    vec_other, tables_other = swap(vec_own), swap(tables_own)
    qkv = (qkv_weight[0], swap(qkv_weight[0]))
    proj = (proj_weight[0], swap(proj_weight[0]))
    up = (up_weight[0], swap(up_weight[0]))
    down = (down_weight[0], swap(down_weight[0]))

    grids, lengths = (grid_big, grid_small), (len_big, len_small)
    entries_big = table_big.shape[1]
    base_big, base_small, corners_all = table_bases(where, tables_own, tables_other, grids, entries_big)
    layers = []
    for layer in range(2):
        vec = jnp.where(core == layer, vec_own, vec_other)
        ups = vec[10:].reshape(1, -1)
        joined = jnp.concatenate([vec[2:3], jnp.zeros_like(vec[2:3]), vec[3:4]], axis=1)
        layers.append((vec, ups, joined, corners_all[layer], base_big[layer], base_small[layer]))

    saved, lefts = [], []
    x = x0
    for layer in range(2):
        vec, ups, joined, corners, big, small = layers[layer]
        passing = () if layer == 0 else (saved[0][2],)
        normed, projected, *passed = qkv_forward(layer, where, x, vec[0:1], vec[1:2], joined, *qkv, (cotangent,) if layer == 0 else (), passing)
        lefts += [(item, swap(item)) for item in passed]
        attended = attention_forward(projected, big, small, corners, sizes)
        made = mlp_forward(layer, where, attended, normed, x, keep, vec, ups, proj, up, down if layer == 0 else None)
        saved.append((x, projected) + tuple(made[:4]))
        if layer == 0:
            x, mlp0 = made[4:]

    rest = list(range(3, bits))
    orders = [([0, 1, 2] + rest, [1, 2] + rest + [0]), ([2, 0, 1] + rest, [2, 0, 1] + rest)]

    def mlp_part(layer, g, mlp, after=(), through=()):
        slope, branch, middle = saved[layer][3:]
        return mlp_backward(layer, where, g, keep, layers[layer][0], slope, middle, branch, mlp, down, up, proj, after=after, through=through)

    def attention_part(layer, ga, after):
        _, _, _, corners, big, small = layers[layer]
        return attention_backward(where, saved[layer][1], ga, big, small, corners, sizes, after=after)

    def qkv_part(layer, gproj, gmid, after, flops=SMALL):
        return qkv_backward(layer, where, gproj, saved[layer][0], gmid, layers[layer][0][0:1], *qkv, after=after, flops=flops)


    kept, sent, ga, gmid, vecs2_1, ups_1, left1 = mlp_part(1, cotangent, None, (lefts[0][1],), (saved[1][2],))
    lefts.append((left1, swap(left1)))
    right = (kept, swap(sent))
    gproj, kept, sent, fold_big1, fold_small1, qv_1 = attention_part(1, ga, (ups_1,))
    blocks = (kept, swap(sent))
    made = weight_grad(where, orders, NAMES[:2], lefts[1], right, blocks, SMALL, (qv_1,))
    most1 = Scatter(made, orders)
    gx1, vecs1_1 = qkv_part(1, gproj, gmid, made[:1])
    made = weight_grad(where, orders, NAMES[2:], lefts[1], right, blocks, SMALL, (vecs1_1,))
    last1 = Scatter(made, orders)

    kept, sent, ga, gmid, vecs2_0, ups_0 = mlp_part(0, gx1, mlp0, made[:1])
    right = (kept, swap(sent))
    all1, token = join_groups([most1, last1], (ups_0,))
    made = weight_grad(where, orders, NAMES[:2], lefts[0], right, None, SMALL, (token,))
    most0 = Scatter(made, orders)
    token = advance([all1], made[:1])
    gproj, kept, sent, fold_big0, fold_small0, qv_0 = attention_part(0, ga, (token,))
    blocks = (kept, swap(sent))
    gx0, vecs1_0 = qkv_part(0, gproj, gmid, (qv_0,), 7 * 10**9)
    token = advance([all1, most0], (vecs1_0,))
    made = weight_grad(where, orders, NAMES[2:], lefts[0], right, blocks, 9 * 10**9, (token,))
    last0 = Scatter(made, orders)
    token = advance([all1], made[:1])
    y1, scale_1 = down_forward(1, where, left1, saved[1][5], keep, layers[1][0], *down, upstream=cotangent, after=(token,))

    def by_line(zero, one):
        both = jnp.pad(jnp.stack([zero, one]), ((0, 0), (0, HEAD_ROWS - HEADS), (0, 0), (0, 0)))
        return jnp.transpose(both, (2, 0, 1, 3)).reshape(zero.shape[1], 2 * HEAD_ROWS, -1)

    folded = table_folds(by_line(fold_big0, fold_big1), by_line(fold_small0, fold_small1), grids, lengths, (scale_1,))
    flat = gather_vectors(
        where, folded, [(vecs1_0, qv_0, vecs2_0, vecs2_0[5:6], ups_0), (vecs1_1, qv_1, vecs2_1, scale_1, ups_1)]
    )
    flat = Total(*flat, bits)
    token = (folded,)
    for group in ([most0], [last0, flat], [most0], [last0, flat]):
        token = (advance(group, token),)
    rows_own = pick_rows(where, (saved[1][0], gx0), (y1, gx1), token)
    rows_came = swap(rows_own[1])
    token = rows_own[2:]
    while any(group.result is None for group in (most0, last0, all1)):
        token = (advance([most0, all1], token, LATE),)
        token = (advance([last0, flat], token, LATE),)
    layer_big, layer_small, grad_big, grad_small = arrange_rows(where, rows_own[0], rows_came, sizes, token)
    token = (layer_small[0, 0, 0, :8, :128],)
    while flat.result is None:
        token = (advance([flat], token),)
    flat = flat.result

    sums = [[(NAMES[:2], most0.result), (NAMES[2:], last0.result)], [(NAMES, all1.result)]]
    came = [[(names, hand_over(item, layer)) for names, item in sums[layer]] for layer in range(2)]
    block = width // devices
    hidden = up_bias.shape[1]
    grad_down, grad_up, grad_proj, grad_qkv = arrange_grads(where, sums, came, block, width, hidden)

    small = arrange_small(where, flat, grids, (entries_big, table_small.shape[1]), width, block, hidden // width, 10)
    grad_up_bias, grad_table_big, grad_table_small = small[10:]

    def vector(row):
        return small[row]

    return (
        layer_big,
        layer_small,
        grad_big,
        grad_small,
        vector(0),
        vector(1),
        grad_qkv,
        vector(2),
        vector(3),
        grad_table_big,
        grad_table_small,
        grad_proj,
        vector(4),
        vector(5),
        vector(6),
        vector(7),
        grad_up,
        grad_up_bias,
        grad_down,
        vector(8),
        vector(9),
    )


def solution(mesh):
    row = P("section", None)
    whole = P("section", None, None)
    dp4 = P(None, "dp", None, None)
    in_specs = (dp4, dp4, P(None, "dp"), dp4, dp4, row, row, whole, row, row, whole, whole, whole, row, row, row, row, whole, row, whole, row, row)
    out5 = P("section", None, "dp", None, None)
    vec = P("section", "dp")
    mat = P("section", "dp", None)
    out_specs = (out5, out5, out5, out5, vec, vec, mat, vec, vec, whole, whole, mat, vec, vec, vec, vec, mat, vec, mat, vec, vec)
    return jax.shard_map(body, mesh=mesh, in_specs=in_specs, out_specs=out_specs, check_vma=False)
```

```python
import math

import jax
import jax.numpy as jnp
from jax import lax
from jax.experimental import pallas as pl
from jax.experimental.pallas import tpu as pltpu
from jax.sharding import PartitionSpec as P

HEADS = 12
EPS = 1e-06
LOW = -1e30
MIB = 1024 * 1024
VMEM_BYTES = 44 * MIB
COST = 0.4
SMALL = 10**8
LATE = 4 * 10**9
F32 = jnp.float32
BF16 = jnp.bfloat16
V = pl.BlockSpec(memory_space=pltpu.VMEM)
S = pl.BlockSpec(memory_space=pltpu.SMEM)
H = pl.BlockSpec(memory_space=pltpu.HBM)


def up_to(value, multiple):
    return -(-value // multiple) * multiple


def mm(left, right):
    return jnp.dot(left, right, preferred_element_type=F32)


def mm_back(left, right):
    return lax.dot_general(left, right, (((1,), (1,)), ((), ())), preferred_element_type=F32)


def mm_outer(left, right):
    return lax.dot_general(left, right, (((0,), (0,)), ((), ())), preferred_element_type=F32)


def norm_parts(values):
    centre = values - jnp.mean(values, axis=-1, keepdims=True)
    spread = jnp.mean(centre * centre, axis=-1, keepdims=True)
    scale = lax.rsqrt(spread + EPS)
    return centre * scale, scale


def norm_back(upstream, values, gain):
    unit, scale = norm_parts(values)
    scaled = upstream * gain
    first = jnp.mean(scaled, axis=-1, keepdims=True)
    second = jnp.mean(scaled * unit, axis=-1, keepdims=True)
    going = scale * (scaled - first - unit * second)
    return (
        going,
        jnp.sum(upstream * unit, axis=0, keepdims=True),
        jnp.sum(upstream, axis=0, keepdims=True),
    )


def gelu_parts(x):
    raised = jnp.exp(-0.5 * x * x)
    t = 1.0 / (1.0 + (0.3275911 * math.sqrt(0.5)) * jnp.abs(x))
    poly = t * (
        0.127414796
        + t * (-0.142248368 + t * (0.7107068705 + t * (-0.7265760135 + t * 0.5307027145)))
    )
    half = poly * raised
    phi = jnp.where(x >= 0, 1.0 - half, half)
    return x * phi, phi + x * (raised * (1.0 / math.sqrt(2.0 * math.pi)))


def column_cuts(width, parts):
    step = width // parts
    return [(slice(None), pl.ds(i * step, step)) for i in range(parts)]


def row_cuts(height, parts):
    step = height // parts
    return [(pl.ds(i * step, step), slice(None)) for i in range(parts)]


def fetch_start(mine, own, other, buffer, sems, cuts):
    for i, cut in enumerate(cuts):

        @pl.when(mine)
        def _():
            pltpu.make_async_copy(own.at[cut], buffer.at[cut], sems.at[i]).start()

        @pl.when(jnp.logical_not(mine))
        def _():
            pltpu.make_async_copy(other.at[cut], buffer.at[cut], sems.at[i]).start()


def fetch_wait(own, buffer, sems, cuts, i):
    pltpu.make_async_copy(own.at[cuts[i]], buffer.at[cuts[i]], sems.at[i]).wait()


def size_of(item):
    return math.prod(item.shape) * jnp.dtype(item.dtype).itemsize


ANY = pl.BlockSpec(memory_space=pl.ANY)


def after_spec(item):
    return V if size_of(item) < 65536 else ANY


def kernel_call(body, ins, outs, scratch, args, flops, after=(), out_specs=None, through=()):
    specs = list(ins) + [after_spec(item) for item in after] + [H] * len(through)
    out_specs = list(out_specs or [V] * len(outs)) + [H] * len(through)
    outs = list(outs) + [shape(item.shape, item.dtype) for item in through]
    count, given, made = len(args), len(specs), len(outs)

    def inner(*refs):
        body(*refs[:count], *refs[given : given + made - len(through)], *refs[given + made :])

    args = tuple(args) + tuple(after) + tuple(through)
    return pl.pallas_call(
        inner,
        in_specs=specs,
        out_specs=out_specs,
        out_shape=[pltpu.HBM(o.shape, o.dtype) if spec is H else o for o, spec in zip(outs, out_specs)],
        scratch_shapes=scratch,
        input_output_aliases={given - len(through) + n: made - len(through) + n for n in range(len(through))},
        compiler_params=pltpu.CompilerParams(vmem_limit_bytes=VMEM_BYTES),
        cost_estimate=pl.CostEstimate(flops=int(flops / COST), bytes_accessed=1024, transcendentals=0),
    )(*in_hbm(args, specs))


def in_hbm(args, specs):
    return [pltpu.with_memory_space_constraint(a, pltpu.HBM) if spec is H else a for a, spec in zip(args, specs)]


def shape(dims, kind):
    return jax.ShapeDtypeStruct(dims, kind)


def qkv_forward(layer, core, x, gain, shift, joined, own, other, after=(), through=()):
    rows, width = x.shape
    triple = own.shape[1]
    cuts = column_cuts(triple, 3)

    def body(core_ref, x_ref, gain_ref, shift_ref, joined_ref, own_ref, other_ref, normed_ref, proj_ref, buf, sems):
        mine = core_ref[0] == layer
        fetch_start(mine, own_ref, other_ref, buf, sems, cuts)
        unit, _ = norm_parts(x_ref[...].astype(F32))
        normed_ref[...] = (unit * gain_ref[...] + shift_ref[...]).astype(BF16)
        for i in range(3):
            fetch_wait(own_ref, buf, sems, cuts, i)

        def step(i, carry):
            cols = pl.ds(pl.multiple_of(i * width, width), width)
            proj_ref[:, cols] = (mm(normed_ref[...], buf[:, cols]) + joined_ref[:, cols]).astype(BF16)
            return carry

        lax.fori_loop(0, 3, step, 0)

    return kernel_call(
        body,
        [S, V, V, V, V, H, H],
        [shape((rows, width), BF16), shape((rows, triple), BF16)],
        [pltpu.VMEM((width, triple), BF16), pltpu.SemaphoreType.DMA((3,))],
        (core, x, gain, shift, joined, own, other),
        5 * 10**9,
        after=after,
        through=through,
    )


def build_bias(base, out_ref, block_ref, grid, corner, crops, length, block_rows):
    lanes = base.shape[1]
    head_patch, patch_head, head_head = corner
    lane = lax.broadcasted_iota(jnp.int32, (block_rows, 256), 1)
    line = lax.broadcasted_iota(jnp.int32, (block_rows, 256), 0)
    first = jnp.where(lane == 0, head_head, head_patch)
    block_ref[...] = jnp.where(lane >= length, LOW, first)
    small = lane[:grid]
    for r in range(grid):
        off = (grid - 1 - r) * grid
        moved = base if off == 0 else pltpu.roll(base, lanes - off, 1)
        moved = moved[:grid, :256]
        value = jnp.where(small == 0, patch_head, jnp.where(small >= length, LOW, moved))
        block_ref[pl.ds(1 + grid * r, grid), :] = value
    if crops == 1:
        return
    out_ref[...] = jnp.full(out_ref.shape, LOW, F32)
    for s in range(crops):
        value = block_ref[pl.ds(0, length), :]
        if s:
            value = pltpu.roll(value, s * length, 1)
        out_ref[pl.ds(s * length, length), :] = value


def pair_bias(pair, corner_ref, bb_ref, bs_ref, big, block, small, sizes):
    crops, len_big, pad_big, slots, len_small, pad_small = sizes
    grid_big, grid_small = math.isqrt(len_big - 1), math.isqrt(len_small - 1)
    for h in range(2):
        head = pair * 2 + h
        build_bias(bb_ref[head], big.at[pl.ds(h * pad_big, pad_big)], big.at[pl.ds(h * pad_big, pad_big)], grid_big, [corner_ref[0, i, head] for i in range(3)], 1, len_big, pad_big)
        build_bias(bs_ref[head], small.at[pl.ds(h * pad_small, pad_small)], block, grid_small, [corner_ref[1, i, head] for i in range(3)], slots, len_small, block.shape[0])


def two_heads(value):
    lane = lax.broadcasted_iota(jnp.int32, (1, 128), 1)
    return jnp.concatenate([jnp.where(lane < 64, value, 0), jnp.where(lane >= 64, value, 0)], axis=0)


def one_line(value):
    count = value.shape[0] // 2
    lane = lax.broadcasted_iota(jnp.int32, (1, 128), 1)
    return jnp.where(lane < 64, value[:count], value[count:])


def attention_probs(scores):
    raised = jnp.exp(scores - jnp.max(scores, axis=-1, keepdims=True))
    return raised * (1.0 / jnp.sum(raised, axis=-1, keepdims=True))


def attention_parts(sizes):
    crops, _, pad_big, _, _, pad_small = sizes
    return [(c * pad_big, pad_big, True) for c in range(crops)] + [(crops * pad_big, pad_small, False)]


def bias_scratch(sizes):
    _, _, pad_big, _, len_small, pad_small = sizes
    return [
        pltpu.VMEM((2 * pad_big, 256), F32),
        pltpu.VMEM((up_to(len_small, 8), 256), F32),
        pltpu.VMEM((2 * pad_small, 256), F32),
    ]


def attention_forward(projected, base_big, base_small, corners, sizes, after=()):
    rows, triple = projected.shape
    width = triple // 3
    pairs = HEADS // 2
    parts = attention_parts(sizes)

    def body(corner_ref, proj_ref, bb_ref, bs_ref, out_ref, big, block, small):
        def step(pair, carry):
            pair_bias(pair, corner_ref, bb_ref, bs_ref, big, block, small, sizes)
            q, k, v = [pl.ds(pl.multiple_of(n * width + pair * 128, 128), 128) for n in range(3)]
            scores = []
            for start, count, is_big in parts:
                part = pl.ds(start, count)
                bias = big if is_big else small
                scores.append(mm_back(two_heads(proj_ref[part, q] * 0.125), proj_ref[part, k]) + bias[:, :count])
            probs = [attention_probs(item).astype(BF16) for item in scores]
            for (start, count, is_big), item in zip(parts, probs):
                part = pl.ds(start, count)
                out_ref[part, q] = one_line(mm(item, proj_ref[part, v])).astype(BF16)
            return carry

        lax.fori_loop(0, pairs, step, 0)

    return kernel_call(
        body,
        [S, V, V, V],
        [shape((rows, width), BF16)],
        bias_scratch(sizes),
        (corners, projected, base_big, base_small),
        10**10,
        after=after,
    )[0]


FF_STEP = 512


def saved_cuts(width, hidden):
    return [(0, hidden), (hidden, width), (hidden + width, width), (hidden + 2 * width, width)]


def mlp_forward(layer, core, attended, normed, x, keep, vec, up_bias, proj, up, down=None):
    rows, width = x.shape
    hidden = up[0].shape[1]
    count = hidden // FF_STEP
    cuts = [(slice(None), slice(None))]
    up_cuts = column_cuts(hidden, count)
    down_cuts = row_cuts(hidden, 2)
    spans = saved_cuts(width, hidden)
    total_cols = hidden + 3 * width
    weights = proj + up + (down or ())

    def body(core_ref, att_ref, n1_ref, x_ref, keep_ref, vec_ref, bias_ref, *refs):
        weight_refs, refs = refs[: len(weights)], refs[len(weights) :]
        left_ref, slope_ref, branch_ref, middle_ref, refs = refs[0], refs[1], refs[2], refs[3], refs[4:]
        if down:
            y_ref, mlp_ref, refs = refs[0], refs[1], refs[2:]
        buf, buf_up, hid, slp, br, mid, n2, sems, sems_up, out_sems = refs[:10]
        mine = core_ref[0] == layer
        fetch_start(mine, weight_refs[0], weight_refs[1], buf, sems, cuts)
        fetch_start(mine, weight_refs[2], weight_refs[3], buf_up, sems_up, up_cuts)
        if down:
            buf_down, mlp_buf, sems_down = refs[10:]
            fetch_start(mine, weight_refs[4], weight_refs[5], buf_down, sems_down, down_cuts)
        going = []

        def send(source, target):
            copy = pltpu.make_async_copy(source, target, out_sems.at[len(going)])
            copy.start()
            going.append(copy)

        def span(n):
            return left_ref.at[:, pl.ds(*spans[n])]

        send(att_ref, span(2))
        send(n1_ref, span(3))
        fetch_wait(weight_refs[0], buf, sems, cuts, 0)
        branch = mm(att_ref[...], buf[...]) + vec_ref[4:5, :]
        br[...] = branch.astype(BF16)
        middle = x_ref[...].astype(F32) + vec_ref[5:6, :] * branch
        mid[...] = middle
        unit, _ = norm_parts(middle)
        n2[...] = (unit * vec_ref[6:7, :] + vec_ref[7:8, :]).astype(BF16)
        send(br, branch_ref)
        send(mid, middle_ref)
        send(n2, span(1))
        for i in range(count):
            fetch_wait(weight_refs[2], buf_up, sems_up, up_cuts, i)

        def pre_of(i):
            cols = pl.ds(i * FF_STEP, FF_STEP)
            return mm(n2[...], buf_up[:, cols]) + bias_ref[:, cols]

        pre = pre_of(0)
        for i in range(count):
            following = pre_of(i + 1) if i + 1 < count else None
            value, slope = gelu_parts(pre)
            cols = pl.ds(i * FF_STEP, FF_STEP)
            hid[:, cols] = value.astype(BF16)
            slp[:, cols] = slope.astype(BF16)
            pre = following
            if i % 2 == 1:
                both = pl.ds((i - 1) * FF_STEP, 2 * FF_STEP)
                send(hid.at[:, both], left_ref.at[:, both])
                send(slp.at[:, both], slope_ref.at[:, both])
        if down:
            for i in range(2):
                fetch_wait(weight_refs[4], buf_down, sems_down, down_cuts, i)
            total = mm(hid[...], buf_down[...]) + vec_ref[8:9, :]
            mlp_buf[...] = total.astype(BF16)
            send(mlp_buf, mlp_ref)
            y_ref[...] = ((mid[...] + vec_ref[9:10, :] * total) * keep_ref[...]).astype(BF16)
        for copy in going:
            copy.wait()

    outs = [shape((rows, total_cols), BF16), shape((rows, hidden), BF16), shape((rows, width), BF16), shape((rows, width), F32)]
    out_specs = [H] * 4
    scratch = [
        pltpu.VMEM((width, width), BF16),
        pltpu.VMEM((width, hidden), BF16),
        pltpu.VMEM((rows, hidden), BF16),
        pltpu.VMEM((rows, hidden), BF16),
        pltpu.VMEM((rows, width), BF16),
        pltpu.VMEM((rows, width), F32),
        pltpu.VMEM((rows, width), BF16),
        pltpu.SemaphoreType.DMA((1,)),
        pltpu.SemaphoreType.DMA((count,)),
        pltpu.SemaphoreType.DMA((6 + count,)),
    ]
    if down:
        outs += [shape((rows, width), BF16), shape((rows, width), BF16)]
        out_specs += [V, H]
        scratch += [
            pltpu.VMEM((hidden, width), BF16),
            pltpu.VMEM((rows, width), BF16),
            pltpu.SemaphoreType.DMA((2,)),
        ]
    return kernel_call(
        body,
        [S, V, V, V, V, V, V] + [H] * len(weights),
        outs,
        scratch,
        (core, attended, normed, x, keep, vec, up_bias) + weights,
        (17 if down else 13) * 10**9,
        out_specs=out_specs,
    )


def down_forward(layer, core, left, middle, keep, vec, own, other, upstream, after=()):
    rows, width = middle.shape
    depth = own.shape[0]
    parts = 4
    cuts = row_cuts(depth, parts)
    step = depth // parts

    def body(core_ref, left_ref, middle_ref, keep_ref, vec_ref, g_ref, own_ref, other_ref, y_ref, sum_ref, buf, hid, mid, sems, in_sems):
        fetch_start(core_ref[0] == layer, own_ref, other_ref, buf, sems, cuts)
        copies = [
            pltpu.make_async_copy(left_ref.at[:, pl.ds(i * step, step)], hid.at[:, pl.ds(i * step, step)], in_sems.at[i])
            for i in range(parts)
        ] + [pltpu.make_async_copy(middle_ref, mid, in_sems.at[parts])]
        for copy in copies:
            copy.start()
        total = vec_ref[8:9, :]
        for i in range(parts):
            fetch_wait(own_ref, buf, sems, cuts, i)
            copies[i].wait()
            part = pl.ds(i * step, step)
            total = total + mm(hid[:, part], buf[part, :])
        copies[parts].wait()
        sum_ref[...] = jnp.sum(g_ref[...].astype(F32) * keep_ref[...] * total, axis=0, keepdims=True)
        y_ref[...] = ((mid[...] + vec_ref[9:10, :] * total) * keep_ref[...]).astype(BF16)

    return kernel_call(
        body,
        [S, H, H, V, V, V, H, H],
        [shape((rows, width), BF16), shape((1, width), F32)],
        [
            pltpu.VMEM((depth, width), BF16),
            pltpu.VMEM((rows, depth), BF16),
            pltpu.VMEM((rows, width), F32),
            pltpu.SemaphoreType.DMA((parts,)),
            pltpu.SemaphoreType.DMA((parts + 1,)),
        ],
        (core, left, middle, keep, vec, upstream, own, other),
        9 * 10**9,
        after=after,
    )


def send_halves(me, copies, pair, source, outs, sems):
    keep, send = outs
    for half in range(2):

        @pl.when(me == half)
        def _():
            pltpu.make_async_copy(source(half), keep, sems.at[pair]).start()
            pltpu.make_async_copy(source(1 - half), send, sems.at[pair + 1]).start()

    copies.append(pltpu.make_async_copy(source(0), keep, sems.at[pair]))
    copies.append(pltpu.make_async_copy(source(1), send, sems.at[pair + 1]))


def mlp_backward(layer, core, upstream, keep, vec, slope, middle, branch, mlp, down, up, proj, after=(), through=()):
    rows, width = middle.shape
    depth = slope.shape[1]
    count = depth // FF_STEP
    half_cols, half_width = depth // 2, width // 2
    wide = half_cols + 2 * half_width
    extra = () if mlp is None else (mlp,)
    down_cuts, up_cuts = row_cuts(depth, count), column_cuts(depth, count)
    cuts = [(slice(None), slice(None))]

    def body(core_ref, g_ref, keep_ref, vec_ref, slope_ref, middle_ref, branch_ref, *refs):
        mlp_refs, refs = refs[: len(extra)], refs[len(extra) :]
        od, td, ou, tu, op, tp, keep_out, send_out, ga_ref, gmid_ref, vecs_ref, ups_ref, low, back_buf, slp, mid, br, mlp_buf, bd, bu, bp, sd, su, sp, sin, sout = refs
        me = core_ref[0]
        mine = me == layer
        fetch_start(mine, od, td, bd, sd, down_cuts)
        coming = [
            pltpu.make_async_copy(source, target, sin.at[n])
            for n, (source, target) in enumerate([(middle_ref, mid), (branch_ref, br)] + [(r, mlp_buf) for r in mlp_refs])
        ]
        slopes = []
        for n in range(count // 2):
            part = pl.ds(n * 2 * FF_STEP, 2 * FF_STEP)
            slopes.append(pltpu.make_async_copy(slope_ref.at[:, part], slp.at[:, part], sin.at[3 + n]))
            slopes[n].start()
        fetch_start(mine, ou, tu, bu, su, up_cuts)
        for copy in coming:
            copy.start()
        fetch_start(mine, op, tp, bp, sp, cuts)
        gm = (vec_ref[9:10, :] * (g_ref[...].astype(F32) * keep_ref[...])).astype(BF16)
        low[...] = gm
        for half in range(2):
            back_buf[half, :, :half_width] = gm[:, half * half_width : (half + 1) * half_width]
        vecs_ref[...] = jnp.zeros_like(vecs_ref)
        vecs_ref[4:5, :] = jnp.sum(gm.astype(F32), axis=0, keepdims=True)
        for i in range(count):
            if i % 2 == 0:
                fetch_wait(od, bd, sd, down_cuts, i)
                fetch_wait(od, bd, sd, down_cuts, i + 1)
                slopes[i // 2].wait()
            cols = pl.ds(i * FF_STEP, FF_STEP)
            gp = (mm_back(low[...], bd[cols, :]) * slp[:, cols].astype(F32)).astype(BF16)
            back_buf[2 * i // count, :, pl.ds(half_width + (i * FF_STEP) % half_cols, FF_STEP)] = gp
            ups_ref[:, cols] = jnp.sum(gp.astype(F32), axis=0, keepdims=True)
        for i in range(count):
            fetch_wait(ou, bu, su, up_cuts, i)
        middle_cols = slice(half_width, half_width + half_cols)
        back = mm_back(back_buf[0, :, middle_cols], bu[:, :half_cols]) + mm_back(back_buf[1, :, middle_cols], bu[:, half_cols:])
        for copy in coming:
            copy.wait()
        going, gain, shift = norm_back(back, mid[...], vec_ref[6:7, :])
        g = g_ref[...].astype(F32) * keep_ref[...]
        gmid = g + going
        gmid_ref[...] = gmid
        gb = (vec_ref[5:6, :] * gmid).astype(BF16)
        low[...] = gb
        for half in range(2):
            back_buf[half, :, half_width + half_cols :] = gb[:, half * half_width : (half + 1) * half_width]
        copies = []
        send_halves(me, copies, 0, lambda half: back_buf.at[half], (keep_out, send_out), sout)
        vecs_ref[0:1, :] = gain
        vecs_ref[1:2, :] = shift
        vecs_ref[2:3, :] = jnp.sum(gmid * br[...].astype(F32), axis=0, keepdims=True)
        vecs_ref[3:4, :] = jnp.sum(gb.astype(F32), axis=0, keepdims=True)
        if extra:
            vecs_ref[5:6, :] = jnp.sum(g * mlp_buf[...].astype(F32), axis=0, keepdims=True)
        fetch_wait(op, bp, sp, cuts, 0)
        ga_ref[...] = mm_back(low[...], bp[...]).astype(BF16)
        for copy in copies:
            copy.wait()

    return kernel_call(
        body,
        [S, V, V, V, H, H, H] + [H] * (len(extra) + 6),
        [
            shape((rows, wide), BF16),
            shape((rows, wide), BF16),
            shape((rows, width), BF16),
            shape((rows, width), F32),
            shape((8, width), F32),
            shape((1, depth), F32),
        ],
        [
            pltpu.VMEM((rows, width), BF16),
            pltpu.VMEM((2, rows, wide), BF16),
            pltpu.VMEM((rows, depth), BF16),
            pltpu.VMEM((rows, width), F32),
            pltpu.VMEM((rows, width), BF16),
            pltpu.VMEM((rows, width), BF16),
            pltpu.VMEM((depth, width), BF16),
            pltpu.VMEM((width, depth), BF16),
            pltpu.VMEM((width, width), BF16),
            pltpu.SemaphoreType.DMA((count,)),
            pltpu.SemaphoreType.DMA((count,)),
            pltpu.SemaphoreType.DMA((1,)),
            pltpu.SemaphoreType.DMA((3 + count // 2,)),
            pltpu.SemaphoreType.DMA((2,)),
        ],
        (core, upstream, keep, vec, slope, middle, branch) + extra + down + up + proj,
        SMALL,
        after=after,
        out_specs=[H, H, V, V, V, V],
        through=through,
    )


def attention_backward(core, projected, upstream, base_big, base_small, corners, sizes, after=()):
    rows, triple = projected.shape
    width = triple // 3
    pairs = HEADS // 2
    crops, len_big, pad_big, slots, len_small, pad_small = sizes
    grid_big, grid_small = math.isqrt(len_big - 1), math.isqrt(len_small - 1)
    half = 3 * pairs // 2

    parts = attention_parts(sizes)

    def body(core_ref, corner_ref, proj_ref, g_ref, bb_ref, bs_ref, gproj_ref, keep_out, send_out, tb_ref, ts_ref, sums_ref, big, block, small, dbig, dsmall, dblock, sout):
        dbig[...] = jnp.zeros_like(dbig)
        dsmall[...] = jnp.zeros_like(dsmall)
        dblock[...] = jnp.zeros_like(dblock)
        tb_ref[...] = jnp.zeros_like(tb_ref)
        ts_ref[...] = jnp.zeros_like(ts_ref)

        def step(pair, carry):
            pair_bias(pair, corner_ref, bb_ref, bs_ref, big, block, small, sizes)

            q, k, v = [pl.ds(pl.multiple_of(n * width + pair * 128, 128), 128) for n in range(3)]
            places = [which * pairs + pair for which in range(3)]
            scores, gprs = [], []
            for start, count, is_big in parts:
                part = pl.ds(start, count)
                bias = big if is_big else small
                scores.append(mm_back(two_heads(proj_ref[part, q] * 0.125), proj_ref[part, k]) + bias[:, :count])
                gprs.append(mm_back(two_heads(g_ref[part, q]), proj_ref[part, v]))
            probs = [attention_probs(item) for item in scores]
            gss = [(p * (gpr - jnp.sum(p * gpr, axis=-1, keepdims=True))).astype(BF16) for p, gpr in zip(probs, gprs)]
            for n, ((start, count, is_big), p, gs) in enumerate(zip(parts, probs, gss)):
                part = pl.ds(start, count)
                dref = dbig if is_big else dsmall
                if n == 0 or not is_big:
                    dref[:, :count] = gs.astype(F32)
                else:
                    dref[:, :count] += gs.astype(F32)
                gproj_ref[places[0], part, :] = (one_line(mm(gs, proj_ref[part, k])) * 0.125).astype(BF16)
                gproj_ref[places[1], part, :] = mm_outer(gs, two_heads(proj_ref[part, q] * 0.125)).astype(BF16)
                gproj_ref[places[2], part, :] = mm_outer(p.astype(BF16), two_heads(g_ref[part, q])).astype(BF16)


            for h in range(2):
                hbig, hsmall = dbig.at[pl.ds(h * pad_big, pad_big)], dsmall.at[pl.ds(h * pad_small, pad_small)]

                def fold(dref, grid, length, out_ref):
                    lanes = out_ref.shape[2]
                    wide = lax.broadcasted_iota(jnp.int32, (grid, 256), 1)
                    inside = (wide > 0) & (wide < length)
                    total = jnp.zeros((grid, lanes), F32)
                    for r in range(grid):
                        value = jnp.where(inside, dref[pl.ds(1 + grid * r, grid), :], 0)
                        if lanes > 256:
                            value = jnp.concatenate([value, jnp.zeros((grid, lanes - 256), F32)], axis=1)
                        off = (grid - 1 - r) * grid
                        total = total + (value if off == 0 else pltpu.roll(value, off, 1))
                    out_ref[pair * 2 + h, :grid, :] = total
                    line = lax.broadcasted_iota(jnp.int32, (length, 256), 0)
                    spot = lax.broadcasted_iota(jnp.int32, (length, 256), 1)
                    value = jnp.where(spot < length, dref[pl.ds(0, length), :], 0)
                    out_ref[pair * 2 + h, grid : grid + 1, :256] = value[0:1, :]
                    out_ref[pair * 2 + h, grid + 1 : grid + 2, :256] = jnp.sum(jnp.where(line > 0, value, 0), axis=0, keepdims=True)

                fold(hbig, grid_big, len_big, tb_ref)
                total = hsmall[pl.ds(0, len_small), :]
                for s in range(1, slots):
                    total = total + pltpu.roll(hsmall[pl.ds(s * len_small, len_small), :], 256 - s * len_small, 1)
                dblock[pl.ds(0, len_small), :] = total
                fold(dblock, grid_small, len_small, ts_ref)
            for n, which in ((0, 0), (1, 2)):
                sums_ref[n : n + 1, q] = jnp.sum(gproj_ref[places[which]].astype(F32), axis=0, keepdims=True)
            return carry

        lax.fori_loop(0, pairs, step, 0)
        copies = []
        send_halves(core_ref[0], copies, 0, lambda n: gproj_ref.at[pl.ds(n * half, half)], (keep_out, send_out), sout)
        for copy in copies:
            copy.wait()

    return kernel_call(
        body,
        [S, S, V, V, V, V],
        [
            shape((2 * half, rows, 128), BF16),
            shape((half, rows, 128), BF16),
            shape((half, rows, 128), BF16),
            shape((HEADS, 16, 512), F32),
            shape((HEADS, 8, 256), F32),
            shape((2, width), F32),
        ],
        bias_scratch(sizes)
        + [
            pltpu.VMEM((2 * pad_big, 256), F32),
            pltpu.VMEM((2 * pad_small, 256), F32),
            pltpu.VMEM((up_to(len_small, 8), 256), F32),
            pltpu.SemaphoreType.DMA((2,)),
        ],
        (core, corners, projected, upstream, base_big, base_small),
        15 * 10**9,
        out_specs=[V, H, H, V, V, V],
        after=after,
    )


def qkv_backward(layer, core, gproj, x, gmid, gain, own, other, after=(), flops=10**8):
    rows, width = x.shape
    blocks = gproj.shape[0]
    triple = blocks * 128
    cuts = column_cuts(triple, 3)
    group = blocks // 3

    def body(core_ref, gproj_ref, x_ref, gmid_ref, gain_ref, own_ref, other_ref, gx_ref, vecs_ref, buf, acc, sems):
        me = core_ref[0]
        fetch_start(me == layer, own_ref, other_ref, buf, sems, cuts)
        for i in range(3):
            fetch_wait(own_ref, buf, sems, cuts, i)
            joined = jnp.concatenate([gproj_ref[n] for n in range(i * group, (i + 1) * group)], axis=1)
            more = mm_back(joined, buf[:, pl.ds(i * width, width)])
            if i == 0:
                acc[...] = more
            else:
                acc[...] += more
        going, gain_sum, shift_sum = norm_back(acc[...], x_ref[...].astype(F32), gain_ref[...])
        gx_ref[...] = (gmid_ref[...] + going).astype(BF16)
        vecs_ref[0:1, :] = gain_sum
        vecs_ref[1:2, :] = shift_sum

    return kernel_call(
        body,
        [S, V, V, V, V, H, H],
        [shape((rows, width), BF16), shape((2, width), F32)],
        [
            pltpu.VMEM((width, triple), BF16),
            pltpu.VMEM((rows, width), F32),
            pltpu.SemaphoreType.DMA((3,)),
        ],
        (core, gproj, x, gmid, gain, own, other),
        flops,
        after=after,
    )


def place_of(relative, order):
    place = 0
    for bit in order:
        place = place * 2 + ((relative >> bit) & 1)
    return place


def piece_plan(names, tiles, quarters):
    counts = [
        {name: tiles[name] // 3 * (2 - p) * (quarters if name == "down" else 1) for name in names} for p in range(2)
    ]
    bases = [{name: sum(counts[p][other] for other in names[:n]) for n, name in enumerate(names)} for p in range(2)]
    return counts, bases, [sum(count.values()) for count in counts]


def weight_grad(where, orders, names, left, right, blocks, flops, after=()):
    devices = 1 << len(orders[0][0])
    pieces = len(orders)
    rows, total_cols = left[0].shape
    width = total_cols - 2 * right[0].shape[1]
    hidden = total_cols - 3 * width
    spans = dict(zip(("down", "up", "proj", "qkv"), saved_cuts(width, hidden)))
    backs = {"down": (0, width // 2), "up": (width // 2, hidden // 2), "proj": (width // 2 + hidden // 2, width // 2), "qkv": (0, 3 * width // 2)}
    block = width // devices
    tiles = {name: backs[name][1] // 128 for name in names}
    counts, bases, subs = piece_plan(names, tiles, hidden // width)
    half = devices // 2
    arrays = tuple(left) + tuple(right) + (tuple(blocks) if "qkv" in names else ())
    copies_needed = sum(2 * (hidden // width) + 2 if name == "down" else 2 + 2 * blocks[0].shape[0] if name == "qkv" else 4 for name in names)

    def body(where_ref, *refs):
        ins, refs = refs[: len(arrays)], refs[len(arrays) + len(after) :]
        outs, refs = refs[: 2 * pieces], refs[2 * pieces :]
        held, refs = refs[:pieces], refs[pieces:]
        lefts, refs = refs[: len(names)], refs[len(names) :]
        rights, refs = refs[: len(names)], refs[len(names) :]
        turned, sems, in_sems = refs
        me, first = where_ref[1], where_ref[0] == 0
        places = [
            [jnp.where(first, place_of(j ^ me, order[0]), place_of(j ^ me, order[1])) for j in range(devices)]
            for order in orders
        ]
        coming = {name: [] for name in names}
        used = 0

        def bring(name, source, target):
            nonlocal used
            copy = pltpu.make_async_copy(source, target, in_sems.at[used])
            copy.start()
            used += 1
            coming[name].append(copy)

        for n, name in enumerate(names):
            for side in range(2):
                lines = pl.ds(side * rows, rows)
                if name == "qkv":
                    for t in range(tiles[name]):
                        bring(name, ins[4 + side].at[t], rights[n].at[lines, pl.ds(t * 128, 128)])
                else:
                    bring(name, ins[2 + side].at[:, pl.ds(*backs[name])], rights[n].at[lines, :])
            low, size = spans[name]
            for start in range(0, size, width):
                for side in range(2):
                    lines = pl.ds(side * rows, rows)
                    bring(name, ins[side].at[:, pl.ds(low + start, width)], lefts[n].at[lines, pl.ds(start, width)])

        def put(name, value, line, tile, extra=0):
            large = tiles[name] // 3 * 2
            p, at = (0, tile) if tile < large else (1, tile - large)
            held[p][places[p][line], bases[p][name] + at * (hidden // width if name == "down" else 1) + extra] = value

        def copies(p):
            return [
                pltpu.make_async_copy(held[p].at[pl.ds(0, half)], outs[2 * p], sems.at[2 * p]),
                pltpu.make_async_copy(held[p].at[pl.ds(half, half)], outs[2 * p + 1], sems.at[2 * p + 1]),
            ]

        for n, name in enumerate(names):
            waits = coming[name]
            final = n + 1 == len(names)
            if name == "down":
                for copy in waits[:2]:
                    copy.wait()
                cols = backs[name][1]
                turned[:cols, :] = rights[n][...].T
                lines = block * (hidden // width)
                for c in range(hidden // width):
                    for copy in waits[2 + 2 * c : 4 + 2 * c]:
                        copy.wait()
                    value = mm(turned[:cols, :], lefts[n][:, pl.ds(c * width, width)]).astype(BF16).T
                    for j in range(width // block):
                        at = c * (width // block) + j
                        for t in range(tiles[name]):
                            put(name, value[j * block : (j + 1) * block, t * 128 : (t + 1) * 128], at // (hidden // width), t, at % (hidden // width))
                done = 0
            else:
                for copy in waits:
                    copy.wait()
                turned[...] = lefts[n][...].T
                done = 0
                for low in range(0, tiles[name], 4):
                    high = min(low + 4, tiles[name])
                    value = mm(turned[...], rights[n][:, low * 128 : high * 128])
                    for j in range(devices):
                        for t in range(low, high):
                            put(name, value[j * block : (j + 1) * block, (t - low) * 128 : (t - low + 1) * 128].astype(BF16), j, t)
                    while final and done < pieces and (tiles[name] // 3 * 2, tiles[name])[done] <= high:
                        for copy in copies(done):
                            copy.start()
                        done += 1
            if final:
                for p in range(done, pieces):
                    for copy in copies(p):
                        copy.start()
        for p in range(pieces):
            for copy in copies(p):
                copy.wait()

    outs = [shape((half, subs[p], block, 128), BF16) for p in range(pieces) for _ in range(2)]
    scratch = [pltpu.VMEM((devices, subs[p], block, 128), BF16) for p in range(pieces)]
    scratch += [pltpu.VMEM((2 * rows, spans[name][1]), BF16) for name in names]
    scratch += [pltpu.VMEM((2 * rows, backs[name][1]), BF16) for name in names]
    scratch += [pltpu.VMEM((width, 2 * rows), BF16)]
    specs = [S] + [H, ANY] * (len(arrays) // 2) + [after_spec(item) for item in after]
    return pl.pallas_call(
        body,
        in_specs=specs,
        out_specs=[H] * (2 * pieces),
        out_shape=outs,
        scratch_shapes=scratch + [pltpu.SemaphoreType.DMA((2 * pieces,)), pltpu.SemaphoreType.DMA((copies_needed,))],
        compiler_params=pltpu.CompilerParams(vmem_limit_bytes=VMEM_BYTES),
        cost_estimate=pl.CostEstimate(flops=int(flops / COST), bytes_accessed=1024, transcendentals=0),
    )(*in_hbm((where, *arrays, *after), specs))


NAMES = ("down", "up", "proj", "qkv")


def add_stage(items, after, flops=10**9):
    args, outs, plan = [], [], []
    for item in items:
        kept, came, how = item
        if how == "joined":
            plan.append((how, len(args), len(kept), len(outs)))
            half = shape((kept[0].shape[0] // 2, sum(k.shape[1] for k in kept)) + kept[0].shape[2:], BF16)
            outs += [half, half]
            args += list(kept) + list(came)
        elif how == "last":
            plan.append((how, len(args), len(kept), len(outs)))
            outs.append(shape((sum(k.shape[1] for k in kept),) + kept[0].shape[2:], F32))
            args += list(kept) + list(came)
        else:
            plan.append((how, len(args), 1, len(outs)))
            if how == "halves":
                half = shape((kept.shape[0] // 2,) + kept.shape[1:], BF16)
                outs += [half, half]
            else:
                outs.append(shape(kept.shape, F32))
            args += [kept, came]

    def body(*refs):
        ins, results = refs[: len(args)], refs[len(args) :]
        for how, at, count, to in plan:
            if how == "last":
                low = 0
                for n in range(count):
                    high = low + ins[at + n].shape[1]
                    results[to][low:high] = ins[at + n][0].astype(F32) + ins[at + count + n][0].astype(F32)
                    low = high
            elif how == "joined":
                half, low = outs[to].shape[0], 0
                for n in range(count):
                    high = low + ins[at + n].shape[1]
                    for part in range(2):
                        cut = pl.ds(part * half, half)
                        value = ins[at + n][cut].astype(F32) + ins[at + count + n][cut].astype(F32)
                        results[to + part][:, low:high] = value.astype(BF16)
                    low = high
            elif how == "whole":
                results[to][...] = ins[at][...] + ins[at + 1][...]
            else:
                half = outs[to].shape[0]
                for n in range(2):
                    cut = pl.ds(n * half, half)
                    results[to + n][...] = (ins[at][cut].astype(F32) + ins[at + 1][cut].astype(F32)).astype(BF16)
        results[-1][...] = jnp.zeros((8, 128), F32)

    args = [pltpu.with_memory_space_constraint(a, pltpu.HBM) if size_of(a) > 500000 else a for a in args]
    made = kernel_call(body, [V] * len(args), outs + [shape((8, 128), F32)], [], tuple(args), flops, after=after)
    results = []
    for how, _, _, to in plan:
        results.append((made[to], made[to + 1]) if how in ("halves", "joined") else made[to])
    return results, made[-1]


class Scatter:
    def __init__(self, made, orders):
        self.keeps, self.sends, self.orders = list(made[0::2]), list(made[1::2]), orders
        self.step, self.result = 0, None
        self.launch()

    def launch(self):
        self.came = [
            across(send, [order[self.step] for order in both]) for send, both in zip(self.sends, self.orders)
        ]

    def items(self):
        if self.step + 1 == len(self.orders[0][0]):
            return [(self.keeps, self.came, "last")]
        return [(keep, came, "halves") for keep, came in zip(self.keeps, self.came)]

    def take(self, results):
        self.step += 1
        if self.step == len(self.orders[0][0]):
            self.result = results[0]
            return
        self.keeps, self.sends = [r[0] for r in results], [r[1] for r in results]
        self.launch()


class Total:
    def __init__(self, value, sent, bits):
        self.value, self.bits, self.step, self.result = value, bits, 0, None
        self.came = swap(sent)

    def items(self):
        return [(self.value, self.came, "whole")]

    def take(self, results):
        self.value = results[0]
        if self.step == self.bits:
            self.result = self.value
            return
        self.came = across(self.value, [self.step, self.step])
        self.step += 1


def join_groups(groups, after):
    pieces = len(groups[0].orders)
    items = [([g.keeps[p] for g in groups], [g.came[p] for g in groups], "joined") for p in range(pieces)]
    results, token = add_stage(items, after, 14 * 10**9)
    joined = groups[0]
    joined.take(results)
    return joined, token


def advance(groups, after, flops=10**9):
    groups = [group for group in groups if group.result is None]
    if not groups:
        return after[0]
    items = [group.items() for group in groups]
    results, token = add_stage([item for part in items for item in part], after, flops)
    for group, part in zip(groups, items):
        group.take(results[: len(part)])
        results = results[len(part) :]
    return token


def gather_vectors(core, folded, parts):
    width = parts[0][0].shape[1]
    args = (core, folded) + tuple(item for part in parts for item in part)
    count = len(parts[0])
    tiles = width // 128
    lines = folded.shape[0]

    def body(core_ref, folded_ref, *refs):
        kept, sent = refs[-2:]
        first = core_ref[0] == 0
        wholes = []
        for layer in range(2):
            vecs1, qv, vecs2, scale, ups = [ref[...] for ref in refs[layer * count : layer * count + count]]
            rows = [vecs1, qv, vecs2[3:4], vecs2[2:3], vecs2[0:2], vecs2[4:5], scale]
            rows += [ups[:, n * width : (n + 1) * width] for n in range(ups.shape[1] // width)]
            rows.append(jnp.zeros((16 - sum(row.shape[0] for row in rows), width), F32))
            wholes.append(jnp.concatenate(rows, axis=0))

        def put(at, zero, one):
            kept[pl.ds(at, 16), :] = jnp.where(first, zero, one)
            sent[pl.ds(at, 16), :] = jnp.where(first, one, zero)

        for t in range(tiles):
            put(t * 16, *[whole[:, t * 128 : (t + 1) * 128] for whole in wholes])
        for n in range(lines):
            put((tiles + n) * 16, folded_ref[n, :HEAD_ROWS], folded_ref[n, HEAD_ROWS:])

    out = shape((16 * (tiles + lines), 128), F32)
    return kernel_call(body, [S] + [V] * (len(args) - 1), [out, out], [], args, SMALL)


def pick_rows(core, zero, one, after):
    rows, width = zero[0].shape

    def body(core_ref, zero_y, zero_g, one_y, one_g, kept, sent, token):
        first = core_ref[0] == 0
        for n, (a, b) in enumerate(((zero_y, one_y), (zero_g, one_g))):
            kept[n] = jnp.where(first, a[...], b[...])
            sent[n] = jnp.where(first, b[...], a[...])
        token[...] = jnp.zeros((8, 128), F32)

    both = shape((2, rows, width), BF16)
    return kernel_call(body, [S, V, V, V, V], [both, both, shape((8, 128), F32)], [], (core, *zero, *one), SMALL, after=after)


def arrange_rows(core, own, came, sizes, after):
    crops, len_big, pad_big, slots, len_small, pad_small = sizes
    width = own.shape[2]
    split = crops * pad_big

    def body(core_ref, own_ref, came_ref, *outs):
        me = core_ref[0]
        for n in range(2):
            out_big, out_small = outs[2 * n : 2 * n + 2]
            for place, ref in ((me, own_ref), (1 - me, came_ref)):
                for c in range(crops):
                    out_big[0, place, c] = ref[n, pl.ds(c * pad_big, len_big), :]
                rest = ref[n, pl.ds(split, pad_small), :].astype(F32)
                for s in range(slots):
                    out_small[0, place, s] = rest[s * len_small : (s + 1) * len_small].astype(BF16)

    big = shape((1, 2, crops, len_big, width), BF16)
    small = shape((1, 2, slots, len_small, width), BF16)
    return kernel_call(body, [S, V, V], [big, small, big, small], [], (core, own, came), SMALL, after=after)


def arrange_grads(core, sums, came, block, width, hidden):
    args = tuple(item for part in (*sums, *came) for _, item in part)
    quarters = hidden // width
    tiles = {"down": width // 256, "up": hidden // 256, "proj": width // 256, "qkv": 3 * width // 256}

    def body(core_ref, *refs):
        outs = dict(zip(NAMES, refs[len(args) :]))

        def put(half, part, refs):
            for (names, _), ref in zip(part, refs):
                counts, bases, subs = piece_plan(names, tiles, quarters)
                for name in names:
                    for tile in range(tiles[name]):
                        large = tiles[name] // 3 * 2
                        p, at = (0, tile) if tile < large else (1, tile - large)
                        times = quarters if name == "down" else 1
                        for q in range(times):
                            value = ref[p * subs[0] + bases[p][name] + at * times + q]
                            outs[name][0, pl.ds(q * block, block), pl.ds((half * tiles[name] + tile) * 128, 128)] = value

        count = len(args) // 2
        starts = [0, len(sums[0]), count, count + len(came[0])]
        for me in range(2):

            @pl.when(core_ref[0] == me)
            def _():
                put(me, sums[me], refs[starts[me] :])
                put(1 - me, came[me], refs[starts[2 + me] :])

    return kernel_call(
        body,
        [S] + [V] * len(args),
        [
            shape((1, quarters * block, width), F32),
            shape((1, block, hidden), F32),
            shape((1, block, width), F32),
            shape((1, block, 3 * width), F32),
        ],
        [],
        (core, *args),
        SMALL,
    )


def swap(value):
    return lax.ppermute(value, "section", [(0, 1), (1, 0)])


def across(value, bits):
    devices = lax.axis_size("dp")
    pairs = [(core * devices + i, core * devices + (i ^ (1 << bits[core]))) for core in range(2) for i in range(devices)]
    return lax.ppermute(value, ("section", "dp"), pairs)


def hand_over(value, layer):
    return lax.ppermute(value, "section", [(1 - layer, layer)])


HEAD_ROWS = 16


def flip_lanes(side):
    row = lax.broadcasted_iota(jnp.int32, (side, 128), 0)
    lane = lax.broadcasted_iota(jnp.int32, (side, 128), 1)
    return jnp.where(row + lane == side - 1, 1.0, 0.0)


def table_bases(core, own, other, grids, entries_big):
    heads = own.shape[1]
    both = 2 * HEAD_ROWS

    def body(core_ref, own_ref, other_ref, out_big, out_small, corners, own_buf, other_buf):
        first = core_ref[0] == 0
        own_buf[...] = own_ref[...]
        other_buf[...] = other_ref[...]
        out_big[...] = jnp.zeros_like(out_big)
        out_small[...] = jnp.zeros_like(out_small)
        corners[...] = jnp.zeros_like(corners)
        lane = lax.broadcasted_iota(jnp.int32, (both, 128), 1)

        def lines(start, count):
            mine, theirs = own_buf[pl.ds(start, count), :], other_buf[pl.ds(start, count), :]
            return jnp.where(first, mine, theirs), jnp.where(first, theirs, mine)

        start = 0
        for n, (out, grid) in enumerate(((out_big, grids[0]), (out_small, grids[1]))):
            side = 2 * grid - 1
            flip = flip_lanes(side)
            flipped = []
            for d in range(side):
                pair = []
                for part in lines(start + (side - 1 - d) * side, side):
                    turned = lax.dot_general(part, flip, (((0,), (0,)), ((), ())), precision=lax.Precision.HIGHEST, preferred_element_type=F32)
                    pair.append(jnp.concatenate([turned, jnp.zeros((HEAD_ROWS - heads, 128), F32)], axis=0))
                flipped.append(jnp.concatenate(pair, axis=0))
            for r in range(grid):
                tiles = [jnp.zeros((both, 128), F32) for _ in range(out.shape[3] // 128)]
                for d in range(side):
                    low = 1 + d * grid
                    shift = (low - (grid - 1 - r)) % 128
                    moved = pltpu.roll(flipped[d], shift, 1) if shift else flipped[d]
                    tile, at = low // 128, low % 128
                    tiles[tile] = jnp.where((lane >= at) & (lane < at + grid), moved, tiles[tile])
                    if at + grid > 128:
                        tiles[tile + 1] = jnp.where(lane < at + grid - 128, moved, tiles[tile + 1])
                value = jnp.concatenate(tiles, axis=1)
                for layer in range(2):
                    out[layer, :, r, :] = value[layer * HEAD_ROWS : layer * HEAD_ROWS + heads]
            for layer, part in enumerate(lines(start + side * side, 3)):
                corners[layer, n, 0:3, 0:heads] = part
            start = entries_big

    return kernel_call(
        body,
        [S, V, V],
        [shape((2, heads, 16, 512), F32), shape((2, heads, 8, 256), F32), shape((2, 2, 8, 128), F32)],
        [pltpu.VMEM(own.shape, F32), pltpu.VMEM(own.shape, F32)],
        (core, own, other),
        SMALL,
    )


def table_folds(big, small, grids, lengths, after):
    heads = big.shape[1]
    counts = [-(-(2 * grid - 1) // 4) for grid in grids]

    def body(big_ref, small_ref, out):
        lane = lax.broadcasted_iota(jnp.int32, (heads, 128), 1)
        base = 0
        ends = []
        for ref, grid, count, length in zip((big_ref, small_ref), grids, counts, lengths):
            for line in range(count):
                total = jnp.zeros((heads, 128), F32)
                for d in range(4 * line, min(4 * line + 4, 2 * grid - 1)):
                    low = 1 + d * grid
                    tile, at = low // 128, low % 128
                    for r in range(grid):
                        to = 32 * (d % 4) + grid - 1 - r
                        moved = ref[r, :, tile * 128 : tile * 128 + 128]
                        if at + grid > 128:
                            moved = jnp.where(lane >= at, moved, ref[r, :, tile * 128 + 128 : tile * 128 + 256])
                        shift = (to - at) % 128
                        moved = pltpu.roll(moved, shift, 1) if shift else moved
                        total = total + jnp.where((lane >= to) & (lane < to + grid), moved, 0)
                out[base + line] = total
            base += count
            first, second = ref[grid], ref[grid + 1]
            wide = lax.broadcasted_iota(jnp.int32, first.shape, 1)
            ends.append(jnp.sum(jnp.where((wide > 0) & (wide < length), first, 0), axis=1, keepdims=True))
            ends.append(second[:, 0:1])
            ends.append(first[:, 0:1])
        last = out[base - 1]
        for n, end in enumerate(ends):
            last = jnp.where(lane == 96 + n, end, last)
        out[base - 1] = last

    return kernel_call(body, [V, V], [shape((sum(counts), heads, 128), F32)], [], (big, small), SMALL, after=after)[0]


def arrange_small(where, flat, grids, entries, width, block, ups, vectors):
    tiles = width // 128
    counts = [-(-(2 * grid - 1) // 4) for grid in grids]

    def body(where_ref, flat_ref, *outs):
        place = where_ref[1]
        lines = jnp.concatenate([flat_ref[pl.ds(t * 16, 16), :] for t in range(tiles)], axis=1)
        moved = pltpu.roll(lines, lax.rem(width - place * block, width), 1)
        for n in range(vectors):
            outs[n][...] = moved[n : n + 1, :block]
        per_row = width // (ups * block)
        moved = pltpu.roll(lines, lax.rem(width - lax.rem(place, per_row) * (ups * block), width), 1)
        row = lax.broadcasted_iota(jnp.int32, (16, ups * block), 0)
        chosen = jnp.where(row == vectors + place // per_row, moved[:, : ups * block], 0)
        outs[vectors][...] = jnp.sum(chosen, axis=0, keepdims=True)
        base = 16 * tiles

        def at(line):
            return flat_ref[pl.ds(base + line * HEAD_ROWS, HEAD_ROWS), :]

        line, last = 0, sum(counts) - 1
        for n, grid in enumerate(grids):
            side = 2 * grid - 1
            out = outs[vectors + 1 + n]
            row = lax.broadcasted_iota(jnp.int32, (side, 128), 0)
            lane = lax.broadcasted_iota(jnp.int32, (side, 128), 1)
            for d in range(side):
                pick = jnp.where(lane - 32 * (d % 4) + row == side - 1, 1.0, 0.0)
                value = lax.dot_general(pick, at(line + d // 4), (((1,), (1,)), ((), ())), precision=lax.Precision.HIGHEST, preferred_element_type=F32)
                out[0, pl.ds((side - 1 - d) * side, side), :] = value[:, :HEADS]
            pick = jnp.where(lane[:3] == 96 + 3 * n + row[:3], 1.0, 0.0)
            value = lax.dot_general(pick, at(last), (((1,), (1,)), ((), ())), precision=lax.Precision.HIGHEST, preferred_element_type=F32)
            out[0, pl.ds(side * side, 3), :] = value[:, :HEADS]
            line += counts[n]

    outs = [shape((1, block), F32)] * vectors + [shape((1, ups * block), F32)] + [shape((1, count, HEADS), F32) for count in entries]
    return kernel_call(body, [S, V], outs, [], (where, flat), SMALL)


def body(input_big, input_small, small_counts, cotangent_big, cotangent_small, norm1_gain, norm1_bias, qkv_weight, query_bias, value_bias, table_big, table_small, proj_weight, proj_bias, attn_scale, norm2_gain, norm2_bias, up_weight, up_bias, down_weight, down_bias, mlp_scale):
    micro, crops, len_big, width = input_big.shape
    slots_all, len_small = input_small.shape[1], input_small.shape[2]
    slots = slots_all // small_counts.shape[1]
    grid_big, grid_small = math.isqrt(len_big - 1), math.isqrt(len_small - 1)
    pad_big = up_to(len_big, 16)
    real_small = slots_all * len_small
    pad_small = up_to(real_small, 16)
    split = crops * pad_big
    rows = split + pad_small
    sizes = (crops, len_big, pad_big, slots_all, len_small, pad_small)
    devices = lax.axis_size("dp")
    bits = devices.bit_length() - 1
    core = lax.axis_index("section")
    place = lax.axis_index("dp")
    where = jnp.stack([core, place]).astype(jnp.int32)
    first = core == 0

    def join(big, small):
        big = lax.dynamic_index_in_dim(big, core, 0, keepdims=False)
        small = lax.dynamic_index_in_dim(small, core, 0, keepdims=False)
        big = jnp.pad(big, ((0, 0), (0, pad_big - len_big), (0, 0))).reshape(split, width)
        small = jnp.pad(small.reshape(real_small, width), ((0, pad_small - real_small), (0, 0)))
        return jnp.concatenate([big, small])

    x0 = join(input_big, input_small)
    cotangent = join(cotangent_big, cotangent_small)
    counts = lax.dynamic_index_in_dim(small_counts, core, 0, keepdims=False)
    line = jnp.arange(rows, dtype=jnp.int32)
    spot = line - split
    slot_of = jnp.arange(slots * len_small, dtype=jnp.int32) // len_small
    small_keep = (slot_of[None, :] < counts[:, None]).astype(F32).reshape(real_small)
    keep = jnp.where(line < split, (line % pad_big < len_big).astype(F32), jnp.pad(small_keep, (split, pad_small - real_small)))
    keep = keep[:, None]

    vec_own = jnp.concatenate(
        [norm1_gain, norm1_bias, query_bias, value_bias, proj_bias, attn_scale, norm2_gain, norm2_bias, down_bias, mlp_scale, up_bias.reshape(-1, width)]
    )
    tables_own = jnp.concatenate([table_big[0], table_small[0]])
    vec_other, tables_other = swap(vec_own), swap(tables_own)
    qkv = (qkv_weight[0], swap(qkv_weight[0]))
    proj = (proj_weight[0], swap(proj_weight[0]))
    up = (up_weight[0], swap(up_weight[0]))
    down = (down_weight[0], swap(down_weight[0]))

    grids, lengths = (grid_big, grid_small), (len_big, len_small)
    entries_big = table_big.shape[1]
    base_big, base_small, corners_all = table_bases(where, tables_own, tables_other, grids, entries_big)
    layers = []
    for layer in range(2):
        vec = jnp.where(core == layer, vec_own, vec_other)
        ups = vec[10:].reshape(1, -1)
        joined = jnp.concatenate([vec[2:3], jnp.zeros_like(vec[2:3]), vec[3:4]], axis=1)
        layers.append((vec, ups, joined, corners_all[layer], base_big[layer], base_small[layer]))

    saved, lefts = [], []
    x = x0
    for layer in range(2):
        vec, ups, joined, corners, big, small = layers[layer]
        passing = () if layer == 0 else (saved[0][2],)
        normed, projected, *passed = qkv_forward(layer, where, x, vec[0:1], vec[1:2], joined, *qkv, (cotangent,) if layer == 0 else (), passing)
        lefts += [(item, swap(item)) for item in passed]
        attended = attention_forward(projected, big, small, corners, sizes)
        made = mlp_forward(layer, where, attended, normed, x, keep, vec, ups, proj, up, down if layer == 0 else None)
        saved.append((x, projected) + tuple(made[:4]))
        if layer == 0:
            x, mlp0 = made[4:]

    rest = list(range(3, bits))
    orders = [([0, 1, 2] + rest, [1, 2] + rest + [0]), ([2, 0, 1] + rest, [2, 0, 1] + rest)]

    def mlp_part(layer, g, mlp, after=(), through=()):
        slope, branch, middle = saved[layer][3:]
        return mlp_backward(layer, where, g, keep, layers[layer][0], slope, middle, branch, mlp, down, up, proj, after=after, through=through)

    def attention_part(layer, ga, after):
        _, _, _, corners, big, small = layers[layer]
        return attention_backward(where, saved[layer][1], ga, big, small, corners, sizes, after=after)

    def qkv_part(layer, gproj, gmid, after, flops=SMALL):
        return qkv_backward(layer, where, gproj, saved[layer][0], gmid, layers[layer][0][0:1], *qkv, after=after, flops=flops)


    kept, sent, ga, gmid, vecs2_1, ups_1, left1 = mlp_part(1, cotangent, None, (lefts[0][1],), (saved[1][2],))
    lefts.append((left1, swap(left1)))
    right = (kept, swap(sent))
    gproj, kept, sent, fold_big1, fold_small1, qv_1 = attention_part(1, ga, (ups_1,))
    blocks = (kept, swap(sent))
    made = weight_grad(where, orders, NAMES[:2], lefts[1], right, blocks, SMALL, (qv_1,))
    most1 = Scatter(made, orders)
    gx1, vecs1_1 = qkv_part(1, gproj, gmid, made[:1])
    made = weight_grad(where, orders, NAMES[2:], lefts[1], right, blocks, SMALL, (vecs1_1,))
    last1 = Scatter(made, orders)

    kept, sent, ga, gmid, vecs2_0, ups_0 = mlp_part(0, gx1, mlp0, made[:1])
    right = (kept, swap(sent))
    all1, token = join_groups([most1, last1], (ups_0,))
    made = weight_grad(where, orders, NAMES[:2], lefts[0], right, None, SMALL, (token,))
    most0 = Scatter(made, orders)
    token = advance([all1], made[:1])
    gproj, kept, sent, fold_big0, fold_small0, qv_0 = attention_part(0, ga, (token,))
    blocks = (kept, swap(sent))
    token = advance([most0], (qv_0,))
    gx0, vecs1_0 = qkv_part(0, gproj, gmid, (token,), 7 * 10**9)
    token = advance([all1], (vecs1_0,))
    made = weight_grad(where, orders, NAMES[2:], lefts[0], right, blocks, SMALL, (token,))
    last0 = Scatter(made, orders)
    token = advance([all1, most0], made[:1])
    y1, scale_1 = down_forward(1, where, left1, saved[1][5], keep, layers[1][0], *down, upstream=cotangent, after=(token,))

    def by_line(zero, one):
        both = jnp.pad(jnp.stack([zero, one]), ((0, 0), (0, HEAD_ROWS - HEADS), (0, 0), (0, 0)))
        return jnp.transpose(both, (2, 0, 1, 3)).reshape(zero.shape[1], 2 * HEAD_ROWS, -1)

    folded = table_folds(by_line(fold_big0, fold_big1), by_line(fold_small0, fold_small1), grids, lengths, (scale_1,))
    flat = gather_vectors(
        where, folded, [(vecs1_0, qv_0, vecs2_0, vecs2_0[5:6], ups_0), (vecs1_1, qv_1, vecs2_1, scale_1, ups_1)]
    )
    flat = Total(*flat, bits)
    token = (folded,)
    token = (advance([last0, flat], token, SMALL),)
    for group in ([most0], [last0, flat]):
        token = (advance(group, token),)
    rows_own = pick_rows(where, (saved[1][0], gx0), (y1, gx1), token)
    rows_came = swap(rows_own[1])
    token = rows_own[2:]
    while any(group.result is None for group in (most0, last0, all1)):
        token = (advance([most0, all1], token, LATE),)
        token = (advance([last0, flat], token, LATE),)
    layer_big, layer_small, grad_big, grad_small = arrange_rows(where, rows_own[0], rows_came, sizes, token)
    token = (layer_small[0, 0, 0, :8, :128],)
    while flat.result is None:
        token = (advance([flat], token),)
    flat = flat.result

    sums = [[(NAMES[:2], most0.result), (NAMES[2:], last0.result)], [(NAMES, all1.result)]]
    came = [[(names, hand_over(item, layer)) for names, item in sums[layer]] for layer in range(2)]
    block = width // devices
    hidden = up_bias.shape[1]
    grad_down, grad_up, grad_proj, grad_qkv = arrange_grads(where, sums, came, block, width, hidden)

    small = arrange_small(where, flat, grids, (entries_big, table_small.shape[1]), width, block, hidden // width, 10)
    grad_up_bias, grad_table_big, grad_table_small = small[10:]

    def vector(row):
        return small[row]

    return (
        layer_big,
        layer_small,
        grad_big,
        grad_small,
        vector(0),
        vector(1),
        grad_qkv,
        vector(2),
        vector(3),
        grad_table_big,
        grad_table_small,
        grad_proj,
        vector(4),
        vector(5),
        vector(6),
        vector(7),
        grad_up,
        grad_up_bias,
        grad_down,
        vector(8),
        vector(9),
    )


def solution(mesh):
    row = P("section", None)
    whole = P("section", None, None)
    dp4 = P(None, "dp", None, None)
    in_specs = (dp4, dp4, P(None, "dp"), dp4, dp4, row, row, whole, row, row, whole, whole, whole, row, row, row, row, whole, row, whole, row, row)
    out5 = P("section", None, "dp", None, None)
    vec = P("section", "dp")
    mat = P("section", "dp", None)
    out_specs = (out5, out5, out5, out5, vec, vec, mat, vec, vec, whole, whole, mat, vec, vec, vec, vec, mat, vec, mat, vec, vec)
    return jax.shard_map(body, mesh=mesh, in_specs=in_specs, out_specs=out_specs, check_vma=False)
```
